512 devices in a mesh: tr: 16 (over z), sec: 32 (over y, x, core).
Axes of the slice: x: 4, y: 4, z: 16, core: 2. Of those that a mesh axis runs over, the one named last changes fastest.
Arguments:
- psi: bfloat16 [32, 512, 8, 512], P('sec', 'tr'), may hold values from -24 to 24
- precond: bfloat16 [32, 512, 8, 512], P('sec', 'tr'), may hold values from 0.25 to 6
- env_left: bfloat16 [3, 32, 512, 512], P(None, 'sec'), may hold values from -1 to 2
- env_right: bfloat16 [3, 32, 512, 512], P(None, 'sec'), may hold values from -1 to 2
- mixers: bfloat16 [3, 8, 8], replicated, may hold values from -3 to 3
- sizes: int32 [32, 2], P('sec'), may hold values from 128 to 512, as said below
Outputs:
- psi_new: bfloat16 [32, 512, 8, 512], P('sec', 'tr')
- residual_new: bfloat16 [32, 512, 8, 512], P('sec', 'tr')
- energy: float32 [], replicated
The draws below stay inside these ranges and needn't reach their ends.
Inputs may be any that keep to these rules, and one draw needn't show every extreme that they name: `sizes`: every entry is a multiple of 128; in each column some sector has 512.
All inputs are finite; a program needn't handle non-finite values.
Results may differ from the reference program's by a relative error of at most 0.023.
Values may be sent and summed in bfloat16 or wider, within the bound.
A program may use at most 64 MiB of HBM per device.

```python
import jax
import jax.numpy as jnp
from jax import lax

BLOCK = 512
PHYS = 8
CHANNELS = 3
UNIT = 128
SECTORS = 32


def draw_sizes(key, part):
    key = jax.random.fold_in(key, 5)
    key_count, key_full = jax.random.split(key)
    blocks = BLOCK // UNIT
    counts = jax.random.randint(key_count, (SECTORS, 2), 1, blocks + 1)
    fullest = jax.random.randint(key_full, (2,), 0, SECTORS)
    places = jnp.arange(SECTORS, dtype=jnp.int32)[:, None]
    counts = jnp.where(places == fullest[None, :], blocks, counts)
    return (counts * UNIT).astype(jnp.int32)


def noise_values(key, shape):
    return jnp.clip(jax.random.normal(key, shape, jnp.float32), -4.0, 4.0)


def draw_psi(key, part):
    key = jax.random.fold_in(key, 11)
    values = noise_values(key, (SECTORS, BLOCK, PHYS, BLOCK))
    ratio = 3.0
    place = jnp.arange(BLOCK, dtype=jnp.float32) / float(BLOCK - 1)
    rising = jnp.exp(jnp.log(ratio) * place)
    return (values * rising[None, :, None, None]).astype(jnp.bfloat16)


def draw_precond(key, part):
    key = jax.random.fold_in(key, 51)
    ratio = 6.0
    spread = jax.random.uniform(key, (SECTORS, BLOCK, PHYS, BLOCK), jnp.float32, jnp.log(0.6), jnp.log(1.6))
    place = jnp.arange(BLOCK, dtype=jnp.float32) / float(BLOCK - 1)
    rising = 0.42 * jnp.exp(jnp.log(ratio) * place)
    values = jnp.exp(spread) * rising[None, :, None, None]
    return jnp.clip(values, 0.25, 6.0).astype(jnp.bfloat16)


def environment(key):
    key_noise, key_diag = jax.random.split(key)
    noise = noise_values(key_noise, (CHANNELS, SECTORS, BLOCK, BLOCK)) * (0.35 / float(BLOCK) ** 0.5) * 2.0
    place = jnp.arange(BLOCK, dtype=jnp.float32) / float(BLOCK - 1)
    ramp = 0.4 + 1.2 * place
    diag = jax.random.uniform(key_diag, (SECTORS, BLOCK), jnp.float32, 0.85, 1.15) * ramp[None, :]
    eye = jnp.eye(BLOCK, dtype=jnp.float32)
    onsite = (jnp.arange(CHANNELS) == 0).astype(jnp.float32)
    return (noise + onsite[:, None, None, None] * diag[None, :, :, None] * eye[None, None, :, :]).astype(jnp.bfloat16)


def draw_env_left(key, part):
    key = jax.random.fold_in(key, 21)
    return environment(key)


def draw_env_right(key, part):
    key = jax.random.fold_in(key, 31)
    return environment(key)


def draw_mixers(key, part):
    key = jax.random.fold_in(key, 41)
    noise = noise_values(key, (CHANNELS, PHYS, PHYS)) * (0.5 / float(PHYS) ** 0.5)
    eye = jnp.eye(PHYS, dtype=jnp.float32)
    onsite = (jnp.arange(CHANNELS) == 0).astype(jnp.float32)
    return (noise + onsite[:, None, None] * eye[None, :, :]).astype(jnp.bfloat16)


def setup_inputs(seed: int = 0) -> dict:
    key_list = jax.random.split(jax.random.key(seed), 7)
    return {
        "psi": draw_psi(jax.random.fold_in(key_list[6], 71), 0),
        "precond": draw_precond(jax.random.fold_in(key_list[6], 71), 0),
        "env_left": draw_env_left(jax.random.fold_in(key_list[6], 71), 0),
        "env_right": draw_env_right(jax.random.fold_in(key_list[6], 71), 0),
        "mixers": draw_mixers(jax.random.fold_in(key_list[6], 71), 0),
        "sizes": draw_sizes(jax.random.fold_in(key_list[6], 71), 0),
    }


OFFSETS = (0, 1, -1)
EPSILON = 1e-06

def displace(vector, offset):
    if offset == 0:
        return vector
    blank = jnp.zeros((abs(offset),) + vector.shape[1:], vector.dtype)
    if offset > 0:
        return jnp.concatenate([blank, vector[:-offset]], 0)
    return jnp.concatenate([vector[-offset:], blank], 0)

def sector_mask(sizes):
    states = jnp.arange(BLOCK, dtype=jnp.int32)
    right_ok = states[None, :] < sizes[:, 1:2]
    left_ok = states[None, :] < sizes[:, 0:1]
    return (right_ok[:, :, None, None] & left_ok[:, None, None, :]).astype(jnp.float32)

def hamiltonian(vector, env_left, env_right, mixers, mask):
    sources = jnp.stack([displace(vector, offset) for offset in OFFSETS], 1)
    lefts = jnp.moveaxis(env_left, 0, 1)
    rights = jnp.moveaxis(env_right, 0, 1)

    def one_sector(items):
        source, left, right, block_mask = items
        total = jnp.zeros((BLOCK, PHYS * BLOCK), jnp.float32)
        for channel in range(len(OFFSETS)):
            mixed = jnp.einsum('bqa,pq->bpa', source[channel].astype(jnp.float32), mixers[channel].astype(jnp.float32)).astype(jnp.bfloat16)
            half = jnp.dot(mixed.reshape(BLOCK * PHYS, BLOCK), left[channel].T, preferred_element_type=jnp.float32).astype(jnp.bfloat16)
            total = total + jnp.dot(right[channel], half.reshape(BLOCK, PHYS * BLOCK), preferred_element_type=jnp.float32)
        return total.reshape(BLOCK, PHYS, BLOCK) * block_mask
    return lax.map(one_sector, (sources, lefts, rights, mask))

def reference(psi, precond, env_left, env_right, mixers, sizes):
    mask = sector_mask(sizes)
    count = float(SECTORS * BLOCK * PHYS * BLOCK)
    start = (psi * mask.astype(jnp.bfloat16)).astype(jnp.float32)
    basis0 = (start * lax.rsqrt(jnp.sum(start * start) / count + EPSILON)).astype(jnp.bfloat16)
    first_vec = basis0.astype(jnp.float32)
    image0 = hamiltonian(basis0, env_left, env_right, mixers, mask)
    theta = jnp.sum(first_vec * image0) / count
    trial = (image0 - theta * first_vec) * precond.astype(jnp.float32)
    along = jnp.sum(first_vec * trial) / count
    trial = trial - along * first_vec
    fresh = jnp.sum(trial * trial) / count
    basis1 = (trial * lax.rsqrt(fresh + EPSILON)).astype(jnp.bfloat16)
    second_vec = basis1.astype(jnp.float32)
    image1 = hamiltonian(basis1, env_left, env_right, mixers, mask)
    cross = 0.5 * (jnp.sum(first_vec * image1) + jnp.sum(second_vec * image0)) / count
    corner = jnp.sum(second_vec * image1) / count
    halfgap = 0.5 * (theta - corner)
    energy = 0.5 * (theta + corner) - jnp.sqrt(halfgap * halfgap + cross * cross)
    weight_one = corner - energy
    weight_two = -cross
    scale = lax.rsqrt(weight_one * weight_one + weight_two * weight_two)
    ritz = (weight_one * first_vec + weight_two * second_vec) * scale
    ritz_image = (weight_one * image0 + weight_two * image1) * scale
    psi_new = ritz.astype(jnp.bfloat16)
    residual_new = (ritz_image - energy * ritz).astype(jnp.bfloat16)
    return (psi_new, residual_new, energy)
```

```python
import jax
import jax.numpy as jnp
from jax import lax
from jax.experimental import pallas as pl
from jax.experimental.pallas import tpu as pltpu
from jax.sharding import PartitionSpec as P

EPSILON = 1e-06
MESH = pl.DeviceIdType.MESH
F32 = jnp.float32
BF16 = jnp.bfloat16
TR = 16
SEC = 32
ROWS = 32
PHYS = 8
WIDTH = 512
HALF = 256
LINES = ROWS * PHYS
COUNT = float(SEC * WIDTH * PHYS * WIDTH)
STEPS = (1, 3, 2)


def dot(a, b):
    return jnp.dot(a, b, preferred_element_type=F32)


def dot_nt(a, b):
    return lax.dot_general(a, b, (((1,), (1,)), ((), ())), preferred_element_type=F32)


def iota(shape, axis):
    return lax.broadcasted_iota(jnp.int32, shape, axis)


def partial_sum(x):
    rows = jnp.sum(x, axis=0, keepdims=True)
    total = rows[:, 0:128]
    for lane in range(128, x.shape[1], 128):
        total = total + rows[:, lane : lane + 128]
    return total


def phys_major(block):
    pieces = [jnp.concatenate([block[2 * p], block[2 * p + 1]], axis=1) for p in range(PHYS)]
    return jnp.concatenate(pieces, axis=0)


def columns_of(value):
    blocks = []
    for j in range(TR):
        p, side = divmod(j, 2)
        blocks.append(value[p * ROWS : (p + 1) * ROWS, side * HALF : (side + 1) * HALF])
    return jnp.stack(blocks, axis=0)


def kernel(
    psi_hbm,
    pc_hbm,
    left_hbm,
    right_hbm,
    mix_hbm,
    sizes_hbm,
    psi_out,
    res_out,
    energy_out,
    psi_in,
    pc_in,
    mix,
    sizes,
    own_env,
    land_env,
    env,
    kron,
    to_new,
    to_old,
    start_rows,
    cols_send,
    cols_mid,
    cols,
    near_cols,
    turn_send,
    turn_recv,
    pc_send,
    pc_mid,
    pc_new,
    vec,
    near_vec,
    half_send,
    half_recv,
    first_send,
    first_mid,
    first_old,
    second_send,
    second_mid,
    second_old,
    red_send,
    red_tr,
    red_sec,
    in_sem,
    scatter_send_sem,
    scatter_recv_sem,
    own_send_sem,
    own_recv_sem,
    gather_send_sem,
    gather_recv_sem,
    near_send_sem,
    near_recv_sem,
    turn_send_sem,
    turn_recv_sem,
    move_send_sem,
    move_one_sem,
    move_two_sem,
    red_send_sem,
    red_recv_sem,
):
    z = lax.axis_index("tr")
    sec = lax.axis_index("sec")
    k = sec // 2
    core = lax.rem(sec, 2)
    y = k // 4
    x = lax.rem(k, 4)

    def ring(z2):
        return {"tr": z2}

    def plane(k2):
        return {"sec": 2 * k2 + core}

    def turned(m):
        return jnp.where(m >= TR - 1, m - (TR - 1), m)

    def ring_peer(i):
        m = turned(i + k)
        step = m // 2 + 1
        return lax.rem(z + jnp.where(lax.rem(m, 2) == 0, step, TR - step), TR)

    def ring_source(i):
        m = turned(i + k)
        step = m // 2 + 1
        return lax.rem(z + jnp.where(lax.rem(m, 2) == 0, TR - step, step), TR)

    def plane_peer(i):
        return 4 * lax.rem(y + i // 4, 4) + lax.rem(x + lax.rem(i, 4), 4)

    def remote(src, dst, send_sem, recv_sem, device):
        return pltpu.make_async_remote_copy(
            src_ref=src,
            dst_ref=dst,
            send_sem=send_sem,
            recv_sem=recv_sem,
            device_id=device,
            device_id_type=MESH,
        )

    def several(ref, count, send_sem, recv_sem):
        part = ref.at[pl.ds(0, count)]
        return remote(part, part, send_sem, recv_sem, ring(lax.rem(z + 1, TR)))

    ends = []

    loads = [
        pltpu.make_async_copy(psi_hbm.at[0], psi_in, in_sem.at[0]),
        pltpu.make_async_copy(pc_hbm.at[0], pc_in, in_sem.at[1]),
        pltpu.make_async_copy(mix_hbm, mix, in_sem.at[2]),
        pltpu.make_async_copy(sizes_hbm, sizes, in_sem.at[3]),
    ]
    env_loads = [
        pltpu.make_async_copy(right_hbm.at[:, 0], own_env.at[0], in_sem.at[4]),
        pltpu.make_async_copy(left_hbm.at[:, 0], own_env.at[1], in_sem.at[5]),
    ]
    for load in loads:
        load.start()
    gap = lax.rem(z - k + TR + 1, TR)

    @pl.when(gap < 3)
    def _():
        for load in env_loads:
            load.start()

    barrier = pltpu.get_barrier_semaphore()

    def greet_tr(i, carry):
        pl.semaphore_signal(barrier, inc=1, device_id=ring(lax.rem(z + i, TR)), device_id_type=MESH)
        return carry

    def greet_sec(i, carry):
        pl.semaphore_signal(
            barrier, inc=1, device_id={"sec": lax.rem(sec + i, SEC)}, device_id_type=MESH
        )
        return carry

    partner = sec + 1 - 2 * core
    pl.semaphore_signal(
        barrier,
        inc=1,
        device_id={"tr": lax.rem(z + 2 * core - 1 + TR, TR), "sec": partner},
        device_id_type=MESH,
    )
    lax.fori_loop(1, SEC, greet_sec, 0)
    lax.fori_loop(1, TR, greet_tr, 0)

    line = iota((LINES, LINES), 0)
    other = iota((LINES, LINES), 1)

    def to_phys_major(value):
        matrix = ((line // ROWS) == lax.rem(other, PHYS)) & (
            lax.rem(line, ROWS) == (other // PHYS)
        )
        return dot(matrix.astype(BF16), value)

    def to_row_major(value):
        matrix = ((other // ROWS) == lax.rem(line, PHYS)) & (
            lax.rem(other, ROWS) == (line // PHYS)
        )
        return dot(matrix.astype(BF16), value)

    loads[3].wait()
    used_left = sizes[0, 0]
    used_right = sizes[0, 1]
    keep = ((z * ROWS + iota((LINES, WIDTH), 0) // PHYS) < used_right) & (
        iota((LINES, WIDTH), 1) < used_left
    )
    loads[0].wait()
    start = jnp.where(keep, psi_in[...].astype(F32).reshape(LINES, WIDTH), 0.0).astype(BF16)
    start_rows[...] = start
    cols_send[...] = columns_of(to_phys_major(start).astype(BF16))
    loads[1].wait()
    pc_send[...] = pc_in[...].astype(F32).reshape(TR, 2 * PHYS, WIDTH).astype(BF16)

    pl.semaphore_wait(barrier, TR + SEC - 1)

    def move_in_plane(n, source, middle):
        def send(i, carry):
            peer = plane_peer(i)
            remote(
                source.at[peer],
                middle.at[k],
                move_send_sem.at[n, 0],
                move_one_sem.at[n, k],
                plane(peer),
            ).start()
            return carry

        lax.fori_loop(1, TR, send, 0)
        middle[k] = source[k]
        ends.append(several(middle, TR - 1, move_send_sem.at[n, 0], move_two_sem.at[n]))

    def arrived(n, middle, index):
        return remote(
            middle.at[index],
            middle.at[index],
            move_send_sem.at[n, 0],
            move_one_sem.at[n, index],
            ring(lax.rem(z + 1, TR)),
        )

    def move_in_ring(n, middle, target):
        def send(i, carry):
            peer = ring_peer(i)

            @pl.when(peer != k)
            def _():
                arrived(n, middle, peer).wait_recv()

            remote(
                middle.at[peer], target.at[z], move_send_sem.at[n, 1], move_two_sem.at[n], ring(peer)
            ).start()
            return carry

        lax.fori_loop(0, TR - 1, send, 0)

        @pl.when(z != k)
        def _():
            arrived(n, middle, z).wait_recv()

        target[z] = middle[z]
        done = several(target, TR - 1, move_send_sem.at[n, 1], move_two_sem.at[n])
        ends.append(done)
        return done

    def back_in_ring(n, source, middle):
        def send(i, carry):
            peer = ring_peer(i)
            remote(
                source.at[peer],
                middle.at[z],
                move_send_sem.at[n, 0],
                move_one_sem.at[n, z],
                ring(peer),
            ).start()
            return carry

        lax.fori_loop(0, TR - 1, send, 0)
        middle[z] = source[z]
        ends.append(several(middle, TR - 1, move_send_sem.at[n, 0], move_two_sem.at[n]))

    def back_in_plane(n, middle, target):
        def forward(index):
            @pl.when(index != k)
            def _():
                remote(
                    middle.at[index],
                    target.at[k],
                    move_send_sem.at[n, 1],
                    move_two_sem.at[n],
                    plane(index),
                ).start()

        def send(i, carry):
            index = ring_source(i)
            arrived(n, middle, index).wait_recv()
            forward(index)
            return carry

        forward(z)
        lax.fori_loop(0, TR - 1, send, 0)
        target[k] = middle[k]
        done = several(target, TR - 1, move_send_sem.at[n, 1], move_two_sem.at[n])
        ends.append(done)
        return done

    def piece(m, i, rows=ROWS, first=0):
        return env.at[m, :, pl.ds(pl.multiple_of(i * ROWS + first, 16), rows), :]

    def scatter(m):
        used = used_right if m == 0 else used_left
        for d in range(3):

            @pl.when(gap == d)
            def _():
                env_loads[m].wait()
                for i in range(d, TR, 3):
                    span = pl.ds(i * ROWS, ROWS)
                    rows = own_env[m, :, span, :]
                    own_env[m, :, span, :] = jnp.where(i * ROWS < used, rows, jnp.zeros_like(rows))

                    @pl.when(k != i)
                    def _():
                        remote(
                            own_env.at[m, :, span, :],
                            land_env.at[m],
                            scatter_send_sem.at[m, i],
                            scatter_recv_sem.at[m],
                            plane(i),
                        ).start()

                    @pl.when(k == i)
                    def _():
                        land_env[m] = own_env[m, :, span, :]

    def scatter_end(m):
        for d in range(3):

            @pl.when(gap == d)
            def _():
                for i in range(d, TR, 3):

                    @pl.when(k != i)
                    def _():
                        remote(
                            own_env.at[m, :, pl.ds(i * ROWS, ROWS), :],
                            land_env.at[m],
                            scatter_send_sem.at[m, i],
                            scatter_recv_sem.at[m],
                            plane(i),
                        ).wait_send()

    shift = lax.rem(k, 3) - 1
    home = lax.rem(z - shift + TR, TR)

    def hand_over(m):
        return remote(
            land_env.at[m], piece(m, k), own_send_sem.at[m], own_recv_sem.at[m], ring(home)
        )

    def keep_here(m):
        return pltpu.make_async_copy(land_env.at[m], piece(m, k), own_recv_sem.at[m])

    def own_start(m):
        @pl.when(home != k)
        def _():
            remote(
                land_env.at[m],
                land_env.at[m],
                own_send_sem.at[m],
                scatter_recv_sem.at[m],
                ring(lax.rem(z + 1, TR)),
            ).wait_recv()

        @pl.when(shift != 0)
        def _():
            hand_over(m).start()

        @pl.when(shift == 0)
        def _():
            keep_here(m).start()

    def own_wait(m):
        @pl.when(shift != 0)
        def _():
            hand_over(m).wait_recv()

        @pl.when(shift == 0)
        def _():
            keep_here(m).wait()

    def row_peer(step):
        return 4 * y + lax.rem(x + step, 4)

    def column_peer(step):
        return 4 * lax.rem(y + step, 4) + x

    def gather_copy(m, ref, i, side, target):
        return remote(ref, ref, gather_send_sem.at[m], gather_recv_sem.at[m, i, side], plane(target))

    def gather_direct(m):
        for step in STEPS:
            gather_copy(m, piece(m, k), k, 0, row_peer(step)).start()
            gather_copy(m, piece(m, k), k, 0, column_peer(step)).start()

    def gather_forward(m):
        for step in STEPS:
            source = row_peer(4 - step)
            gather_copy(m, piece(m, source), source, 0, source).wait_recv()
            for turn in STEPS:
                gather_copy(m, piece(m, source, 16, 0), source, 0, column_peer(turn)).start()
            source = column_peer(4 - step)
            gather_copy(m, piece(m, source), source, 0, source).wait_recv()
            for turn in STEPS:
                gather_copy(m, piece(m, source, 16, 16), source, 1, row_peer(turn)).start()

    def gather_wait(m):
        for dy in STEPS:
            for dx in STEPS:
                source = 4 * lax.rem(y + dy, 4) + lax.rem(x + dx, 4)
                gather_copy(m, piece(m, source, 16, 0), source, 0, source).wait_recv()
                gather_copy(m, piece(m, source, 16, 16), source, 1, source).wait_recv()

    def gather_end(m):
        sent = env.at[m, :, pl.ds(0, WIDTH - ROWS), :]
        remote(
            sent, sent, gather_send_sem.at[m], own_recv_sem.at[m], ring(lax.rem(z + 1, TR))
        ).wait_send()

    def turn(n, source, target):
        def send(i, carry):
            peer = plane_peer(i)
            remote(
                source.at[peer], target.at[k], turn_send_sem.at[n], turn_recv_sem.at[n], plane(peer)
            ).start()
            return carry

        lax.fori_loop(1, TR, send, 0)
        target[k] = source[k]
        done = several(target, TR - 1, turn_send_sem.at[n], turn_recv_sem.at[n])
        ends.append(done)
        return done

    sector = 2 * z + core

    def shifts(n, source, target):
        copies = []
        for way in range(2):
            copy = remote(
                source,
                target.at[way],
                near_send_sem.at[n, way],
                near_recv_sem.at[n, way],
                {"tr": lax.rem(z + core - way + TR, TR), "sec": partner},
            )
            copy.start()
            copies.append(copy)
        ends.extend(copies)
        return copies

    def inside(way, value):
        exists = sector > 0 if way == 0 else sector < SEC - 1
        return jnp.where(exists, value, jnp.zeros_like(value))

    move_in_plane(0, cols_send, cols_mid)
    scatter(0)
    scatter(1)
    own_start(0)
    cols_done = move_in_ring(0, cols_mid, cols)
    own_start(1)
    own_wait(0)
    gather_direct(0)
    move_in_plane(1, pc_send, pc_mid)

    wide_line = iota((WIDTH, WIDTH), 0)
    wide_other = iota((WIDTH, WIDTH), 1)

    def old_row(r):
        return lax.rem(r, 32) // 2 * 32 + r // 32 * 2 + lax.rem(r, 2)

    to_new[...] = (old_row(wide_line) == wide_other).astype(BF16)
    gather_forward(0)
    own_wait(1)
    gather_direct(1)
    to_old[...] = (old_row(wide_other) == wide_line).astype(BF16)
    loads[2].wait()
    spread = ((iota((LINES, PHYS), 0) // ROWS) == iota((LINES, PHYS), 1)).astype(BF16)
    same_row = lax.rem(line, ROWS) == lax.rem(other, ROWS)
    for c in range(3):
        mixed = dot_nt(dot(spread, mix[c]).astype(BF16), spread)
        kron[c] = jnp.where(same_row, mixed, 0.0).astype(BF16)

    cols_done.wait_recv()
    copies = shifts(0, cols, near_cols)
    own_cols = cols[...].reshape(WIDTH, HALF)
    gather_wait(0)
    turns = []

    def reordered(value):
        return dot(to_new[...], value).astype(BF16).reshape(TR, ROWS, HALF)

    def right_part(c, value):
        return reordered(dot(env[0, c], value).astype(BF16))

    turn_send[0, :, 0] = right_part(0, own_cols)
    turn_send[0, :, 1] = reordered(own_cols)
    turns.append(turn(0, turn_send.at[0], turn_recv.at[0]))
    gather_forward(1)
    for way in range(2):
        copies[way].wait_recv()
        turn_send[1, :, way] = right_part(
            way + 1, inside(way, near_cols[way].reshape(WIDTH, HALF))
        )
    turns.append(turn(1, turn_send.at[1], turn_recv.at[1]))
    pc_done = move_in_ring(1, pc_mid, pc_new)
    gather_wait(1)
    total = None
    for c, (group, place) in enumerate(((0, 0), (1, 0), (1, 1))):
        if place == 0:
            turns[group].wait_recv()
        mixed = dot(kron[c], phys_major(turn_recv[group, :, place])).astype(BF16)
        term = dot_nt(mixed, env[1, c])
        total = term if total is None else total + term
    rounded = total.astype(BF16)
    first_send[...] = to_row_major(rounded).astype(BF16).reshape(TR, 2 * PHYS, WIDTH)
    image0 = rounded.astype(F32)
    s = phys_major(turn_recv[0, :, 1]).astype(F32)
    pc_done.wait_recv()
    factors = to_phys_major(pc_new[...].reshape(LINES, WIDTH))

    def tr_start(h, block):
        red_send[h, 0] = block

        def send(i, carry):
            remote(
                red_send.at[h, 0],
                red_tr.at[h, z],
                red_send_sem.at[h, 0],
                red_recv_sem.at[h, 0],
                ring(ring_peer(i)),
            ).start()
            return carry

        lax.fori_loop(0, TR - 1, send, 0)
        red_tr[h, z] = block
        done = several(red_tr.at[h], TR - 1, red_send_sem.at[h, 0], red_recv_sem.at[h, 0])
        ends.append(done)
        return done

    def sec_start(h, block):
        red_send[h, 1] = block

        def send(i, carry):
            remote(
                red_send.at[h, 1],
                red_sec.at[h, sec],
                red_send_sem.at[h, 1],
                red_recv_sem.at[h, 1],
                {"sec": lax.rem(sec + i, SEC)},
            ).start()
            return carry

        lax.fori_loop(1, SEC, send, 0)
        red_sec[h, sec] = block
        done = several(red_sec.at[h], SEC - 1, red_send_sem.at[h, 1], red_recv_sem.at[h, 1])
        ends.append(done)
        return done

    def means(block):
        whole = jnp.sum(block, axis=1, keepdims=True)
        return [whole[n : n + 1] / COUNT for n in range(4)]

    weighted = s * factors
    parts = (s * s, s * image0, weighted * image0, weighted * s)
    block = jnp.concatenate([partial_sum(part) for part in parts] * 2, axis=0)
    tr_start(0, block).wait_recv()
    back_in_ring(2, first_send, first_mid)
    sec_start(0, jnp.sum(red_tr[0], axis=0)).wait_recv()
    ss, sw, spw, sps = means(jnp.sum(red_sec[0], axis=0))
    norm = lax.rsqrt(ss + EPSILON)
    theta = norm * norm * sw
    along = norm * norm * (spw - theta * sps)

    def trial_of(image, vector, weights):
        return (image - theta * vector) * weights - along * vector

    trial = trial_of(image0, s, factors)
    trial_bf = trial.astype(BF16)
    vec[...] = trial_bf

    copies = shifts(1, vec, near_vec)
    turns = []

    def left_part(c, value):
        mixed = dot(kron[c], value).astype(BF16)
        return columns_of(dot_nt(mixed, env[1, c]).astype(BF16))

    half_send[0, :, 0] = left_part(0, trial_bf)
    half_send[0, :, 1] = columns_of(trial_bf)
    turns.append(turn(2, half_send.at[0], half_recv.at[0]))
    for way in range(2):
        copies[way].wait_recv()
        half_send[1, :, way] = left_part(way + 1, inside(way, near_vec[way]))
    turns.append(turn(3, half_send.at[1], half_recv.at[1]))
    second = trial_bf.astype(F32)
    tt = partial_sum(trial * trial)
    t0 = partial_sum(second * image0)
    total = None
    for c, (group, place) in enumerate(((0, 0), (1, 0), (1, 1))):
        if place == 0:
            turns[group].wait_recv()
        half = dot(to_old[...], half_recv[group, :, place].reshape(WIDTH, HALF)).astype(BF16)
        term = dot(env[0, c], half)
        total = term if total is None else total + term
    second_send[...] = total.astype(BF16).reshape(TR, ROWS, HALF)
    back_in_ring(3, second_send, second_mid)
    image1_cols = total.astype(BF16).astype(F32)
    trial_cols = dot(to_old[...], half_recv[0, :, 1].reshape(WIDTH, HALF))
    s1 = partial_sum(cols[...].reshape(WIDTH, HALF).astype(F32) * image1_cols)
    t1 = partial_sum(trial_cols * image1_cols)
    block = jnp.concatenate([tt, s1, t0, t1] * 2, axis=0)
    sec_start(1, block).wait_recv()
    sums_done = tr_start(1, jnp.sum(red_sec[1], axis=0))
    first_done = back_in_plane(2, first_mid, first_old)
    second_done = back_in_plane(3, second_mid, second_old)
    sums_done.wait_recv()
    tt, s1, t0, t1 = means(jnp.sum(red_tr[1], axis=0))

    fresh = norm * norm * tt
    grow = norm * lax.rsqrt(fresh + EPSILON)
    cross = 0.5 * norm * grow * (s1 + t0)
    corner = grow * grow * t1
    halfgap = 0.5 * (theta - corner)
    energy = 0.5 * (theta + corner) - jnp.sqrt(halfgap * halfgap + cross * cross)
    weight_one = corner - energy
    weight_two = -cross
    scale = lax.rsqrt(weight_one * weight_one + weight_two * weight_two)
    one = weight_one * scale * norm
    two = weight_two * scale * grow
    energy_out[...] = energy

    first_done.wait_recv()
    old_image = first_old[...].reshape(LINES, WIDTH).astype(F32)
    old_start = start_rows[...].astype(F32)
    old_factors = pc_send[...].reshape(LINES, WIDTH).astype(F32)
    old_trial = trial_of(old_image, old_start, old_factors).astype(BF16).astype(F32)
    ritz = one * old_start + two * old_trial
    psi_out[...] = ritz.reshape(ROWS, PHYS, WIDTH).astype(BF16)[None]
    partial = one * old_image - energy * ritz
    second_done.wait_recv()
    residual = partial + two * to_row_major(phys_major(second_old[...]))
    res_out[...] = residual.reshape(ROWS, PHYS, WIDTH).astype(BF16)[None]

    for m in range(2):
        scatter_end(m)
        gather_end(m)

        @pl.when(shift != 0)
        def _():
            hand_over(m).wait_send()

    for end in ends:
        end.wait_send()


def body(psi, precond, env_left, env_right, mixers, sizes):
    anywhere = pl.BlockSpec(memory_space=pl.ANY)
    vmem = pl.BlockSpec(memory_space=pltpu.VMEM)
    dma = pltpu.SemaphoreType.DMA
    columns = (TR, ROWS, HALF)
    pairs = (2, TR, 2, ROWS, HALF)
    rows = (TR, 2 * PHYS, WIDTH)
    psi_new, residual_new, energy = pl.pallas_call(
        kernel,
        out_shape=(
            jax.ShapeDtypeStruct(psi.shape, BF16),
            jax.ShapeDtypeStruct(psi.shape, BF16),
            jax.ShapeDtypeStruct((1, 1), F32),
        ),
        in_specs=[anywhere] * 6,
        out_specs=(vmem, vmem, vmem),
        scratch_shapes=[
            pltpu.VMEM((ROWS, PHYS, WIDTH), BF16),
            pltpu.VMEM((ROWS, PHYS, WIDTH), BF16),
            pltpu.VMEM((3, PHYS, PHYS), BF16),
            pltpu.SMEM((1, 2), jnp.int32),
            pltpu.VMEM((2, 3, WIDTH, WIDTH), BF16),
            pltpu.VMEM((2, 3, ROWS, WIDTH), BF16),
            pltpu.VMEM((2, 3, WIDTH, WIDTH), BF16),
            pltpu.VMEM((3, LINES, LINES), BF16),
            pltpu.VMEM((WIDTH, WIDTH), BF16),
            pltpu.VMEM((WIDTH, WIDTH), BF16),
            pltpu.VMEM((LINES, WIDTH), BF16),
            pltpu.VMEM(columns, BF16),
            pltpu.VMEM(columns, BF16),
            pltpu.VMEM(columns, BF16),
            pltpu.VMEM((2, *columns), BF16),
            pltpu.VMEM(pairs, BF16),
            pltpu.VMEM(pairs, BF16),
            pltpu.VMEM(rows, BF16),
            pltpu.VMEM(rows, BF16),
            pltpu.VMEM(rows, BF16),
            pltpu.VMEM((LINES, WIDTH), BF16),
            pltpu.VMEM((2, LINES, WIDTH), BF16),
            pltpu.VMEM(pairs, BF16),
            pltpu.VMEM(pairs, BF16),
            pltpu.VMEM(rows, BF16),
            pltpu.VMEM(rows, BF16),
            pltpu.VMEM(rows, BF16),
            pltpu.VMEM(columns, BF16),
            pltpu.VMEM(columns, BF16),
            pltpu.VMEM(columns, BF16),
            pltpu.VMEM((2, 2, 8, 128), F32),
            pltpu.VMEM((2, TR, 8, 128), F32),
            pltpu.VMEM((2, SEC, 8, 128), F32),
            dma((6,)),
            dma((2, TR)),
            dma((2,)),
            dma((2,)),
            dma((2,)),
            dma((2,)),
            dma((2, TR, 2)),
            dma((2, 2)),
            dma((2, 2)),
            dma((4,)),
            dma((4,)),
            dma((4, 2)),
            dma((4, TR)),
            dma((4,)),
            dma((2, 2)),
            dma((2, 2)),
        ],
        compiler_params=pltpu.CompilerParams(
            collective_id=0, has_side_effects=True, vmem_limit_bytes=60 * 1024 * 1024
        ),
        cost_estimate=pl.CostEstimate(
            flops=2_200_000_000, bytes_accessed=2_000_000, transcendentals=0
        ),
    )(psi, precond, env_left, env_right, mixers, sizes)
    return psi_new, residual_new, energy.reshape(())


def solution(mesh):
    placed = (
        P("sec", "tr", None, None),
        P("sec", "tr", None, None),
        P(None, "sec", None, None),
        P(None, "sec", None, None),
        P(),
        P("sec", None),
    )
    return jax.shard_map(
        body,
        mesh=mesh,
        in_specs=placed,
        out_specs=(P("sec", "tr", None, None), P("sec", "tr", None, None), P()),
        check_vma=False,
    )
```

```python
import jax
import jax.numpy as jnp
from jax import lax
from jax.experimental import pallas as pl
from jax.experimental.pallas import tpu as pltpu
from jax.sharding import PartitionSpec as P

EPSILON = 1e-06
MESH = pl.DeviceIdType.MESH
F32 = jnp.float32
BF16 = jnp.bfloat16
TR = 16
SEC = 32
ROWS = 32
PHYS = 8
WIDTH = 512
HALF = 256
LINES = ROWS * PHYS
COUNT = float(SEC * WIDTH * PHYS * WIDTH)


def dot(a, b):
    return jnp.dot(a, b, preferred_element_type=F32)


def dot_nt(a, b):
    return lax.dot_general(a, b, (((1,), (1,)), ((), ())), preferred_element_type=F32)


def iota(shape, axis):
    return lax.broadcasted_iota(jnp.int32, shape, axis)


def partial_sum(x):
    rows = jnp.sum(x, axis=0, keepdims=True)
    total = rows[:, 0:128]
    for lane in range(128, x.shape[1], 128):
        total = total + rows[:, lane : lane + 128]
    return total


def phys_major(block):
    pieces = [jnp.concatenate([block[2 * p], block[2 * p + 1]], axis=1) for p in range(PHYS)]
    return jnp.concatenate(pieces, axis=0)


def store_columns(ref, value):
    for j in range(TR):
        p, side = divmod(j, 2)
        ref[j] = value[p * ROWS : (p + 1) * ROWS, side * HALF : (side + 1) * HALF]


def kernel(
    psi_hbm,
    pc_hbm,
    left_hbm,
    right_hbm,
    mix_hbm,
    sizes_hbm,
    psi_out,
    res_out,
    energy_out,
    psi_in,
    pc_in,
    mix,
    sizes,
    own_env,
    land_env,
    env,
    kron,
    to_new,
    to_old,
    start_rows,
    cols_send,
    cols_mid,
    cols,
    near_cols,
    turn_send,
    turn_recv,
    pc_send,
    pc_mid,
    pc_new,
    vec,
    near_vec,
    half_send,
    half_recv,
    first_send,
    first_mid,
    first_old,
    second_send,
    second_mid,
    second_old,
    red_send,
    red_tr,
    red_sec,
    in_sem,
    scatter_send_sem,
    scatter_recv_sem,
    own_send_sem,
    own_recv_sem,
    gather_send_sem,
    gather_recv_sem,
    near_send_sem,
    near_recv_sem,
    turn_send_sem,
    turn_recv_sem,
    move_send_sem,
    move_one_sem,
    move_two_sem,
    red_send_sem,
    red_recv_sem,
):
    z = lax.axis_index("tr")
    sec = lax.axis_index("sec")
    k = sec // 2
    core = lax.rem(sec, 2)
    y = k // 4
    x = lax.rem(k, 4)

    def ring(z2):
        return {"tr": z2}

    def plane(k2):
        return {"sec": 2 * k2 + core}

    def turned(m):
        return jnp.where(m >= TR - 1, m - (TR - 1), m)

    def ring_peer(i):
        m = turned(i + k)
        step = m // 2 + 1
        return lax.rem(z + jnp.where(lax.rem(m, 2) == 0, step, TR - step), TR)

    def ring_source(i):
        m = turned(i + k)
        step = m // 2 + 1
        return lax.rem(z + jnp.where(lax.rem(m, 2) == 0, TR - step, step), TR)

    def plane_peer(i):
        return 4 * lax.rem(y + i // 4, 4) + lax.rem(x + lax.rem(i, 4), 4)

    def remote(src, dst, send_sem, recv_sem, device):
        return pltpu.make_async_remote_copy(
            src_ref=src,
            dst_ref=dst,
            send_sem=send_sem,
            recv_sem=recv_sem,
            device_id=device,
            device_id_type=MESH,
        )

    def several(ref, count, send_sem, recv_sem):
        part = ref.at[pl.ds(0, count)]
        return remote(part, part, send_sem, recv_sem, ring(lax.rem(z + 1, TR)))

    ends = []

    loads = [
        pltpu.make_async_copy(psi_hbm.at[0], psi_in, in_sem.at[0]),
        pltpu.make_async_copy(pc_hbm.at[0], pc_in, in_sem.at[1]),
        pltpu.make_async_copy(mix_hbm, mix, in_sem.at[2]),
        pltpu.make_async_copy(sizes_hbm, sizes, in_sem.at[3]),
    ]
    env_loads = [
        pltpu.make_async_copy(right_hbm.at[:, 0], own_env.at[0], in_sem.at[4]),
        pltpu.make_async_copy(left_hbm.at[:, 0], own_env.at[1], in_sem.at[5]),
    ]
    for load in loads:
        load.start()
    gap = lax.rem(z - k + TR + 1, TR)

    @pl.when(gap < 4)
    def _():
        for load in env_loads:
            load.start()

    barrier = pltpu.get_barrier_semaphore()

    def greet_tr(i, carry):
        pl.semaphore_signal(barrier, inc=1, device_id=ring(lax.rem(z + i, TR)), device_id_type=MESH)
        return carry

    def greet_sec(i, carry):
        pl.semaphore_signal(
            barrier, inc=1, device_id={"sec": lax.rem(sec + i, SEC)}, device_id_type=MESH
        )
        return carry

    partner = sec + 1 - 2 * core
    pl.semaphore_signal(
        barrier,
        inc=1,
        device_id={"tr": lax.rem(z + 2 * core - 1 + TR, TR), "sec": partner},
        device_id_type=MESH,
    )
    lax.fori_loop(1, SEC, greet_sec, 0)
    lax.fori_loop(1, TR, greet_tr, 0)

    line = iota((LINES, LINES), 0)
    other = iota((LINES, LINES), 1)

    def to_phys_major(value):
        matrix = ((line // ROWS) == lax.rem(other, PHYS)) & (
            lax.rem(line, ROWS) == (other // PHYS)
        )
        return dot(matrix.astype(BF16), value)

    def to_row_major(value):
        matrix = ((other // ROWS) == lax.rem(line, PHYS)) & (
            lax.rem(other, ROWS) == (line // PHYS)
        )
        return dot(matrix.astype(BF16), value)

    loads[3].wait()
    used_left = sizes[0, 0]
    used_right = sizes[0, 1]
    keep = ((z * ROWS + iota((LINES, WIDTH), 0) // PHYS) < used_right) & (
        iota((LINES, WIDTH), 1) < used_left
    )
    loads[0].wait()
    start = jnp.where(keep, psi_in[...].astype(F32).reshape(LINES, WIDTH), 0.0).astype(BF16)
    start_rows[...] = start
    store_columns(cols_send, to_phys_major(start).astype(BF16))
    loads[1].wait()
    pc_send[...] = pc_in[...].astype(F32).reshape(TR, 2 * PHYS, WIDTH).astype(BF16)

    pl.semaphore_wait(barrier, TR + SEC - 1)

    def move_in_plane(n, source, middle):
        def send(i, carry):
            peer = plane_peer(i)
            remote(
                source.at[peer],
                middle.at[k],
                move_send_sem.at[n, 0],
                move_one_sem.at[n, k],
                plane(peer),
            ).start()
            return carry

        lax.fori_loop(1, TR, send, 0)
        middle[k] = source[k]
        ends.append(several(middle, TR - 1, move_send_sem.at[n, 0], move_two_sem.at[n]))

    def arrived(n, middle, index):
        return remote(
            middle.at[index],
            middle.at[index],
            move_send_sem.at[n, 0],
            move_one_sem.at[n, index],
            ring(lax.rem(z + 1, TR)),
        )

    def ring_sends(n, middle, target, begin, end):
        def send(i, carry):
            peer = ring_peer(i)

            @pl.when(peer != k)
            def _():
                arrived(n, middle, peer).wait_recv()

            remote(
                middle.at[peer], target.at[z], move_send_sem.at[n, 1], move_two_sem.at[n], ring(peer)
            ).start()
            return carry

        lax.fori_loop(begin, end, send, 0)

    def ring_rest(n, middle, target):
        @pl.when(z != k)
        def _():
            arrived(n, middle, z).wait_recv()

        target[z] = middle[z]
        done = several(target, TR - 1, move_send_sem.at[n, 1], move_two_sem.at[n])
        ends.append(done)
        return done

    def back_in_ring(n, source, middle):
        def send(i, carry):
            peer = ring_peer(i)
            remote(
                source.at[peer],
                middle.at[z],
                move_send_sem.at[n, 0],
                move_one_sem.at[n, z],
                ring(peer),
            ).start()
            return carry

        lax.fori_loop(0, TR - 1, send, 0)
        middle[z] = source[z]
        ends.append(several(middle, TR - 1, move_send_sem.at[n, 0], move_two_sem.at[n]))

    def back_in_plane(n, middle, target):
        def forward(index):
            @pl.when(index != k)
            def _():
                remote(
                    middle.at[index],
                    target.at[k],
                    move_send_sem.at[n, 1],
                    move_two_sem.at[n],
                    plane(index),
                ).start()

        def send(i, carry):
            index = ring_source(i)
            arrived(n, middle, index).wait_recv()
            forward(index)
            return carry

        forward(z)
        lax.fori_loop(0, TR - 1, send, 0)
        target[k] = middle[k]
        done = several(target, TR - 1, move_send_sem.at[n, 1], move_two_sem.at[n])
        ends.append(done)
        return done

    def env_matrix(m, c):
        return env[m, c].reshape(WIDTH, WIDTH)

    def piece(m, dy, dx, lanes=pl.ds(0, WIDTH)):
        return env.at[m, :, lax.rem(y + dy + 4, 4), lax.rem(x + dx + 4, 4), :, lanes]

    def row_set(m, dy, lanes):
        return env.at[m, :, lax.rem(y + dy + 4, 4), :, :, lanes]

    def column_set(m, dx, lanes):
        return env.at[m, :, :, lax.rem(x + dx + 4, 4), :, lanes]

    def scatter_copy(m, d, n):
        return remote(
            own_env.at[m, :, pl.ds((4 * d + n) * ROWS, ROWS), :],
            land_env.at[m],
            scatter_send_sem.at[m, n],
            scatter_recv_sem.at[m],
            plane(4 * d + n),
        )

    def scatter(m):
        used = used_right if m == 0 else used_left
        for d in range(4):

            @pl.when(gap == d)
            def _():
                env_loads[m].wait()
                span = pl.ds(4 * d * ROWS, 4 * ROWS)
                rows = own_env[m, :, span, :]
                own_env[m, :, span, :] = jnp.where(4 * d * ROWS < used, rows, jnp.zeros_like(rows))
                for n in range(4):

                    @pl.when(k != 4 * d + n)
                    def _():
                        scatter_copy(m, d, n).start()

                    @pl.when(k == 4 * d + n)
                    def _():
                        land_env[m] = own_env[m, :, pl.ds((4 * d + n) * ROWS, ROWS), :]

    def scatter_end(m):
        for d in range(4):

            @pl.when(gap == d)
            def _():
                for n in range(4):

                    @pl.when(k != 4 * d + n)
                    def _():
                        scatter_copy(m, d, n).wait_send()

    shift = y - 1
    home = lax.rem(z - shift + TR, TR)

    def hand_over(m):
        return remote(
            land_env.at[m], piece(m, 0, 0), own_send_sem.at[m], own_recv_sem.at[m], ring(home)
        )

    def keep_here(m):
        return pltpu.make_async_copy(land_env.at[m], piece(m, 0, 0), own_recv_sem.at[m])

    def own_start(m):
        @pl.when(home != k)
        def _():
            remote(
                land_env.at[m],
                land_env.at[m],
                own_send_sem.at[m],
                scatter_recv_sem.at[m],
                ring(lax.rem(z + 1, TR)),
            ).wait_recv()

        @pl.when(shift != 0)
        def _():
            hand_over(m).start()

        @pl.when(shift == 0)
        def _():
            keep_here(m).start()

    def own_wait(m):
        @pl.when(shift != 0)
        def _():
            hand_over(m).wait_recv()

        @pl.when(shift == 0)
        def _():
            keep_here(m).wait()

    first = pl.ds(0, HALF)
    last = pl.ds(HALF, HALF)
    quarters = [pl.ds(128 * n, 128) for n in range(4)]

    def hop(m, n, ref, dy, dx):
        target = 4 * lax.rem(y + dy + 4, 4) + lax.rem(x + dx + 4, 4)
        return remote(ref, ref, gather_send_sem.at[m], gather_recv_sem.at[m, n], plane(target))

    def gather_one(m):
        own_wait(m)
        hop(m, 0, piece(m, 0, 0, first), 0, 1).start()
        hop(m, 1, piece(m, 0, 0, first), 0, -1).start()
        hop(m, 2, piece(m, 0, 0, last), 1, 0).start()
        hop(m, 3, piece(m, 0, 0, last), -1, 0).start()

    def gather_two(m):
        hop(m, 0, piece(m, 0, -1, first), 0, -1).wait_recv()
        hop(m, 4, piece(m, 0, -1, quarters[0]), 0, 1).start()
        hop(m, 1, piece(m, 0, 1, first), 0, 1).wait_recv()
        hop(m, 5, piece(m, 0, 1, quarters[1]), 0, -1).start()
        hop(m, 2, piece(m, -1, 0, last), -1, 0).wait_recv()
        hop(m, 6, piece(m, -1, 0, quarters[2]), 1, 0).start()
        hop(m, 3, piece(m, 1, 0, last), 1, 0).wait_recv()
        hop(m, 7, piece(m, 1, 0, quarters[3]), -1, 0).start()

    def gather_three(m):
        hop(m, 4, piece(m, 0, 2, quarters[0]), 0, -1).wait_recv()
        hop(m, 5, piece(m, 0, 2, quarters[1]), 0, 1).wait_recv()
        hop(m, 8, row_set(m, 0, first), 1, 0).start()
        hop(m, 9, row_set(m, 0, first), -1, 0).start()
        hop(m, 6, piece(m, 2, 0, quarters[2]), -1, 0).wait_recv()
        hop(m, 7, piece(m, 2, 0, quarters[3]), 1, 0).wait_recv()
        hop(m, 10, column_set(m, 0, last), 0, 1).start()
        hop(m, 11, column_set(m, 0, last), 0, -1).start()

    def gather_four(m):
        hop(m, 8, row_set(m, -1, first), -1, 0).wait_recv()
        hop(m, 12, row_set(m, -1, quarters[0]), 1, 0).start()
        hop(m, 9, row_set(m, 1, first), 1, 0).wait_recv()
        hop(m, 13, row_set(m, 1, quarters[1]), -1, 0).start()
        hop(m, 10, column_set(m, -1, last), 0, -1).wait_recv()
        hop(m, 14, column_set(m, -1, quarters[2]), 0, 1).start()
        hop(m, 11, column_set(m, 1, last), 0, 1).wait_recv()
        hop(m, 15, column_set(m, 1, quarters[3]), 0, -1).start()

    def gather_wait(m):
        hop(m, 12, row_set(m, 2, quarters[0]), -1, 0).wait_recv()
        hop(m, 13, row_set(m, 2, quarters[1]), 1, 0).wait_recv()
        hop(m, 14, column_set(m, 2, quarters[2]), 0, -1).wait_recv()
        hop(m, 15, column_set(m, 2, quarters[3]), 0, 1).wait_recv()

    def gather_end(m):
        sent = own_env.at[m, :, pl.ds(0, WIDTH - ROWS), :]
        remote(
            sent, sent, gather_send_sem.at[m], own_recv_sem.at[m], ring(lax.rem(z + 1, TR))
        ).wait_send()

    def turn(n, source, target):
        def send(i, carry):
            peer = plane_peer(i)
            remote(
                source.at[:, peer],
                target.at[:, k],
                turn_send_sem.at[n],
                turn_recv_sem.at[n],
                plane(peer),
            ).start()
            return carry

        lax.fori_loop(1, TR, send, 0)
        for place in range(2):
            target[place, k] = source[place, k]
        part = target.at[:, pl.ds(0, TR - 1)]
        done = remote(
            part, part, turn_send_sem.at[n], turn_recv_sem.at[n], ring(lax.rem(z + 1, TR))
        )
        ends.append(done)
        return done

    sector = 2 * z + core

    def shifts(n, source, target):
        copies = []
        for way in range(2):
            copy = remote(
                source,
                target.at[way],
                near_send_sem.at[n, way],
                near_recv_sem.at[n, way],
                {"tr": lax.rem(z + core - way + TR, TR), "sec": partner},
            )
            copy.start()
            copies.append(copy)
        ends.extend(copies)
        return copies

    def inside(way, value):
        exists = sector > 0 if way == 0 else sector < SEC - 1
        return jnp.where(exists, value, jnp.zeros_like(value))

    move_in_plane(0, cols_send, cols_mid)
    scatter(0)
    scatter(1)
    own_start(0)
    ring_sends(0, cols_mid, cols, 0, 7)
    own_start(1)
    ring_sends(0, cols_mid, cols, 7, TR - 1)
    cols_done = ring_rest(0, cols_mid, cols)
    gather_one(0)

    wide_line = iota((WIDTH, WIDTH), 0)
    wide_other = iota((WIDTH, WIDTH), 1)

    def old_row(r):
        return lax.rem(r, 32) // 2 * 32 + r // 32 * 2 + lax.rem(r, 2)

    to_new[...] = (old_row(wide_line) == wide_other).astype(BF16)
    gather_two(0)
    gather_one(1)
    move_in_plane(1, pc_send, pc_mid)
    gather_three(0)
    gather_two(1)
    to_old[...] = (old_row(wide_other) == wide_line).astype(BF16)
    loads[2].wait()
    spread = ((iota((LINES, PHYS), 0) // ROWS) == iota((LINES, PHYS), 1)).astype(BF16)
    same_row = lax.rem(line, ROWS) == lax.rem(other, ROWS)
    for c in range(3):
        mixed = dot_nt(dot(spread, mix[c]).astype(BF16), spread)
        kron[c] = jnp.where(same_row, mixed, 0.0).astype(BF16)
    gather_three(1)
    gather_four(0)

    cols_done.wait_recv()
    copies = shifts(0, cols, near_cols)
    own_cols = cols[...].reshape(WIDTH, HALF)
    gather_wait(0)
    turns = []

    def reordered(value):
        return dot(to_new[...], value).astype(BF16).reshape(TR, ROWS, HALF)

    def right_part(c, value):
        return reordered(dot(env_matrix(0, c), value).astype(BF16))

    turn_send[0, 0] = right_part(0, own_cols)
    turn_send[0, 1] = reordered(own_cols)
    turns.append(turn(0, turn_send.at[0], turn_recv.at[0]))
    gather_four(1)
    for way in range(2):
        copies[way].wait_recv()
        turn_send[1, way] = right_part(
            way + 1, inside(way, near_cols[way].reshape(WIDTH, HALF))
        )
    turns.append(turn(1, turn_send.at[1], turn_recv.at[1]))
    ring_sends(1, pc_mid, pc_new, 0, TR - 1)
    pc_done = ring_rest(1, pc_mid, pc_new)
    gather_wait(1)
    total = None
    for c, (group, place) in enumerate(((0, 0), (1, 0), (1, 1))):
        if place == 0:
            turns[group].wait_recv()
        mixed = dot(kron[c], phys_major(turn_recv[group, place])).astype(BF16)
        term = dot_nt(mixed, env_matrix(1, c))
        total = term if total is None else total + term
    rounded = total.astype(BF16)
    first_send[...] = to_row_major(rounded).astype(BF16).reshape(TR, 2 * PHYS, WIDTH)
    image0 = rounded.astype(F32)
    s = phys_major(turn_recv[0, 1]).astype(F32)
    pc_done.wait_recv()
    factors = to_phys_major(pc_new[...].reshape(LINES, WIDTH))

    def tr_start(h, block):
        red_send[h, 0] = block

        def send(i, carry):
            remote(
                red_send.at[h, 0],
                red_tr.at[h, z],
                red_send_sem.at[h, 0],
                red_recv_sem.at[h, 0],
                ring(ring_peer(i)),
            ).start()
            return carry

        lax.fori_loop(0, TR - 1, send, 0)
        red_tr[h, z] = block
        done = several(red_tr.at[h], TR - 1, red_send_sem.at[h, 0], red_recv_sem.at[h, 0])
        ends.append(done)
        return done

    def sec_start(h, block):
        red_send[h, 1] = block

        def send(i, carry):
            remote(
                red_send.at[h, 1],
                red_sec.at[h, sec],
                red_send_sem.at[h, 1],
                red_recv_sem.at[h, 1],
                {"sec": lax.rem(sec + i, SEC)},
            ).start()
            return carry

        lax.fori_loop(1, SEC, send, 0)
        red_sec[h, sec] = block
        done = several(red_sec.at[h], SEC - 1, red_send_sem.at[h, 1], red_recv_sem.at[h, 1])
        ends.append(done)
        return done

    def means(block):
        whole = jnp.sum(block, axis=1, keepdims=True)
        return [whole[n : n + 1] / COUNT for n in range(4)]

    weighted = s * factors
    parts = (s * s, s * image0, weighted * image0, weighted * s)
    block = jnp.concatenate([partial_sum(part) for part in parts] * 2, axis=0)
    tr_start(0, block).wait_recv()
    back_in_ring(2, first_send, first_mid)
    sec_start(0, jnp.sum(red_tr[0], axis=0)).wait_recv()
    ss, sw, spw, sps = means(jnp.sum(red_sec[0], axis=0))
    norm = lax.rsqrt(ss + EPSILON)
    theta = norm * norm * sw
    along = norm * norm * (spw - theta * sps)

    def trial_of(image, vector, weights):
        return (image - theta * vector) * weights - along * vector

    trial = trial_of(image0, s, factors)
    trial_bf = trial.astype(BF16)
    vec[...] = trial_bf

    copies = shifts(1, vec, near_vec)
    turns = []

    def left_part(c, value):
        mixed = dot(kron[c], value).astype(BF16)
        return dot_nt(mixed, env_matrix(1, c)).astype(BF16)

    store_columns(half_send.at[0, 0], left_part(0, trial_bf))
    store_columns(half_send.at[0, 1], trial_bf)
    turns.append(turn(2, half_send.at[0], half_recv.at[0]))
    for way in range(2):
        copies[way].wait_recv()
        store_columns(half_send.at[1, way], left_part(way + 1, inside(way, near_vec[way])))
    turns.append(turn(3, half_send.at[1], half_recv.at[1]))
    second = trial_bf.astype(F32)
    tt = partial_sum(trial * trial)
    t0 = partial_sum(second * image0)
    total = None
    for c, (group, place) in enumerate(((0, 0), (1, 0), (1, 1))):
        if place == 0:
            turns[group].wait_recv()
        half = dot(to_old[...], half_recv[group, place].reshape(WIDTH, HALF)).astype(BF16)
        term = dot(env_matrix(0, c), half)
        total = term if total is None else total + term
    second_send[...] = total.astype(BF16).reshape(TR, ROWS, HALF)
    back_in_ring(3, second_send, second_mid)
    image1_cols = total.astype(BF16).astype(F32)
    trial_cols = dot(to_old[...], half_recv[0, 1].reshape(WIDTH, HALF))
    s1 = partial_sum(cols[...].reshape(WIDTH, HALF).astype(F32) * image1_cols)
    t1 = partial_sum(trial_cols * image1_cols)
    block = jnp.concatenate([tt, s1, t0, t1] * 2, axis=0)
    sec_start(1, block).wait_recv()
    sums_done = tr_start(1, jnp.sum(red_sec[1], axis=0))
    first_done = back_in_plane(2, first_mid, first_old)
    second_done = back_in_plane(3, second_mid, second_old)
    sums_done.wait_recv()
    tt, s1, t0, t1 = means(jnp.sum(red_tr[1], axis=0))

    fresh = norm * norm * tt
    grow = norm * lax.rsqrt(fresh + EPSILON)
    cross = 0.5 * norm * grow * (s1 + t0)
    corner = grow * grow * t1
    halfgap = 0.5 * (theta - corner)
    energy = 0.5 * (theta + corner) - jnp.sqrt(halfgap * halfgap + cross * cross)
    weight_one = corner - energy
    weight_two = -cross
    scale = lax.rsqrt(weight_one * weight_one + weight_two * weight_two)
    one = weight_one * scale * norm
    two = weight_two * scale * grow
    energy_out[...] = energy

    first_done.wait_recv()
    old_image = first_old[...].reshape(LINES, WIDTH).astype(F32)
    old_start = start_rows[...].astype(F32)
    old_factors = pc_send[...].reshape(LINES, WIDTH).astype(F32)
    old_trial = trial_of(old_image, old_start, old_factors).astype(BF16).astype(F32)
    ritz = one * old_start + two * old_trial
    psi_out[...] = ritz.reshape(ROWS, PHYS, WIDTH).astype(BF16)[None]
    partial = one * old_image - energy * ritz
    second_done.wait_recv()
    residual = partial + two * to_row_major(phys_major(second_old[...]))
    res_out[...] = residual.reshape(ROWS, PHYS, WIDTH).astype(BF16)[None]

    for m in range(2):
        scatter_end(m)
        gather_end(m)

        @pl.when(shift != 0)
        def _():
            hand_over(m).wait_send()

    for end in ends:
        end.wait_send()


def body(psi, precond, env_left, env_right, mixers, sizes):
    anywhere = pl.BlockSpec(memory_space=pl.ANY)
    vmem = pl.BlockSpec(memory_space=pltpu.VMEM)
    dma = pltpu.SemaphoreType.DMA
    columns = (TR, ROWS, HALF)
    pairs = (2, 2, TR, ROWS, HALF)
    rows = (TR, 2 * PHYS, WIDTH)
    psi_new, residual_new, energy = pl.pallas_call(
        kernel,
        out_shape=(
            jax.ShapeDtypeStruct(psi.shape, BF16),
            jax.ShapeDtypeStruct(psi.shape, BF16),
            jax.ShapeDtypeStruct((1, 1), F32),
        ),
        in_specs=[anywhere] * 6,
        out_specs=(vmem, vmem, vmem),
        scratch_shapes=[
            pltpu.VMEM((ROWS, PHYS, WIDTH), BF16),
            pltpu.VMEM((ROWS, PHYS, WIDTH), BF16),
            pltpu.VMEM((3, PHYS, PHYS), BF16),
            pltpu.SMEM((1, 2), jnp.int32),
            pltpu.VMEM((2, 3, WIDTH, WIDTH), BF16),
            pltpu.VMEM((2, 3, ROWS, WIDTH), BF16),
            pltpu.VMEM((2, 3, 4, 4, ROWS, WIDTH), BF16),
            pltpu.VMEM((3, LINES, LINES), BF16),
            pltpu.VMEM((WIDTH, WIDTH), BF16),
            pltpu.VMEM((WIDTH, WIDTH), BF16),
            pltpu.VMEM((LINES, WIDTH), BF16),
            pltpu.VMEM(columns, BF16),
            pltpu.VMEM(columns, BF16),
            pltpu.VMEM(columns, BF16),
            pltpu.VMEM((2, *columns), BF16),
            pltpu.VMEM(pairs, BF16),
            pltpu.VMEM(pairs, BF16),
            pltpu.VMEM(rows, BF16),
            pltpu.VMEM(rows, BF16),
            pltpu.VMEM(rows, BF16),
            pltpu.VMEM((LINES, WIDTH), BF16),
            pltpu.VMEM((2, LINES, WIDTH), BF16),
            pltpu.VMEM(pairs, BF16),
            pltpu.VMEM(pairs, BF16),
            pltpu.VMEM(rows, BF16),
            pltpu.VMEM(rows, BF16),
            pltpu.VMEM(rows, BF16),
            pltpu.VMEM(columns, BF16),
            pltpu.VMEM(columns, BF16),
            pltpu.VMEM(columns, BF16),
            pltpu.VMEM((2, 2, 8, 128), F32),
            pltpu.VMEM((2, TR, 8, 128), F32),
            pltpu.VMEM((2, SEC, 8, 128), F32),
            dma((6,)),
            dma((2, 4)),
            dma((2,)),
            dma((2,)),
            dma((2,)),
            dma((2,)),
            dma((2, 16)),
            dma((2, 2)),
            dma((2, 2)),
            dma((4,)),
            dma((4,)),
            dma((4, 2)),
            dma((4, TR)),
            dma((4,)),
            dma((2, 2)),
            dma((2, 2)),
        ],
        compiler_params=pltpu.CompilerParams(
            collective_id=0, has_side_effects=True, vmem_limit_bytes=60 * 1024 * 1024
        ),
        cost_estimate=pl.CostEstimate(
            flops=2_200_000_000, bytes_accessed=2_000_000, transcendentals=0
        ),
    )(psi, precond, env_left, env_right, mixers, sizes)
    return psi_new, residual_new, energy.reshape(())


def solution(mesh):
    placed = (
        P("sec", "tr", None, None),
        P("sec", "tr", None, None),
        P(None, "sec", None, None),
        P(None, "sec", None, None),
        P(),
        P("sec", None),
    )
    return jax.shard_map(
        body,
        mesh=mesh,
        in_specs=placed,
        out_specs=(P("sec", "tr", None, None), P("sec", "tr", None, None), P()),
        check_vma=False,
    )
```

```python
import jax
import jax.numpy as jnp
from jax import lax
from jax.experimental import pallas as pl
from jax.experimental.pallas import tpu as pltpu
from jax.sharding import PartitionSpec as P

EPSILON = 1e-06
MESH = pl.DeviceIdType.MESH
F32 = jnp.float32
BF16 = jnp.bfloat16
TR = 16
SEC = 32
ROWS = 32
PHYS = 8
WIDTH = 512
HALF = 256
LINES = ROWS * PHYS
COUNT = float(SEC * WIDTH * PHYS * WIDTH)
STEPS = (1, 3, 2)


def dot(a, b):
    return jnp.dot(a, b, preferred_element_type=F32)


def dot_nt(a, b):
    return lax.dot_general(a, b, (((1,), (1,)), ((), ())), preferred_element_type=F32)


def iota(shape, axis):
    return lax.broadcasted_iota(jnp.int32, shape, axis)


def partial_sum(x):
    rows = jnp.sum(x, axis=0, keepdims=True)
    total = rows[:, 0:128]
    for lane in range(128, x.shape[1], 128):
        total = total + rows[:, lane : lane + 128]
    return total


def phys_major(block):
    pieces = [jnp.concatenate([block[2 * p], block[2 * p + 1]], axis=1) for p in range(PHYS)]
    return jnp.concatenate(pieces, axis=0)


def store_columns(ref, value):
    for j in range(TR):
        p, side = divmod(j, 2)
        ref[j] = value[p * ROWS : (p + 1) * ROWS, side * HALF : (side + 1) * HALF]


def kernel(
    psi_hbm,
    pc_hbm,
    left_hbm,
    right_hbm,
    mix_hbm,
    sizes_hbm,
    psi_out,
    res_out,
    energy_out,
    psi_in,
    pc_in,
    mix,
    sizes,
    own_env,
    land_env,
    env,
    kron,
    to_new,
    to_old,
    start_rows,
    cols_send,
    cols_mid,
    cols,
    near_cols,
    turn_send,
    turn_recv,
    pc_send,
    pc_mid,
    pc_new,
    vec,
    near_vec,
    half_send,
    half_recv,
    first_send,
    first_old,
    second_send,
    second_old,
    red_send,
    red_tr,
    red_sec,
    in_sem,
    scatter_send_sem,
    scatter_recv_sem,
    own_send_sem,
    own_recv_sem,
    gather_send_sem,
    gather_recv_sem,
    near_send_sem,
    near_recv_sem,
    turn_send_sem,
    turn_recv_sem,
    move_send_sem,
    move_one_sem,
    move_two_sem,
    red_send_sem,
    red_recv_sem,
):
    z = lax.axis_index("tr")
    sec = lax.axis_index("sec")
    k = sec // 2
    core = lax.rem(sec, 2)
    y = k // 4
    x = lax.rem(k, 4)

    def ring(z2):
        return {"tr": z2}

    def plane(k2):
        return {"sec": 2 * k2 + core}

    def turned(m):
        return jnp.where(m >= TR - 1, m - (TR - 1), m)

    def ring_peer(i):
        m = turned(i + k)
        step = m // 2 + 1
        return lax.rem(z + jnp.where(lax.rem(m, 2) == 0, step, TR - step), TR)

    def ring_source(i):
        m = turned(i + k)
        step = m // 2 + 1
        return lax.rem(z + jnp.where(lax.rem(m, 2) == 0, TR - step, step), TR)

    def plane_peer(i):
        return 4 * lax.rem(y + i // 4, 4) + lax.rem(x + lax.rem(i, 4), 4)

    def remote(src, dst, send_sem, recv_sem, device):
        return pltpu.make_async_remote_copy(
            src_ref=src,
            dst_ref=dst,
            send_sem=send_sem,
            recv_sem=recv_sem,
            device_id=device,
            device_id_type=MESH,
        )

    def several(ref, count, send_sem, recv_sem):
        part = ref.at[pl.ds(0, count)]
        return remote(part, part, send_sem, recv_sem, ring(lax.rem(z + 1, TR)))

    ends = []

    loads = [
        pltpu.make_async_copy(psi_hbm.at[0], psi_in, in_sem.at[0]),
        pltpu.make_async_copy(pc_hbm.at[0], pc_in, in_sem.at[1]),
        pltpu.make_async_copy(mix_hbm, mix, in_sem.at[2]),
        pltpu.make_async_copy(sizes_hbm, sizes, in_sem.at[3]),
    ]
    env_loads = [
        pltpu.make_async_copy(right_hbm.at[:, 0], own_env.at[0], in_sem.at[4]),
        pltpu.make_async_copy(left_hbm.at[:, 0], own_env.at[1], in_sem.at[5]),
    ]
    for load in loads:
        load.start()
    gap = lax.rem(z - k + TR + 1, TR)

    @pl.when(gap < 3)
    def _():
        for load in env_loads:
            load.start()

    barrier = pltpu.get_barrier_semaphore()

    def greet_tr(i, carry):
        pl.semaphore_signal(barrier, inc=1, device_id=ring(lax.rem(z + i, TR)), device_id_type=MESH)
        return carry

    def greet_sec(i, carry):
        pl.semaphore_signal(
            barrier, inc=1, device_id={"sec": lax.rem(sec + i, SEC)}, device_id_type=MESH
        )
        return carry

    partner = sec + 1 - 2 * core
    pl.semaphore_signal(
        barrier,
        inc=1,
        device_id={"tr": lax.rem(z + 2 * core - 1 + TR, TR), "sec": partner},
        device_id_type=MESH,
    )
    def greet_far(j, carry):
        @pl.when((k != z) | (j != k))
        def _():
            pl.semaphore_signal(
                barrier,
                inc=1,
                device_id={"tr": k, "sec": 2 * j + core},
                device_id_type=MESH,
            )

        return carry

    lax.fori_loop(1, SEC, greet_sec, 0)
    lax.fori_loop(1, TR, greet_tr, 0)
    lax.fori_loop(0, TR, greet_far, 0)

    line = iota((LINES, LINES), 0)
    other = iota((LINES, LINES), 1)

    def to_phys_major(value):
        matrix = ((line // ROWS) == lax.rem(other, PHYS)) & (
            lax.rem(line, ROWS) == (other // PHYS)
        )
        return dot(matrix.astype(BF16), value)

    def to_row_major(value):
        matrix = ((other // ROWS) == lax.rem(line, PHYS)) & (
            lax.rem(other, ROWS) == (line // PHYS)
        )
        return dot(matrix.astype(BF16), value)

    loads[3].wait()
    used_left = sizes[0, 0]
    used_right = sizes[0, 1]
    keep = ((z * ROWS + iota((LINES, WIDTH), 0) // PHYS) < used_right) & (
        iota((LINES, WIDTH), 1) < used_left
    )
    loads[0].wait()
    start = jnp.where(keep, psi_in[...].astype(F32).reshape(LINES, WIDTH), 0.0).astype(BF16)
    start_rows[...] = start
    store_columns(cols_send, to_phys_major(start).astype(BF16))
    loads[1].wait()
    pc_send[...] = pc_in[...].astype(F32).reshape(TR, 2 * PHYS, WIDTH).astype(BF16)

    pl.semaphore_wait(barrier, TR + SEC - 1 + TR - jnp.where(k == z, 1, 0))

    def move_in_plane(n, source, middle):
        def send(i, carry):
            peer = plane_peer(i)
            remote(
                source.at[peer],
                middle.at[k],
                move_send_sem.at[n, 0],
                move_one_sem.at[n, k],
                plane(peer),
            ).start()
            return carry

        lax.fori_loop(1, TR, send, 0)
        middle[k] = source[k]
        ends.append(several(middle, TR - 1, move_send_sem.at[n, 0], move_two_sem.at[n]))

    def arrived(n, middle, index):
        return remote(
            middle.at[index],
            middle.at[index],
            move_send_sem.at[n, 0],
            move_one_sem.at[n, index],
            ring(lax.rem(z + 1, TR)),
        )

    def move_in_ring(n, middle, target):
        def send(i, carry):
            peer = ring_peer(i)

            @pl.when(peer != k)
            def _():
                arrived(n, middle, peer).wait_recv()

            remote(
                middle.at[peer], target.at[z], move_send_sem.at[n, 1], move_two_sem.at[n], ring(peer)
            ).start()
            return carry

        lax.fori_loop(0, TR - 1, send, 0)

        @pl.when(z != k)
        def _():
            arrived(n, middle, z).wait_recv()

        target[z] = middle[z]
        done = several(target, TR - 1, move_send_sem.at[n, 1], move_two_sem.at[n])
        ends.append(done)
        return done

    def back(n, source, target, begin, end):
        def send(i, carry):
            peer = ring_peer(i)
            remote(
                source.at[peer],
                target.at[k],
                move_send_sem.at[n, 0],
                move_two_sem.at[n],
                {"tr": peer, "sec": 2 * z + core},
            ).start()
            return carry

        lax.fori_loop(begin, end, send, 0)

    def back_home(n, source, target):
        @pl.when(z != k)
        def _():
            remote(
                source.at[z],
                target.at[k],
                move_send_sem.at[n, 0],
                move_two_sem.at[n],
                {"tr": z, "sec": 2 * z + core},
            ).start()

        @pl.when(z == k)
        def _():
            target[k] = source[k]

    def back_wait(n, target, sent):
        for same in range(2):

            @pl.when((z == k) if same else (z != k))
            def _():
                done = several(target, TR - same, move_send_sem.at[n, 0], move_two_sem.at[n])
                if sent:
                    done.wait_send()
                else:
                    done.wait_recv()

    def piece(m, i, rows=ROWS, first=0):
        return env.at[m, :, pl.ds(pl.multiple_of(i * ROWS + first, 16), rows), :]

    def scatter(m):
        used = used_right if m == 0 else used_left
        for d in range(3):

            @pl.when(gap == d)
            def _():
                env_loads[m].wait()
                for i in range(d, TR, 3):
                    span = pl.ds(i * ROWS, ROWS)
                    rows = own_env[m, :, span, :]
                    own_env[m, :, span, :] = jnp.where(i * ROWS < used, rows, jnp.zeros_like(rows))

                    @pl.when(k != i)
                    def _():
                        remote(
                            own_env.at[m, :, span, :],
                            land_env.at[m],
                            scatter_send_sem.at[m, i],
                            scatter_recv_sem.at[m],
                            plane(i),
                        ).start()

                    @pl.when(k == i)
                    def _():
                        land_env[m] = own_env[m, :, span, :]

    def scatter_end(m):
        for d in range(3):

            @pl.when(gap == d)
            def _():
                for i in range(d, TR, 3):

                    @pl.when(k != i)
                    def _():
                        remote(
                            own_env.at[m, :, pl.ds(i * ROWS, ROWS), :],
                            land_env.at[m],
                            scatter_send_sem.at[m, i],
                            scatter_recv_sem.at[m],
                            plane(i),
                        ).wait_send()

    shift = lax.rem(k, 3) - 1
    home = lax.rem(z - shift + TR, TR)

    def hand_over(m):
        return remote(
            land_env.at[m], piece(m, k), own_send_sem.at[m], own_recv_sem.at[m], ring(home)
        )

    def keep_here(m):
        return pltpu.make_async_copy(land_env.at[m], piece(m, k), own_recv_sem.at[m])

    def own_start(m):
        @pl.when(home != k)
        def _():
            remote(
                land_env.at[m],
                land_env.at[m],
                own_send_sem.at[m],
                scatter_recv_sem.at[m],
                ring(lax.rem(z + 1, TR)),
            ).wait_recv()

        @pl.when(shift != 0)
        def _():
            hand_over(m).start()

        @pl.when(shift == 0)
        def _():
            keep_here(m).start()

    def own_wait(m):
        @pl.when(shift != 0)
        def _():
            hand_over(m).wait_recv()

        @pl.when(shift == 0)
        def _():
            keep_here(m).wait()

    def row_peer(step):
        return 4 * y + lax.rem(x + step, 4)

    def column_peer(step):
        return 4 * lax.rem(y + step, 4) + x

    def gather_copy(m, ref, i, side, target):
        return remote(ref, ref, gather_send_sem.at[m], gather_recv_sem.at[m, i, side], plane(target))

    def gather_direct(m):
        for step in STEPS:
            gather_copy(m, piece(m, k), k, 0, row_peer(step)).start()
            gather_copy(m, piece(m, k), k, 0, column_peer(step)).start()

    def gather_forward(m):
        for step in STEPS:
            source = row_peer(4 - step)
            gather_copy(m, piece(m, source), source, 0, source).wait_recv()
            for turn in STEPS:
                gather_copy(m, piece(m, source, 16, 0), source, 0, column_peer(turn)).start()
            source = column_peer(4 - step)
            gather_copy(m, piece(m, source), source, 0, source).wait_recv()
            for turn in STEPS:
                gather_copy(m, piece(m, source, 16, 16), source, 1, row_peer(turn)).start()

    def gather_wait(m):
        for dy in STEPS:
            for dx in STEPS:
                source = 4 * lax.rem(y + dy, 4) + lax.rem(x + dx, 4)
                gather_copy(m, piece(m, source, 16, 0), source, 0, source).wait_recv()
                gather_copy(m, piece(m, source, 16, 16), source, 1, source).wait_recv()

    def gather_end(m):
        sent = env.at[m, :, pl.ds(0, WIDTH - ROWS), :]
        remote(
            sent, sent, gather_send_sem.at[m], own_recv_sem.at[m], ring(lax.rem(z + 1, TR))
        ).wait_send()

    def turn(n, source, target):
        def send(i, carry):
            peer = plane_peer(i)
            remote(
                source.at[:, peer],
                target.at[:, k],
                turn_send_sem.at[n],
                turn_recv_sem.at[n],
                plane(peer),
            ).start()
            return carry

        lax.fori_loop(1, TR, send, 0)
        for place in range(2):
            target[place, k] = source[place, k]
        part = target.at[:, pl.ds(0, TR - 1)]
        done = remote(
            part, part, turn_send_sem.at[n], turn_recv_sem.at[n], ring(lax.rem(z + 1, TR))
        )
        ends.append(done)
        return done

    sector = 2 * z + core

    def shifts(n, source, target):
        copies = []
        for way in range(2):
            copy = remote(
                source,
                target.at[way],
                near_send_sem.at[n, way],
                near_recv_sem.at[n, way],
                {"tr": lax.rem(z + core - way + TR, TR), "sec": partner},
            )
            copy.start()
            copies.append(copy)
        ends.extend(copies)
        return copies

    def inside(way, value):
        exists = sector > 0 if way == 0 else sector < SEC - 1
        return jnp.where(exists, value, jnp.zeros_like(value))

    move_in_plane(0, cols_send, cols_mid)
    scatter(0)
    scatter(1)
    own_start(0)
    cols_done = move_in_ring(0, cols_mid, cols)
    own_start(1)
    own_wait(0)
    gather_direct(0)
    move_in_plane(1, pc_send, pc_mid)

    wide_line = iota((WIDTH, WIDTH), 0)
    wide_other = iota((WIDTH, WIDTH), 1)

    def old_row(r):
        return lax.rem(r, 32) // 2 * 32 + r // 32 * 2 + lax.rem(r, 2)

    to_new[...] = (old_row(wide_line) == wide_other).astype(BF16)
    gather_forward(0)
    own_wait(1)
    gather_direct(1)
    to_old[...] = (old_row(wide_other) == wide_line).astype(BF16)
    loads[2].wait()
    spread = ((iota((LINES, PHYS), 0) // ROWS) == iota((LINES, PHYS), 1)).astype(BF16)
    same_row = lax.rem(line, ROWS) == lax.rem(other, ROWS)
    for c in range(3):
        mixed = dot_nt(dot(spread, mix[c]).astype(BF16), spread)
        kron[c] = jnp.where(same_row, mixed, 0.0).astype(BF16)

    cols_done.wait_recv()
    copies = shifts(0, cols, near_cols)
    own_cols = cols[...].reshape(WIDTH, HALF)
    gather_wait(0)
    turns = []

    def reordered(value):
        return dot(to_new[...], value).astype(BF16).reshape(TR, ROWS, HALF)

    def right_part(c, value):
        return reordered(dot(env[0, c], value).astype(BF16))

    turn_send[0, 0] = right_part(0, own_cols)
    turn_send[0, 1] = reordered(own_cols)
    turns.append(turn(0, turn_send.at[0], turn_recv.at[0]))
    gather_forward(1)
    for way in range(2):
        copies[way].wait_recv()
        turn_send[1, way] = right_part(
            way + 1, inside(way, near_cols[way].reshape(WIDTH, HALF))
        )
    turns.append(turn(1, turn_send.at[1], turn_recv.at[1]))
    pc_done = move_in_ring(1, pc_mid, pc_new)
    gather_wait(1)
    total = None
    for c, (group, place) in enumerate(((0, 0), (1, 0), (1, 1))):
        if place == 0:
            turns[group].wait_recv()
        mixed = dot(kron[c], phys_major(turn_recv[group, place])).astype(BF16)
        term = dot_nt(mixed, env[1, c])
        total = term if total is None else total + term
    rounded = total.astype(BF16)
    first_send[...] = to_row_major(rounded).astype(BF16).reshape(TR, 2 * PHYS, WIDTH)
    image0 = rounded.astype(F32)
    s = phys_major(turn_recv[0, 1]).astype(F32)
    pc_done.wait_recv()
    factors = to_phys_major(pc_new[...].reshape(LINES, WIDTH))

    def tr_start(h, block):
        red_send[h, 0] = block

        def send(i, carry):
            remote(
                red_send.at[h, 0],
                red_tr.at[h, z],
                red_send_sem.at[h, 0],
                red_recv_sem.at[h, 0],
                ring(ring_peer(i)),
            ).start()
            return carry

        lax.fori_loop(0, TR - 1, send, 0)
        red_tr[h, z] = block
        done = several(red_tr.at[h], TR - 1, red_send_sem.at[h, 0], red_recv_sem.at[h, 0])
        ends.append(done)
        return done

    def sec_start(h, block):
        red_send[h, 1] = block

        def send(i, carry):
            remote(
                red_send.at[h, 1],
                red_sec.at[h, sec],
                red_send_sem.at[h, 1],
                red_recv_sem.at[h, 1],
                {"sec": lax.rem(sec + i, SEC)},
            ).start()
            return carry

        lax.fori_loop(1, SEC, send, 0)
        red_sec[h, sec] = block
        done = several(red_sec.at[h], SEC - 1, red_send_sem.at[h, 1], red_recv_sem.at[h, 1])
        ends.append(done)
        return done

    def means(block):
        whole = jnp.sum(block, axis=1, keepdims=True)
        return [whole[n : n + 1] / COUNT for n in range(4)]

    weighted = s * factors
    parts = (s * s, s * image0, weighted * image0, weighted * s)
    block = jnp.concatenate([partial_sum(part) for part in parts] * 2, axis=0)
    tr_start(0, block).wait_recv()
    sums_done = sec_start(0, jnp.sum(red_tr[0], axis=0))
    back(2, first_send, first_old, 0, 5)
    sums_done.wait_recv()
    ss, sw, spw, sps = means(jnp.sum(red_sec[0], axis=0))
    norm = lax.rsqrt(ss + EPSILON)
    theta = norm * norm * sw
    along = norm * norm * (spw - theta * sps)

    def trial_of(image, vector, weights):
        return (image - theta * vector) * weights - along * vector

    trial = trial_of(image0, s, factors)
    trial_bf = trial.astype(BF16)
    vec[...] = trial_bf

    copies = shifts(1, vec, near_vec)
    turns = []

    def left_part(c, value):
        mixed = dot(kron[c], value).astype(BF16)
        return dot_nt(mixed, env[1, c]).astype(BF16)

    store_columns(half_send.at[0, 0], left_part(0, trial_bf))
    store_columns(half_send.at[0, 1], trial_bf)
    turns.append(turn(2, half_send.at[0], half_recv.at[0]))
    for way in range(2):
        copies[way].wait_recv()
        store_columns(half_send.at[1, way], left_part(way + 1, inside(way, near_vec[way])))
    turns.append(turn(3, half_send.at[1], half_recv.at[1]))
    back(2, first_send, first_old, 5, TR - 1)
    back_home(2, first_send, first_old)
    second = trial_bf.astype(F32)
    tt = partial_sum(trial * trial)
    t0 = partial_sum(second * image0)
    total = None
    for c, (group, place) in enumerate(((0, 0), (1, 0), (1, 1))):
        if place == 0:
            turns[group].wait_recv()
        half = dot(to_old[...], half_recv[group, place].reshape(WIDTH, HALF)).astype(BF16)
        term = dot(env[0, c], half)
        total = term if total is None else total + term
    second_send[...] = total.astype(BF16).reshape(TR, ROWS, HALF)
    back(3, second_send, second_old, 0, TR - 1)
    back_home(3, second_send, second_old)
    image1_cols = total.astype(BF16).astype(F32)
    trial_cols = dot(to_old[...], half_recv[0, 1].reshape(WIDTH, HALF))
    s1 = partial_sum(cols[...].reshape(WIDTH, HALF).astype(F32) * image1_cols)
    t1 = partial_sum(trial_cols * image1_cols)
    block = jnp.concatenate([tt, s1, t0, t1] * 2, axis=0)
    sec_start(1, block).wait_recv()
    sums_done = tr_start(1, jnp.sum(red_sec[1], axis=0))
    sums_done.wait_recv()
    tt, s1, t0, t1 = means(jnp.sum(red_tr[1], axis=0))

    fresh = norm * norm * tt
    grow = norm * lax.rsqrt(fresh + EPSILON)
    cross = 0.5 * norm * grow * (s1 + t0)
    corner = grow * grow * t1
    halfgap = 0.5 * (theta - corner)
    energy = 0.5 * (theta + corner) - jnp.sqrt(halfgap * halfgap + cross * cross)
    weight_one = corner - energy
    weight_two = -cross
    scale = lax.rsqrt(weight_one * weight_one + weight_two * weight_two)
    one = weight_one * scale * norm
    two = weight_two * scale * grow
    energy_out[...] = energy

    back_wait(2, first_old, False)
    old_image = first_old[...].reshape(LINES, WIDTH).astype(F32)
    old_start = start_rows[...].astype(F32)
    old_factors = pc_send[...].reshape(LINES, WIDTH).astype(F32)
    old_trial = trial_of(old_image, old_start, old_factors).astype(BF16).astype(F32)
    ritz = one * old_start + two * old_trial
    psi_out[...] = ritz.reshape(ROWS, PHYS, WIDTH).astype(BF16)[None]
    partial = one * old_image - energy * ritz
    back_wait(3, second_old, False)
    residual = partial + two * to_row_major(phys_major(second_old[...]))
    res_out[...] = residual.reshape(ROWS, PHYS, WIDTH).astype(BF16)[None]

    for m in range(2):
        scatter_end(m)
        gather_end(m)

        @pl.when(shift != 0)
        def _():
            hand_over(m).wait_send()

    back_wait(2, first_old, True)
    back_wait(3, second_old, True)
    for end in ends:
        end.wait_send()


def body(psi, precond, env_left, env_right, mixers, sizes):
    anywhere = pl.BlockSpec(memory_space=pl.ANY)
    vmem = pl.BlockSpec(memory_space=pltpu.VMEM)
    dma = pltpu.SemaphoreType.DMA
    columns = (TR, ROWS, HALF)
    pairs = (2, 2, TR, ROWS, HALF)
    rows = (TR, 2 * PHYS, WIDTH)
    psi_new, residual_new, energy = pl.pallas_call(
        kernel,
        out_shape=(
            jax.ShapeDtypeStruct(psi.shape, BF16),
            jax.ShapeDtypeStruct(psi.shape, BF16),
            jax.ShapeDtypeStruct((1, 1), F32),
        ),
        in_specs=[anywhere] * 6,
        out_specs=(vmem, vmem, vmem),
        scratch_shapes=[
            pltpu.VMEM((ROWS, PHYS, WIDTH), BF16),
            pltpu.VMEM((ROWS, PHYS, WIDTH), BF16),
            pltpu.VMEM((3, PHYS, PHYS), BF16),
            pltpu.SMEM((1, 2), jnp.int32),
            pltpu.VMEM((2, 3, WIDTH, WIDTH), BF16),
            pltpu.VMEM((2, 3, ROWS, WIDTH), BF16),
            pltpu.VMEM((2, 3, WIDTH, WIDTH), BF16),
            pltpu.VMEM((3, LINES, LINES), BF16),
            pltpu.VMEM((WIDTH, WIDTH), BF16),
            pltpu.VMEM((WIDTH, WIDTH), BF16),
            pltpu.VMEM((LINES, WIDTH), BF16),
            pltpu.VMEM(columns, BF16),
            pltpu.VMEM(columns, BF16),
            pltpu.VMEM(columns, BF16),
            pltpu.VMEM((2, *columns), BF16),
            pltpu.VMEM(pairs, BF16),
            pltpu.VMEM(pairs, BF16),
            pltpu.VMEM(rows, BF16),
            pltpu.VMEM(rows, BF16),
            pltpu.VMEM(rows, BF16),
            pltpu.VMEM((LINES, WIDTH), BF16),
            pltpu.VMEM((2, LINES, WIDTH), BF16),
            pltpu.VMEM(pairs, BF16),
            pltpu.VMEM(pairs, BF16),
            pltpu.VMEM(rows, BF16),
            pltpu.VMEM(rows, BF16),
            pltpu.VMEM(columns, BF16),
            pltpu.VMEM(columns, BF16),
            pltpu.VMEM((2, 2, 8, 128), F32),
            pltpu.VMEM((2, TR, 8, 128), F32),
            pltpu.VMEM((2, SEC, 8, 128), F32),
            dma((6,)),
            dma((2, TR)),
            dma((2,)),
            dma((2,)),
            dma((2,)),
            dma((2,)),
            dma((2, TR, 2)),
            dma((2, 2)),
            dma((2, 2)),
            dma((4,)),
            dma((4,)),
            dma((4, 2)),
            dma((4, TR)),
            dma((4,)),
            dma((2, 2)),
            dma((2, 2)),
        ],
        compiler_params=pltpu.CompilerParams(
            collective_id=0, has_side_effects=True, vmem_limit_bytes=60 * 1024 * 1024
        ),
        cost_estimate=pl.CostEstimate(
            flops=2_200_000_000, bytes_accessed=2_000_000, transcendentals=0
        ),
    )(psi, precond, env_left, env_right, mixers, sizes)
    return psi_new, residual_new, energy.reshape(())


def solution(mesh):
    placed = (
        P("sec", "tr", None, None),
        P("sec", "tr", None, None),
        P(None, "sec", None, None),
        P(None, "sec", None, None),
        P(),
        P("sec", None),
    )
    return jax.shard_map(
        body,
        mesh=mesh,
        in_specs=placed,
        out_specs=(P("sec", "tr", None, None), P("sec", "tr", None, None), P()),
        check_vma=False,
    )
```

```python
import jax
import jax.numpy as jnp
from jax import lax
from jax.experimental import pallas as pl
from jax.experimental.pallas import tpu as pltpu
from jax.sharding import PartitionSpec as P

EPSILON = 1e-06
MESH = pl.DeviceIdType.MESH
F32 = jnp.float32
BF16 = jnp.bfloat16
TR = 16
SEC = 32
ROWS = 32
PHYS = 8
WIDTH = 512
HALF = 256
LINES = ROWS * PHYS
COUNT = float(SEC * WIDTH * PHYS * WIDTH)
STEPS = (1, 3, 2)


def dot(a, b):
    return jnp.dot(a, b, preferred_element_type=F32)


def dot_nt(a, b):
    return lax.dot_general(a, b, (((1,), (1,)), ((), ())), preferred_element_type=F32)


def iota(shape, axis):
    return lax.broadcasted_iota(jnp.int32, shape, axis)


def partial_sum(x):
    rows = jnp.sum(x, axis=0, keepdims=True)
    total = rows[:, 0:128]
    for lane in range(128, x.shape[1], 128):
        total = total + rows[:, lane : lane + 128]
    return total


def phys_major(block):
    pieces = [jnp.concatenate([block[2 * p], block[2 * p + 1]], axis=1) for p in range(PHYS)]
    return jnp.concatenate(pieces, axis=0)


def store_columns(ref, value):
    for j in range(TR):
        p, side = divmod(j, 2)
        ref[j] = value[p * ROWS : (p + 1) * ROWS, side * HALF : (side + 1) * HALF]


def kernel(
    psi_hbm,
    pc_hbm,
    left_hbm,
    right_hbm,
    mix_hbm,
    sizes_hbm,
    psi_out,
    res_out,
    energy_out,
    psi_in,
    pc_in,
    mix,
    sizes,
    own_env,
    land_env,
    env,
    kron,
    to_new,
    to_old,
    start_rows,
    cols_send,
    cols_mid,
    cols,
    near_cols,
    turn_send,
    turn_recv,
    pc_send,
    pc_mid,
    pc_new,
    vec,
    near_vec,
    half_send,
    half_recv,
    first_send,
    first_old,
    second_send,
    second_old,
    red_send,
    red_tr,
    red_sec,
    in_sem,
    scatter_send_sem,
    scatter_recv_sem,
    own_send_sem,
    own_recv_sem,
    gather_send_sem,
    gather_recv_sem,
    near_send_sem,
    near_recv_sem,
    turn_send_sem,
    turn_recv_sem,
    move_send_sem,
    move_one_sem,
    move_two_sem,
    red_send_sem,
    red_recv_sem,
):
    z = lax.axis_index("tr")
    sec = lax.axis_index("sec")
    k = sec // 2
    core = lax.rem(sec, 2)
    y = k // 4
    x = lax.rem(k, 4)

    def ring(z2):
        return {"tr": z2}

    def plane(k2):
        return {"sec": 2 * k2 + core}

    def turned(m):
        return jnp.where(m >= TR - 1, m - (TR - 1), m)

    def ring_peer(i):
        m = turned(i + k)
        step = m // 2 + 1
        return lax.rem(z + jnp.where(lax.rem(m, 2) == 0, step, TR - step), TR)

    def ring_source(i):
        m = turned(i + k)
        step = m // 2 + 1
        return lax.rem(z + jnp.where(lax.rem(m, 2) == 0, TR - step, step), TR)

    def plane_peer(i):
        return 4 * lax.rem(y + i // 4, 4) + lax.rem(x + lax.rem(i, 4), 4)

    def remote(src, dst, send_sem, recv_sem, device):
        return pltpu.make_async_remote_copy(
            src_ref=src,
            dst_ref=dst,
            send_sem=send_sem,
            recv_sem=recv_sem,
            device_id=device,
            device_id_type=MESH,
        )

    def several(ref, count, send_sem, recv_sem):
        part = ref.at[pl.ds(0, count)]
        return remote(part, part, send_sem, recv_sem, ring(lax.rem(z + 1, TR)))

    ends = []

    loads = [
        pltpu.make_async_copy(psi_hbm.at[0], psi_in, in_sem.at[0]),
        pltpu.make_async_copy(pc_hbm.at[0], pc_in, in_sem.at[1]),
        pltpu.make_async_copy(mix_hbm, mix, in_sem.at[2]),
        pltpu.make_async_copy(sizes_hbm, sizes, in_sem.at[3]),
    ]
    env_loads = [
        pltpu.make_async_copy(right_hbm.at[:, 0], own_env.at[0], in_sem.at[4]),
        pltpu.make_async_copy(left_hbm.at[:, 0], own_env.at[1], in_sem.at[5]),
    ]
    for load in loads:
        load.start()
    gap = lax.rem(z - k + TR + 1, TR)

    @pl.when(gap < 4)
    def _():
        for load in env_loads:
            load.start()

    barrier = pltpu.get_barrier_semaphore()

    def greet_tr(i, carry):
        pl.semaphore_signal(barrier, inc=1, device_id=ring(lax.rem(z + i, TR)), device_id_type=MESH)
        return carry

    def greet_sec(i, carry):
        pl.semaphore_signal(
            barrier, inc=1, device_id={"sec": lax.rem(sec + i, SEC)}, device_id_type=MESH
        )
        return carry

    partner = sec + 1 - 2 * core
    pl.semaphore_signal(
        barrier,
        inc=1,
        device_id={"tr": lax.rem(z + 2 * core - 1 + TR, TR), "sec": partner},
        device_id_type=MESH,
    )
    def greet_far(j, carry):
        @pl.when((k != z) | (j != k))
        def _():
            pl.semaphore_signal(
                barrier,
                inc=1,
                device_id={"tr": k, "sec": 2 * j + core},
                device_id_type=MESH,
            )

        return carry

    lax.fori_loop(1, SEC, greet_sec, 0)
    lax.fori_loop(1, TR, greet_tr, 0)
    lax.fori_loop(0, TR, greet_far, 0)

    line = iota((LINES, LINES), 0)
    other = iota((LINES, LINES), 1)

    def to_phys_major(value):
        matrix = ((line // ROWS) == lax.rem(other, PHYS)) & (
            lax.rem(line, ROWS) == (other // PHYS)
        )
        return dot(matrix.astype(BF16), value)

    def to_row_major(value):
        matrix = ((other // ROWS) == lax.rem(line, PHYS)) & (
            lax.rem(other, ROWS) == (line // PHYS)
        )
        return dot(matrix.astype(BF16), value)

    loads[3].wait()
    used_left = sizes[0, 0]
    used_right = sizes[0, 1]
    keep = ((z * ROWS + iota((LINES, WIDTH), 0) // PHYS) < used_right) & (
        iota((LINES, WIDTH), 1) < used_left
    )
    loads[0].wait()
    start = jnp.where(keep, psi_in[...].astype(F32).reshape(LINES, WIDTH), 0.0).astype(BF16)
    start_rows[...] = start
    store_columns(cols_send, to_phys_major(start).astype(BF16))
    loads[1].wait()
    pc_send[...] = pc_in[...].astype(F32).reshape(TR, 2 * PHYS, WIDTH).astype(BF16)

    pl.semaphore_wait(barrier, TR + SEC - 1 + TR - jnp.where(k == z, 1, 0))

    def move_in_plane(n, source, middle):
        def send(i, carry):
            peer = plane_peer(i)
            remote(
                source.at[peer],
                middle.at[k],
                move_send_sem.at[n, 0],
                move_one_sem.at[n, k],
                plane(peer),
            ).start()
            return carry

        lax.fori_loop(1, TR, send, 0)
        middle[k] = source[k]
        ends.append(several(middle, TR - 1, move_send_sem.at[n, 0], move_two_sem.at[n]))

    def arrived(n, middle, index):
        return remote(
            middle.at[index],
            middle.at[index],
            move_send_sem.at[n, 0],
            move_one_sem.at[n, index],
            ring(lax.rem(z + 1, TR)),
        )

    def move_in_ring(n, middle, target):
        def send(i, carry):
            peer = ring_peer(i)

            @pl.when(peer != k)
            def _():
                arrived(n, middle, peer).wait_recv()

            remote(
                middle.at[peer], target.at[z], move_send_sem.at[n, 1], move_two_sem.at[n], ring(peer)
            ).start()
            return carry

        lax.fori_loop(0, TR - 1, send, 0)

        @pl.when(z != k)
        def _():
            arrived(n, middle, z).wait_recv()

        target[z] = middle[z]
        done = several(target, TR - 1, move_send_sem.at[n, 1], move_two_sem.at[n])
        ends.append(done)
        return done

    def back(n, source, target, begin, end):
        def send(i, carry):
            peer = ring_peer(i)
            remote(
                source.at[peer],
                target.at[k],
                move_send_sem.at[n, 0],
                move_two_sem.at[n],
                {"tr": peer, "sec": 2 * z + core},
            ).start()
            return carry

        lax.fori_loop(begin, end, send, 0)

    def back_home(n, source, target):
        @pl.when(z != k)
        def _():
            remote(
                source.at[z],
                target.at[k],
                move_send_sem.at[n, 0],
                move_two_sem.at[n],
                {"tr": z, "sec": 2 * z + core},
            ).start()

        @pl.when(z == k)
        def _():
            target[k] = source[k]

    def back_wait(n, target, sent):
        for same in range(2):

            @pl.when((z == k) if same else (z != k))
            def _():
                done = several(target, TR - same, move_send_sem.at[n, 0], move_two_sem.at[n])
                if sent:
                    done.wait_send()
                else:
                    done.wait_recv()

    def env_matrix(m, c):
        return env[m, c].reshape(WIDTH, WIDTH)

    def piece(m, dy, dx, part=(pl.ds(0, ROWS), pl.ds(0, WIDTH))):
        return env.at[m, :, lax.rem(y + dy + 4, 4), lax.rem(x + dx + 4, 4), part[0], part[1]]

    def row_set(m, dy, part):
        return env.at[m, :, lax.rem(y + dy + 4, 4), :, part[0], part[1]]

    def column_set(m, dx, part):
        return env.at[m, :, :, lax.rem(x + dx + 4, 4), part[0], part[1]]

    def scatter_copy(m, d, n):
        return remote(
            own_env.at[m, :, pl.ds((4 * d + n) * ROWS, ROWS), :],
            land_env.at[m],
            scatter_send_sem.at[m, n],
            scatter_recv_sem.at[m],
            plane(4 * d + n),
        )

    def scatter(m):
        used = used_right if m == 0 else used_left
        for d in range(4):

            @pl.when(gap == d)
            def _():
                env_loads[m].wait()
                span = pl.ds(4 * d * ROWS, 4 * ROWS)
                rows = own_env[m, :, span, :]
                own_env[m, :, span, :] = jnp.where(4 * d * ROWS < used, rows, jnp.zeros_like(rows))
                for n in range(4):

                    @pl.when(k != 4 * d + n)
                    def _():
                        scatter_copy(m, d, n).start()

                    @pl.when(k == 4 * d + n)
                    def _():
                        land_env[m] = own_env[m, :, pl.ds((4 * d + n) * ROWS, ROWS), :]

    def scatter_end(m):
        for d in range(4):

            @pl.when(gap == d)
            def _():
                for n in range(4):

                    @pl.when(k != 4 * d + n)
                    def _():
                        scatter_copy(m, d, n).wait_send()

    shift = y - 1
    home = lax.rem(z - shift + TR, TR)

    def hand_over(m):
        return remote(
            land_env.at[m], piece(m, 0, 0), own_send_sem.at[m], own_recv_sem.at[m], ring(home)
        )

    def keep_here(m):
        return pltpu.make_async_copy(land_env.at[m], piece(m, 0, 0), own_recv_sem.at[m])

    def own_start(m):
        @pl.when(home != k)
        def _():
            remote(
                land_env.at[m],
                land_env.at[m],
                own_send_sem.at[m],
                scatter_recv_sem.at[m],
                ring(lax.rem(z + 1, TR)),
            ).wait_recv()

        @pl.when(shift != 0)
        def _():
            hand_over(m).start()

        @pl.when(shift == 0)
        def _():
            keep_here(m).start()

    def own_wait(m):
        @pl.when(shift != 0)
        def _():
            hand_over(m).wait_recv()

        @pl.when(shift == 0)
        def _():
            keep_here(m).wait()

    first = (pl.ds(0, 16), pl.ds(0, WIDTH))
    last = (pl.ds(16, 16), pl.ds(0, WIDTH))
    quarters = [(pl.ds(n // 2 * 16, 16), pl.ds(n % 2 * HALF, HALF)) for n in range(4)]

    def hop(m, n, ref, dy, dx):
        target = 4 * lax.rem(y + dy + 4, 4) + lax.rem(x + dx + 4, 4)
        return remote(ref, ref, gather_send_sem.at[m], gather_recv_sem.at[m, n], plane(target))

    def gather_one(m):
        own_wait(m)
        hop(m, 0, piece(m, 0, 0, first), 0, 1).start()
        hop(m, 1, piece(m, 0, 0, first), 0, -1).start()
        hop(m, 2, piece(m, 0, 0, last), 1, 0).start()
        hop(m, 3, piece(m, 0, 0, last), -1, 0).start()

    def gather_two(m):
        hop(m, 0, piece(m, 0, -1, first), 0, -1).wait_recv()
        hop(m, 4, piece(m, 0, -1, quarters[0]), 0, 1).start()
        hop(m, 1, piece(m, 0, 1, first), 0, 1).wait_recv()
        hop(m, 5, piece(m, 0, 1, quarters[1]), 0, -1).start()
        hop(m, 2, piece(m, -1, 0, last), -1, 0).wait_recv()
        hop(m, 6, piece(m, -1, 0, quarters[2]), 1, 0).start()
        hop(m, 3, piece(m, 1, 0, last), 1, 0).wait_recv()
        hop(m, 7, piece(m, 1, 0, quarters[3]), -1, 0).start()

    def gather_three(m):
        hop(m, 4, piece(m, 0, 2, quarters[0]), 0, -1).wait_recv()
        hop(m, 5, piece(m, 0, 2, quarters[1]), 0, 1).wait_recv()
        hop(m, 8, row_set(m, 0, first), 1, 0).start()
        hop(m, 9, row_set(m, 0, first), -1, 0).start()
        hop(m, 6, piece(m, 2, 0, quarters[2]), -1, 0).wait_recv()
        hop(m, 7, piece(m, 2, 0, quarters[3]), 1, 0).wait_recv()
        hop(m, 10, column_set(m, 0, last), 0, 1).start()
        hop(m, 11, column_set(m, 0, last), 0, -1).start()

    def gather_four(m):
        hop(m, 8, row_set(m, -1, first), -1, 0).wait_recv()
        hop(m, 12, row_set(m, -1, quarters[0]), 1, 0).start()
        hop(m, 9, row_set(m, 1, first), 1, 0).wait_recv()
        hop(m, 13, row_set(m, 1, quarters[1]), -1, 0).start()
        hop(m, 10, column_set(m, -1, last), 0, -1).wait_recv()
        hop(m, 14, column_set(m, -1, quarters[2]), 0, 1).start()
        hop(m, 11, column_set(m, 1, last), 0, 1).wait_recv()
        hop(m, 15, column_set(m, 1, quarters[3]), 0, -1).start()

    def gather_wait(m):
        hop(m, 12, row_set(m, 2, quarters[0]), -1, 0).wait_recv()
        hop(m, 13, row_set(m, 2, quarters[1]), 1, 0).wait_recv()
        hop(m, 14, column_set(m, 2, quarters[2]), 0, -1).wait_recv()
        hop(m, 15, column_set(m, 2, quarters[3]), 0, 1).wait_recv()

    def gather_end(m):
        sent = own_env.at[m, :, pl.ds(0, WIDTH - ROWS), :]
        remote(
            sent, sent, gather_send_sem.at[m], own_recv_sem.at[m], ring(lax.rem(z + 1, TR))
        ).wait_send()

    def turn(n, sources, targets, begin, count):
        source = sources.at[pl.ds(begin, count)]
        target = targets.at[pl.ds(begin, count)]

        def send(i, carry):
            peer = plane_peer(i)
            remote(
                source.at[:, peer],
                target.at[:, k],
                turn_send_sem.at[n],
                turn_recv_sem.at[n],
                plane(peer),
            ).start()
            return carry

        lax.fori_loop(1, TR, send, 0)
        for place in range(begin, begin + count):
            targets[place, k] = sources[place, k]
        part = target.at[:, pl.ds(0, TR - 1)]
        done = remote(
            part, part, turn_send_sem.at[n], turn_recv_sem.at[n], ring(lax.rem(z + 1, TR))
        )
        ends.append(done)
        return done

    sector = 2 * z + core

    def shifts(n, source, target):
        copies = []
        for way in range(2):
            copy = remote(
                source,
                target.at[way],
                near_send_sem.at[n, way],
                near_recv_sem.at[n, way],
                {"tr": lax.rem(z + core - way + TR, TR), "sec": partner},
            )
            copy.start()
            copies.append(copy)
        ends.extend(copies)
        return copies

    def inside(way, value):
        exists = sector > 0 if way == 0 else sector < SEC - 1
        return jnp.where(exists, value, jnp.zeros_like(value))

    move_in_plane(0, cols_send, cols_mid)
    scatter(0)
    own_start(0)
    cols_done = move_in_ring(0, cols_mid, cols)
    scatter(1)
    gather_one(0)
    move_in_plane(1, pc_send, pc_mid)

    wide_line = iota((WIDTH, WIDTH), 0)
    wide_other = iota((WIDTH, WIDTH), 1)

    def old_row(r):
        return lax.rem(r, 32) // 2 * 32 + r // 32 * 2 + lax.rem(r, 2)

    to_new[...] = (old_row(wide_line) == wide_other).astype(BF16)
    gather_two(0)
    to_old[...] = (old_row(wide_other) == wide_line).astype(BF16)
    loads[2].wait()
    spread = ((iota((LINES, PHYS), 0) // ROWS) == iota((LINES, PHYS), 1)).astype(BF16)
    same_row = lax.rem(line, ROWS) == lax.rem(other, ROWS)
    for c in range(3):
        mixed = dot_nt(dot(spread, mix[c]).astype(BF16), spread)
        kron[c] = jnp.where(same_row, mixed, 0.0).astype(BF16)
    own_start(1)
    gather_three(0)

    def reordered(value):
        return dot(to_new[...], value).astype(BF16).reshape(TR, ROWS, HALF)

    def right_part(c, value):
        return reordered(dot(env_matrix(0, c), value).astype(BF16))

    cols_done.wait_recv()
    copies = shifts(0, cols, near_cols)
    own_cols = cols[...].reshape(WIDTH, HALF)
    turn_send[3] = reordered(own_cols)
    start_turn = turn(2, turn_send, turn_recv, 3, 1)
    gather_four(0)
    gather_one(1)
    gather_wait(0)
    turn_send[0] = right_part(0, own_cols)
    turns = [turn(0, turn_send, turn_recv, 0, 1)]
    gather_two(1)
    for way in range(2):
        copies[way].wait_recv()
        turn_send[way + 1] = right_part(
            way + 1, inside(way, near_cols[way].reshape(WIDTH, HALF))
        )
    turns.append(turn(1, turn_send, turn_recv, 1, 2))
    gather_three(1)
    pc_done = move_in_ring(1, pc_mid, pc_new)
    gather_four(1)
    gather_wait(1)
    total = None
    for c in range(3):
        if c < 2:
            turns[c].wait_recv()
        mixed = dot(kron[c], phys_major(turn_recv[c])).astype(BF16)
        term = dot_nt(mixed, env_matrix(1, c))
        total = term if total is None else total + term
    rounded = total.astype(BF16)
    first_send[...] = to_row_major(rounded).astype(BF16).reshape(TR, 2 * PHYS, WIDTH)
    image0 = rounded.astype(F32)
    start_turn.wait_recv()
    s = phys_major(turn_recv[3]).astype(F32)
    pc_done.wait_recv()
    factors = to_phys_major(pc_new[...].reshape(LINES, WIDTH))

    def tr_start(h, block):
        red_send[h, 0] = block

        def send(i, carry):
            remote(
                red_send.at[h, 0],
                red_tr.at[h, z],
                red_send_sem.at[h, 0],
                red_recv_sem.at[h, 0],
                ring(ring_peer(i)),
            ).start()
            return carry

        lax.fori_loop(0, TR - 1, send, 0)
        red_tr[h, z] = block
        done = several(red_tr.at[h], TR - 1, red_send_sem.at[h, 0], red_recv_sem.at[h, 0])
        ends.append(done)
        return done

    def sec_start(h, block):
        red_send[h, 1] = block

        def send(i, carry):
            remote(
                red_send.at[h, 1],
                red_sec.at[h, sec],
                red_send_sem.at[h, 1],
                red_recv_sem.at[h, 1],
                {"sec": lax.rem(sec + i, SEC)},
            ).start()
            return carry

        lax.fori_loop(1, SEC, send, 0)
        red_sec[h, sec] = block
        done = several(red_sec.at[h], SEC - 1, red_send_sem.at[h, 1], red_recv_sem.at[h, 1])
        ends.append(done)
        return done

    def means(block):
        whole = jnp.sum(block, axis=1, keepdims=True)
        return [whole[n : n + 1] / COUNT for n in range(4)]

    weighted = s * factors
    parts = (s * s, s * image0, weighted * image0, weighted * s)
    block = jnp.concatenate([partial_sum(part) for part in parts] * 2, axis=0)
    tr_start(0, block).wait_recv()
    sums_done = sec_start(0, jnp.sum(red_tr[0], axis=0))
    back(2, first_send, first_old, 0, 5)
    sums_done.wait_recv()
    ss, sw, spw, sps = means(jnp.sum(red_sec[0], axis=0))
    norm = lax.rsqrt(ss + EPSILON)
    theta = norm * norm * sw
    along = norm * norm * (spw - theta * sps)

    def trial_of(image, vector, weights):
        return (image - theta * vector) * weights - along * vector

    trial = trial_of(image0, s, factors)
    trial_bf = trial.astype(BF16)
    vec[...] = trial_bf

    copies = shifts(1, vec, near_vec)
    turns = []

    def left_part(c, value):
        mixed = dot(kron[c], value).astype(BF16)
        return dot_nt(mixed, env_matrix(1, c)).astype(BF16)

    store_columns(half_send.at[0], left_part(0, trial_bf))
    turns = [turn(3, half_send, half_recv, 0, 1)]
    store_columns(half_send.at[3], trial_bf)
    for way in range(2):
        copies[way].wait_recv()
        store_columns(half_send.at[way + 1], left_part(way + 1, inside(way, near_vec[way])))
    turns.append(turn(4, half_send, half_recv, 1, 2))
    trial_turn = turn(5, half_send, half_recv, 3, 1)
    back(2, first_send, first_old, 5, TR - 1)
    back_home(2, first_send, first_old)
    second = trial_bf.astype(F32)
    tt = partial_sum(trial * trial)
    t0 = partial_sum(second * image0)
    total = None
    for c in range(3):
        if c < 2:
            turns[c].wait_recv()
        half = dot(to_old[...], half_recv[c].reshape(WIDTH, HALF)).astype(BF16)
        term = dot(env_matrix(0, c), half)
        total = term if total is None else total + term
    second_send[...] = total.astype(BF16).reshape(TR, ROWS, HALF)
    back(3, second_send, second_old, 0, TR - 1)
    back_home(3, second_send, second_old)
    image1_cols = total.astype(BF16).astype(F32)
    trial_turn.wait_recv()
    trial_cols = dot(to_old[...], half_recv[3].reshape(WIDTH, HALF))
    s1 = partial_sum(cols[...].reshape(WIDTH, HALF).astype(F32) * image1_cols)
    t1 = partial_sum(trial_cols * image1_cols)
    block = jnp.concatenate([tt, s1, t0, t1] * 2, axis=0)
    sec_start(1, block).wait_recv()
    sums_done = tr_start(1, jnp.sum(red_sec[1], axis=0))
    sums_done.wait_recv()
    tt, s1, t0, t1 = means(jnp.sum(red_tr[1], axis=0))

    fresh = norm * norm * tt
    grow = norm * lax.rsqrt(fresh + EPSILON)
    cross = 0.5 * norm * grow * (s1 + t0)
    corner = grow * grow * t1
    halfgap = 0.5 * (theta - corner)
    energy = 0.5 * (theta + corner) - jnp.sqrt(halfgap * halfgap + cross * cross)
    weight_one = corner - energy
    weight_two = -cross
    scale = lax.rsqrt(weight_one * weight_one + weight_two * weight_two)
    one = weight_one * scale * norm
    two = weight_two * scale * grow
    energy_out[...] = energy

    back_wait(2, first_old, False)
    old_image = first_old[...].reshape(LINES, WIDTH).astype(F32)
    old_start = start_rows[...].astype(F32)
    old_factors = pc_send[...].reshape(LINES, WIDTH).astype(F32)
    old_trial = trial_of(old_image, old_start, old_factors).astype(BF16).astype(F32)
    ritz = one * old_start + two * old_trial
    psi_out[...] = ritz.reshape(ROWS, PHYS, WIDTH).astype(BF16)[None]
    partial = one * old_image - energy * ritz
    back_wait(3, second_old, False)
    residual = partial + two * to_row_major(phys_major(second_old[...]))
    res_out[...] = residual.reshape(ROWS, PHYS, WIDTH).astype(BF16)[None]

    for m in range(2):
        scatter_end(m)
        gather_end(m)

        @pl.when(shift != 0)
        def _():
            hand_over(m).wait_send()

    back_wait(2, first_old, True)
    back_wait(3, second_old, True)
    for end in ends:
        end.wait_send()


def body(psi, precond, env_left, env_right, mixers, sizes):
    anywhere = pl.BlockSpec(memory_space=pl.ANY)
    vmem = pl.BlockSpec(memory_space=pltpu.VMEM)
    dma = pltpu.SemaphoreType.DMA
    columns = (TR, ROWS, HALF)
    fours = (4, TR, ROWS, HALF)
    rows = (TR, 2 * PHYS, WIDTH)
    psi_new, residual_new, energy = pl.pallas_call(
        kernel,
        out_shape=(
            jax.ShapeDtypeStruct(psi.shape, BF16),
            jax.ShapeDtypeStruct(psi.shape, BF16),
            jax.ShapeDtypeStruct((1, 1), F32),
        ),
        in_specs=[anywhere] * 6,
        out_specs=(vmem, vmem, vmem),
        scratch_shapes=[
            pltpu.VMEM((ROWS, PHYS, WIDTH), BF16),
            pltpu.VMEM((ROWS, PHYS, WIDTH), BF16),
            pltpu.VMEM((3, PHYS, PHYS), BF16),
            pltpu.SMEM((1, 2), jnp.int32),
            pltpu.VMEM((2, 3, WIDTH, WIDTH), BF16),
            pltpu.VMEM((2, 3, ROWS, WIDTH), BF16),
            pltpu.VMEM((2, 3, 4, 4, ROWS, WIDTH), BF16),
            pltpu.VMEM((3, LINES, LINES), BF16),
            pltpu.VMEM((WIDTH, WIDTH), BF16),
            pltpu.VMEM((WIDTH, WIDTH), BF16),
            pltpu.VMEM((LINES, WIDTH), BF16),
            pltpu.VMEM(columns, BF16),
            pltpu.VMEM(columns, BF16),
            pltpu.VMEM(columns, BF16),
            pltpu.VMEM((2, *columns), BF16),
            pltpu.VMEM(fours, BF16),
            pltpu.VMEM(fours, BF16),
            pltpu.VMEM(rows, BF16),
            pltpu.VMEM(rows, BF16),
            pltpu.VMEM(rows, BF16),
            pltpu.VMEM((LINES, WIDTH), BF16),
            pltpu.VMEM((2, LINES, WIDTH), BF16),
            pltpu.VMEM(fours, BF16),
            pltpu.VMEM(fours, BF16),
            pltpu.VMEM(rows, BF16),
            pltpu.VMEM(rows, BF16),
            pltpu.VMEM(columns, BF16),
            pltpu.VMEM(columns, BF16),
            pltpu.VMEM((2, 2, 8, 128), F32),
            pltpu.VMEM((2, TR, 8, 128), F32),
            pltpu.VMEM((2, SEC, 8, 128), F32),
            dma((6,)),
            dma((2, 4)),
            dma((2,)),
            dma((2,)),
            dma((2,)),
            dma((2,)),
            dma((2, 16)),
            dma((2, 2)),
            dma((2, 2)),
            dma((6,)),
            dma((6,)),
            dma((4, 2)),
            dma((4, TR)),
            dma((4,)),
            dma((2, 2)),
            dma((2, 2)),
        ],
        compiler_params=pltpu.CompilerParams(
            collective_id=0, has_side_effects=True, vmem_limit_bytes=60 * 1024 * 1024
        ),
        cost_estimate=pl.CostEstimate(
            flops=2_200_000_000, bytes_accessed=2_000_000, transcendentals=0
        ),
    )(psi, precond, env_left, env_right, mixers, sizes)
    return psi_new, residual_new, energy.reshape(())


def solution(mesh):
    placed = (
        P("sec", "tr", None, None),
        P("sec", "tr", None, None),
        P(None, "sec", None, None),
        P(None, "sec", None, None),
        P(),
        P("sec", None),
    )
    return jax.shard_map(
        body,
        mesh=mesh,
        in_specs=placed,
        out_specs=(P("sec", "tr", None, None), P("sec", "tr", None, None), P()),
        check_vma=False,
    )
```

```python
import jax
import jax.numpy as jnp
from jax import lax
from jax.experimental import pallas as pl
from jax.experimental.pallas import tpu as pltpu
from jax.sharding import PartitionSpec as P

EPSILON = 1e-06
MESH = pl.DeviceIdType.MESH
F32 = jnp.float32
BF16 = jnp.bfloat16
TR = 16
SEC = 32
ROWS = 32
PHYS = 8
WIDTH = 512
HALF = 256
LINES = ROWS * PHYS
COUNT = float(SEC * WIDTH * PHYS * WIDTH)
STEPS = (1, 3, 2)


def dot(a, b):
    return jnp.dot(a, b, preferred_element_type=F32)


def dot_nt(a, b):
    return lax.dot_general(a, b, (((1,), (1,)), ((), ())), preferred_element_type=F32)


def iota(shape, axis):
    return lax.broadcasted_iota(jnp.int32, shape, axis)


def wrap(value, size):
    return jnp.where(value >= size, value - size, value)


def over(value, bits):
    return lax.shift_right_logical(value, jnp.full_like(value, bits))


def under(value, bits):
    return value - lax.shift_left(over(value, bits), jnp.full_like(value, bits))


def partial_sum(x):
    rows = jnp.sum(x, axis=0, keepdims=True)
    total = rows[:, 0:128]
    for lane in range(128, x.shape[1], 128):
        total = total + rows[:, lane : lane + 128]
    return total


def phys_major(block):
    pieces = [jnp.concatenate([block[2 * p], block[2 * p + 1]], axis=1) for p in range(PHYS)]
    return jnp.concatenate(pieces, axis=0)


def store_columns(ref, value):
    for j in range(TR):
        p, side = divmod(j, 2)
        ref[j] = value[p * ROWS : (p + 1) * ROWS, side * HALF : (side + 1) * HALF]


def kernel(
    psi_hbm,
    pc_hbm,
    left_hbm,
    right_hbm,
    mix_hbm,
    sizes_hbm,
    psi_out,
    res_out,
    energy_out,
    psi_in,
    pc_in,
    mix,
    sizes,
    own_env,
    land_env,
    env,
    kron,
    swap,
    to_new,
    to_old,
    start_rows,
    cols_send,
    cols_mid,
    cols,
    near_cols,
    turn_send,
    turn_recv,
    pc_send,
    pc_mid,
    pc_new,
    vec,
    near_vec,
    half_send,
    half_recv,
    first_send,
    first_old,
    second_send,
    second_old,
    red_send,
    red_tr,
    red_sec,
    in_sem,
    scatter_send_sem,
    scatter_recv_sem,
    own_send_sem,
    own_recv_sem,
    gather_send_sem,
    gather_recv_sem,
    near_send_sem,
    near_recv_sem,
    turn_send_sem,
    turn_recv_sem,
    move_send_sem,
    move_one_sem,
    move_two_sem,
    red_send_sem,
    red_recv_sem,
):
    z = lax.axis_index("tr")
    sec = lax.axis_index("sec")
    k = over(sec, 1)
    core = sec - 2 * k
    y = over(k, 2)
    x = k - 4 * y
    next_z = wrap(z + 1, TR)
    rows_at = [y] + [wrap(y + d, 4) for d in range(1, 4)]
    columns_at = [x] + [wrap(x + d, 4) for d in range(1, 4)]

    def ring(z2):
        return {"tr": z2}

    def plane(k2):
        return {"sec": 2 * k2 + core}

    def turned(m):
        return jnp.where(m >= TR - 1, m - (TR - 1), m)

    def ring_peer(i):
        m = turned(i + k)
        half = over(m, 1)
        step = half + 1
        return wrap(z + jnp.where(m == 2 * half, step, TR - step), TR)

    def plane_peer(i):
        down = over(i, 2)
        return 4 * wrap(y + down, 4) + wrap(x + i - 4 * down, 4)

    def remote(src, dst, send_sem, recv_sem, device):
        return pltpu.make_async_remote_copy(
            src_ref=src,
            dst_ref=dst,
            send_sem=send_sem,
            recv_sem=recv_sem,
            device_id=device,
            device_id_type=MESH,
        )

    def several(ref, count, send_sem, recv_sem):
        part = ref.at[pl.ds(0, count)]
        return remote(part, part, send_sem, recv_sem, ring(next_z))

    ends = []

    loads = [
        pltpu.make_async_copy(psi_hbm.at[0], psi_in, in_sem.at[0]),
        pltpu.make_async_copy(pc_hbm.at[0], pc_in, in_sem.at[1]),
        pltpu.make_async_copy(mix_hbm, mix, in_sem.at[2]),
        pltpu.make_async_copy(sizes_hbm, sizes, in_sem.at[3]),
    ]
    env_loads = [
        pltpu.make_async_copy(right_hbm.at[:, 0], own_env.at[0], in_sem.at[4]),
        pltpu.make_async_copy(left_hbm.at[:, 0], own_env.at[1], in_sem.at[5]),
    ]
    for load in loads:
        load.start()
    gap = lax.rem(z - k + TR + 1, TR)

    @pl.when(gap < 4)
    def _():
        for load in env_loads:
            load.start()

    barrier = pltpu.get_barrier_semaphore()

    def greet_tr(i, carry):
        pl.semaphore_signal(barrier, inc=1, device_id=ring(wrap(z + i, TR)), device_id_type=MESH)
        return carry

    def greet_sec(i, carry):
        pl.semaphore_signal(
            barrier, inc=1, device_id={"sec": wrap(sec + i, SEC)}, device_id_type=MESH
        )
        return carry

    partner = sec + 1 - 2 * core
    pl.semaphore_signal(
        barrier,
        inc=1,
        device_id={"tr": lax.rem(z + 2 * core - 1 + TR, TR), "sec": partner},
        device_id_type=MESH,
    )
    def greet_far(j, carry):
        @pl.when((k != z) | (j != k))
        def _():
            pl.semaphore_signal(
                barrier,
                inc=1,
                device_id={"tr": k, "sec": 2 * j + core},
                device_id_type=MESH,
            )

        return carry

    lax.fori_loop(1, SEC, greet_sec, 0)
    lax.fori_loop(1, TR, greet_tr, 0)
    lax.fori_loop(0, TR, greet_far, 0)

    line = iota((LINES, LINES), 0)
    other = iota((LINES, LINES), 1)

    for n, (one, two) in enumerate(((line, other), (other, line))):
        same = one == under(two, 3) * ROWS + over(two, 3)
        swap[n] = same.astype(BF16)

    def to_phys_major(value):
        return dot(swap[0], value)

    def to_row_major(value):
        return dot(swap[1], value)

    loads[3].wait()
    used_left = sizes[0, 0]
    used_right = sizes[0, 1]
    keep = ((z * ROWS + over(iota((LINES, WIDTH), 0), 3)) < used_right) & (
        iota((LINES, WIDTH), 1) < used_left
    )
    loads[0].wait()
    start = jnp.where(keep, psi_in[...].astype(F32).reshape(LINES, WIDTH), 0.0).astype(BF16)
    start_rows[...] = start
    store_columns(cols_send, to_phys_major(start).astype(BF16))
    loads[1].wait()
    pc_send[...] = pc_in[...].astype(F32).reshape(TR, 2 * PHYS, WIDTH).astype(BF16)

    pl.semaphore_wait(barrier, TR + SEC - 1 + TR - jnp.where(k == z, 1, 0))

    def move_in_plane(n, source, middle):
        def send(i, carry):
            peer = plane_peer(i)
            remote(
                source.at[peer],
                middle.at[k],
                move_send_sem.at[n, 0],
                move_one_sem.at[n, k],
                plane(peer),
            ).start()
            return carry

        lax.fori_loop(1, TR, send, 0)
        middle[k] = source[k]
        ends.append(several(middle, TR - 1, move_send_sem.at[n, 0], move_two_sem.at[n]))

    def arrived(n, middle, index):
        return remote(
            middle.at[index],
            middle.at[index],
            move_send_sem.at[n, 0],
            move_one_sem.at[n, index],
            ring(next_z),
        )

    def move_in_ring(n, middle, target):
        def send(i, carry):
            peer = ring_peer(i)

            @pl.when(peer != k)
            def _():
                arrived(n, middle, peer).wait_recv()

            remote(
                middle.at[peer], target.at[z], move_send_sem.at[n, 1], move_two_sem.at[n], ring(peer)
            ).start()
            return carry

        lax.fori_loop(0, TR - 1, send, 0)

        @pl.when(z != k)
        def _():
            arrived(n, middle, z).wait_recv()

        target[z] = middle[z]
        done = several(target, TR - 1, move_send_sem.at[n, 1], move_two_sem.at[n])
        ends.append(done)
        return done

    def back(n, source, target, begin, end):
        def send(i, carry):
            peer = ring_peer(i)
            remote(
                source.at[peer],
                target.at[k],
                move_send_sem.at[n, 0],
                move_two_sem.at[n],
                {"tr": peer, "sec": 2 * z + core},
            ).start()
            return carry

        lax.fori_loop(begin, end, send, 0)

    def back_home(n, source, target):
        @pl.when(z != k)
        def _():
            remote(
                source.at[z],
                target.at[k],
                move_send_sem.at[n, 0],
                move_two_sem.at[n],
                {"tr": z, "sec": 2 * z + core},
            ).start()

        @pl.when(z == k)
        def _():
            target[k] = source[k]

    def back_wait(n, target, sent):
        for same in range(2):

            @pl.when((z == k) if same else (z != k))
            def _():
                done = several(target, TR - same, move_send_sem.at[n, 0], move_two_sem.at[n])
                if sent:
                    done.wait_send()
                else:
                    done.wait_recv()

    def env_matrix(m, c):
        return env[m, c].reshape(WIDTH, WIDTH)

    def piece(m, dy, dx, part=(pl.ds(0, ROWS), pl.ds(0, WIDTH))):
        return env.at[m, :, rows_at[dy % 4], columns_at[dx % 4], part[0], part[1]]

    def row_set(m, dy, part):
        return env.at[m, :, rows_at[dy % 4], :, part[0], part[1]]

    def column_set(m, dx, part):
        return env.at[m, :, :, columns_at[dx % 4], part[0], part[1]]

    def scatter_copy(m, d, n):
        return remote(
            own_env.at[m, :, pl.ds((4 * d + n) * ROWS, ROWS), :],
            land_env.at[m],
            scatter_send_sem.at[m, n],
            scatter_recv_sem.at[m],
            plane(4 * d + n),
        )

    def scatter(m):
        used = used_right if m == 0 else used_left
        for d in range(4):

            @pl.when(gap == d)
            def _():
                env_loads[m].wait()
                span = pl.ds(4 * d * ROWS, 4 * ROWS)
                rows = own_env[m, :, span, :]
                own_env[m, :, span, :] = jnp.where(4 * d * ROWS < used, rows, jnp.zeros_like(rows))
                for n in range(4):

                    @pl.when(k != 4 * d + n)
                    def _():
                        scatter_copy(m, d, n).start()

                    @pl.when(k == 4 * d + n)
                    def _():
                        land_env[m] = own_env[m, :, pl.ds((4 * d + n) * ROWS, ROWS), :]

    def scatter_end(m):
        for d in range(4):

            @pl.when(gap == d)
            def _():
                for n in range(4):

                    @pl.when(k != 4 * d + n)
                    def _():
                        scatter_copy(m, d, n).wait_send()

    shift = y - 1
    home = lax.rem(z - shift + TR, TR)

    def hand_over(m):
        return remote(
            land_env.at[m], piece(m, 0, 0), own_send_sem.at[m], own_recv_sem.at[m], ring(home)
        )

    def keep_here(m):
        return pltpu.make_async_copy(land_env.at[m], piece(m, 0, 0), own_recv_sem.at[m])

    def own_start(m):
        @pl.when(home != k)
        def _():
            remote(
                land_env.at[m],
                land_env.at[m],
                own_send_sem.at[m],
                scatter_recv_sem.at[m],
                ring(next_z),
            ).wait_recv()

        @pl.when(shift != 0)
        def _():
            hand_over(m).start()

        @pl.when(shift == 0)
        def _():
            keep_here(m).start()

    def own_wait(m):
        @pl.when(shift != 0)
        def _():
            hand_over(m).wait_recv()

        @pl.when(shift == 0)
        def _():
            keep_here(m).wait()

    first = (pl.ds(0, 16), pl.ds(0, WIDTH))
    last = (pl.ds(16, 16), pl.ds(0, WIDTH))
    quarters = [(pl.ds(n // 2 * 16, 16), pl.ds(n % 2 * HALF, HALF)) for n in range(4)]

    def hop(m, n, ref, dy, dx):
        target = 4 * rows_at[dy % 4] + columns_at[dx % 4]
        return remote(ref, ref, gather_send_sem.at[m], gather_recv_sem.at[m, n], plane(target))

    def gather_one(m):
        own_wait(m)
        hop(m, 0, piece(m, 0, 0, first), 0, 1).start()
        hop(m, 1, piece(m, 0, 0, first), 0, -1).start()
        hop(m, 2, piece(m, 0, 0, last), 1, 0).start()
        hop(m, 3, piece(m, 0, 0, last), -1, 0).start()

    def gather_two(m):
        hop(m, 0, piece(m, 0, -1, first), 0, -1).wait_recv()
        hop(m, 4, piece(m, 0, -1, quarters[0]), 0, 1).start()
        hop(m, 1, piece(m, 0, 1, first), 0, 1).wait_recv()
        hop(m, 5, piece(m, 0, 1, quarters[1]), 0, -1).start()
        hop(m, 2, piece(m, -1, 0, last), -1, 0).wait_recv()
        hop(m, 6, piece(m, -1, 0, quarters[2]), 1, 0).start()
        hop(m, 3, piece(m, 1, 0, last), 1, 0).wait_recv()
        hop(m, 7, piece(m, 1, 0, quarters[3]), -1, 0).start()

    def gather_three(m):
        hop(m, 4, piece(m, 0, 2, quarters[0]), 0, -1).wait_recv()
        hop(m, 5, piece(m, 0, 2, quarters[1]), 0, 1).wait_recv()
        hop(m, 8, row_set(m, 0, first), 1, 0).start()
        hop(m, 9, row_set(m, 0, first), -1, 0).start()
        hop(m, 6, piece(m, 2, 0, quarters[2]), -1, 0).wait_recv()
        hop(m, 7, piece(m, 2, 0, quarters[3]), 1, 0).wait_recv()
        hop(m, 10, column_set(m, 0, last), 0, 1).start()
        hop(m, 11, column_set(m, 0, last), 0, -1).start()

    def gather_four(m):
        hop(m, 8, row_set(m, -1, first), -1, 0).wait_recv()
        hop(m, 12, row_set(m, -1, quarters[0]), 1, 0).start()
        hop(m, 9, row_set(m, 1, first), 1, 0).wait_recv()
        hop(m, 13, row_set(m, 1, quarters[1]), -1, 0).start()
        hop(m, 10, column_set(m, -1, last), 0, -1).wait_recv()
        hop(m, 14, column_set(m, -1, quarters[2]), 0, 1).start()
        hop(m, 11, column_set(m, 1, last), 0, 1).wait_recv()
        hop(m, 15, column_set(m, 1, quarters[3]), 0, -1).start()

    def gather_wait(m):
        hop(m, 12, row_set(m, 2, quarters[0]), -1, 0).wait_recv()
        hop(m, 13, row_set(m, 2, quarters[1]), 1, 0).wait_recv()
        hop(m, 14, column_set(m, 2, quarters[2]), 0, -1).wait_recv()
        hop(m, 15, column_set(m, 2, quarters[3]), 0, 1).wait_recv()

    def gather_end(m):
        sent = own_env.at[m, :, pl.ds(0, WIDTH - ROWS), :]
        remote(
            sent, sent, gather_send_sem.at[m], own_recv_sem.at[m], ring(next_z)
        ).wait_send()

    def turn(n, sources, targets, begin, count):
        source = sources.at[pl.ds(begin, count)]
        target = targets.at[pl.ds(begin, count)]

        def send(i, carry):
            peer = plane_peer(i)
            remote(
                source.at[:, peer],
                target.at[:, k],
                turn_send_sem.at[n],
                turn_recv_sem.at[n],
                plane(peer),
            ).start()
            return carry

        lax.fori_loop(1, TR, send, 0)
        for place in range(begin, begin + count):
            targets[place, k] = sources[place, k]
        part = target.at[:, pl.ds(0, TR - 1)]
        done = remote(
            part, part, turn_send_sem.at[n], turn_recv_sem.at[n], ring(next_z)
        )
        ends.append(done)
        return done

    sector = 2 * z + core

    def shifts(n, source, target):
        copies = []
        for way in range(2):
            copy = remote(
                source,
                target.at[way],
                near_send_sem.at[n, way],
                near_recv_sem.at[n, way],
                {"tr": lax.rem(z + core - way + TR, TR), "sec": partner},
            )
            copy.start()
            copies.append(copy)
        ends.extend(copies)
        return copies

    def inside(way, value):
        exists = sector > 0 if way == 0 else sector < SEC - 1
        return jnp.where(exists, value, jnp.zeros_like(value))

    move_in_plane(0, cols_send, cols_mid)
    scatter(0)
    own_start(0)
    cols_done = move_in_ring(0, cols_mid, cols)
    scatter(1)
    gather_one(0)
    move_in_plane(1, pc_send, pc_mid)

    wide_line = iota((WIDTH, WIDTH), 0)
    wide_other = iota((WIDTH, WIDTH), 1)

    def old_row(r):
        pair = over(r, 1)
        return under(pair, 4) * 32 + over(r, 5) * 2 + r - 2 * pair

    to_new[...] = (old_row(wide_line) == wide_other).astype(BF16)
    gather_two(0)
    to_old[...] = (old_row(wide_other) == wide_line).astype(BF16)
    loads[2].wait()
    spread = (over(iota((LINES, PHYS), 0), 5) == iota((LINES, PHYS), 1)).astype(BF16)
    same_row = under(line, 5) == under(other, 5)
    for c in range(3):
        mixed = dot_nt(dot(spread, mix[c]).astype(BF16), spread)
        kron[c] = jnp.where(same_row, mixed, 0.0).astype(BF16)
    own_start(1)
    gather_three(0)

    def reordered(value):
        return dot(to_new[...], value).astype(BF16).reshape(TR, ROWS, HALF)

    def right_part(c, value):
        return reordered(dot(env_matrix(0, c), value).astype(BF16))

    cols_done.wait_recv()
    copies = shifts(0, cols, near_cols)
    own_cols = cols[...].reshape(WIDTH, HALF)
    turn_send[3] = reordered(own_cols)
    start_turn = turn(2, turn_send, turn_recv, 3, 1)
    gather_four(0)
    gather_one(1)
    gather_wait(0)
    turn_send[0] = right_part(0, own_cols)
    turns = [turn(0, turn_send, turn_recv, 0, 1)]
    gather_two(1)
    for way in range(2):
        copies[way].wait_recv()
        turn_send[way + 1] = right_part(
            way + 1, inside(way, near_cols[way].reshape(WIDTH, HALF))
        )
    turns.append(turn(1, turn_send, turn_recv, 1, 2))
    gather_three(1)
    pc_done = move_in_ring(1, pc_mid, pc_new)
    gather_four(1)
    gather_wait(1)
    total = None
    for c in range(3):
        if c < 2:
            turns[c].wait_recv()
        mixed = dot(kron[c], phys_major(turn_recv[c])).astype(BF16)
        term = dot_nt(mixed, env_matrix(1, c))
        total = term if total is None else total + term
    rounded = total.astype(BF16)
    first_send[...] = to_row_major(rounded).astype(BF16).reshape(TR, 2 * PHYS, WIDTH)
    image0 = rounded.astype(F32)
    start_turn.wait_recv()
    s = phys_major(turn_recv[3]).astype(F32)
    pc_done.wait_recv()
    factors = to_phys_major(pc_new[...].reshape(LINES, WIDTH))

    def tr_start(h, block):
        red_send[h, 0] = block

        def send(i, carry):
            remote(
                red_send.at[h, 0],
                red_tr.at[h, z],
                red_send_sem.at[h, 0],
                red_recv_sem.at[h, 0],
                ring(ring_peer(i)),
            ).start()
            return carry

        lax.fori_loop(0, TR - 1, send, 0)
        red_tr[h, z] = block
        done = several(red_tr.at[h], TR - 1, red_send_sem.at[h, 0], red_recv_sem.at[h, 0])
        ends.append(done)
        return done

    def sec_start(h, block):
        red_send[h, 1] = block

        def send(i, carry):
            remote(
                red_send.at[h, 1],
                red_sec.at[h, sec],
                red_send_sem.at[h, 1],
                red_recv_sem.at[h, 1],
                {"sec": wrap(sec + i, SEC)},
            ).start()
            return carry

        lax.fori_loop(1, SEC, send, 0)
        red_sec[h, sec] = block
        done = several(red_sec.at[h], SEC - 1, red_send_sem.at[h, 1], red_recv_sem.at[h, 1])
        ends.append(done)
        return done

    def means(block):
        whole = jnp.sum(block, axis=1, keepdims=True)
        return [whole[n : n + 1] / COUNT for n in range(4)]

    weighted = s * factors
    parts = (s * s, s * image0, weighted * image0, weighted * s)
    block = jnp.concatenate([partial_sum(part) for part in parts] * 2, axis=0)
    tr_start(0, block).wait_recv()
    sums_done = sec_start(0, jnp.sum(red_tr[0], axis=0))
    back(2, first_send, first_old, 0, 5)
    sums_done.wait_recv()
    ss, sw, spw, sps = means(jnp.sum(red_sec[0], axis=0))
    norm = lax.rsqrt(ss + EPSILON)
    theta = norm * norm * sw
    along = norm * norm * (spw - theta * sps)

    def trial_of(image, vector, weights):
        return (image - theta * vector) * weights - along * vector

    trial = trial_of(image0, s, factors)
    trial_bf = trial.astype(BF16)
    vec[...] = trial_bf

    copies = shifts(1, vec, near_vec)
    turns = []

    def left_part(c, value):
        mixed = dot(kron[c], value).astype(BF16)
        return dot_nt(mixed, env_matrix(1, c)).astype(BF16)

    store_columns(half_send.at[0], left_part(0, trial_bf))
    turns = [turn(3, half_send, half_recv, 0, 1)]
    store_columns(half_send.at[3], trial_bf)
    for way in range(2):
        copies[way].wait_recv()
        store_columns(half_send.at[way + 1], left_part(way + 1, inside(way, near_vec[way])))
    turns.append(turn(4, half_send, half_recv, 1, 2))
    trial_turn = turn(5, half_send, half_recv, 3, 1)
    back(2, first_send, first_old, 5, TR - 1)
    back_home(2, first_send, first_old)
    second = trial_bf.astype(F32)
    tt = partial_sum(trial * trial)
    t0 = partial_sum(second * image0)
    total = None
    for c in range(3):
        if c < 2:
            turns[c].wait_recv()
        half = dot(to_old[...], half_recv[c].reshape(WIDTH, HALF)).astype(BF16)
        term = dot(env_matrix(0, c), half)
        total = term if total is None else total + term
    second_send[...] = total.astype(BF16).reshape(TR, ROWS, HALF)
    back(3, second_send, second_old, 0, TR - 1)
    back_home(3, second_send, second_old)
    image1_cols = total.astype(BF16).astype(F32)
    trial_turn.wait_recv()
    trial_cols = dot(to_old[...], half_recv[3].reshape(WIDTH, HALF))
    s1 = partial_sum(cols[...].reshape(WIDTH, HALF).astype(F32) * image1_cols)
    t1 = partial_sum(trial_cols * image1_cols)
    block = jnp.concatenate([tt, s1, t0, t1] * 2, axis=0)
    sec_start(1, block).wait_recv()
    sums_done = tr_start(1, jnp.sum(red_sec[1], axis=0))
    sums_done.wait_recv()
    tt, s1, t0, t1 = means(jnp.sum(red_tr[1], axis=0))

    fresh = norm * norm * tt
    grow = norm * lax.rsqrt(fresh + EPSILON)
    cross = 0.5 * norm * grow * (s1 + t0)
    corner = grow * grow * t1
    halfgap = 0.5 * (theta - corner)
    energy = 0.5 * (theta + corner) - jnp.sqrt(halfgap * halfgap + cross * cross)
    weight_one = corner - energy
    weight_two = -cross
    scale = lax.rsqrt(weight_one * weight_one + weight_two * weight_two)
    one = weight_one * scale * norm
    two = weight_two * scale * grow
    energy_out[...] = energy

    back_wait(2, first_old, False)
    old_image = first_old[...].reshape(LINES, WIDTH).astype(F32)
    old_start = start_rows[...].astype(F32)
    old_factors = pc_send[...].reshape(LINES, WIDTH).astype(F32)
    old_trial = trial_of(old_image, old_start, old_factors).astype(BF16).astype(F32)
    ritz = one * old_start + two * old_trial
    psi_out[...] = ritz.reshape(ROWS, PHYS, WIDTH).astype(BF16)[None]
    partial = one * old_image - energy * ritz
    back_wait(3, second_old, False)
    residual = partial + two * to_row_major(phys_major(second_old[...]))
    res_out[...] = residual.reshape(ROWS, PHYS, WIDTH).astype(BF16)[None]

    for m in range(2):
        scatter_end(m)
        gather_end(m)

        @pl.when(shift != 0)
        def _():
            hand_over(m).wait_send()

    back_wait(2, first_old, True)
    back_wait(3, second_old, True)
    for end in ends:
        end.wait_send()


def body(psi, precond, env_left, env_right, mixers, sizes):
    anywhere = pl.BlockSpec(memory_space=pl.ANY)
    vmem = pl.BlockSpec(memory_space=pltpu.VMEM)
    dma = pltpu.SemaphoreType.DMA
    columns = (TR, ROWS, HALF)
    fours = (4, TR, ROWS, HALF)
    rows = (TR, 2 * PHYS, WIDTH)
    psi_new, residual_new, energy = pl.pallas_call(
        kernel,
        out_shape=(
            jax.ShapeDtypeStruct(psi.shape, BF16),
            jax.ShapeDtypeStruct(psi.shape, BF16),
            jax.ShapeDtypeStruct((1, 1), F32),
        ),
        in_specs=[anywhere] * 6,
        out_specs=(vmem, vmem, vmem),
        scratch_shapes=[
            pltpu.VMEM((ROWS, PHYS, WIDTH), BF16),
            pltpu.VMEM((ROWS, PHYS, WIDTH), BF16),
            pltpu.VMEM((3, PHYS, PHYS), BF16),
            pltpu.SMEM((1, 2), jnp.int32),
            pltpu.VMEM((2, 3, WIDTH, WIDTH), BF16),
            pltpu.VMEM((2, 3, ROWS, WIDTH), BF16),
            pltpu.VMEM((2, 3, 4, 4, ROWS, WIDTH), BF16),
            pltpu.VMEM((3, LINES, LINES), BF16),
            pltpu.VMEM((2, LINES, LINES), BF16),
            pltpu.VMEM((WIDTH, WIDTH), BF16),
            pltpu.VMEM((WIDTH, WIDTH), BF16),
            pltpu.VMEM((LINES, WIDTH), BF16),
            pltpu.VMEM(columns, BF16),
            pltpu.VMEM(columns, BF16),
            pltpu.VMEM(columns, BF16),
            pltpu.VMEM((2, *columns), BF16),
            pltpu.VMEM(fours, BF16),
            pltpu.VMEM(fours, BF16),
            pltpu.VMEM(rows, BF16),
            pltpu.VMEM(rows, BF16),
            pltpu.VMEM(rows, BF16),
            pltpu.VMEM((LINES, WIDTH), BF16),
            pltpu.VMEM((2, LINES, WIDTH), BF16),
            pltpu.VMEM(fours, BF16),
            pltpu.VMEM(fours, BF16),
            pltpu.VMEM(rows, BF16),
            pltpu.VMEM(rows, BF16),
            pltpu.VMEM(columns, BF16),
            pltpu.VMEM(columns, BF16),
            pltpu.VMEM((2, 2, 8, 128), F32),
            pltpu.VMEM((2, TR, 8, 128), F32),
            pltpu.VMEM((2, SEC, 8, 128), F32),
            dma((6,)),
            dma((2, 4)),
            dma((2,)),
            dma((2,)),
            dma((2,)),
            dma((2,)),
            dma((2, 16)),
            dma((2, 2)),
            dma((2, 2)),
            dma((6,)),
            dma((6,)),
            dma((4, 2)),
            dma((4, TR)),
            dma((4,)),
            dma((2, 2)),
            dma((2, 2)),
        ],
        compiler_params=pltpu.CompilerParams(
            collective_id=0, has_side_effects=True, vmem_limit_bytes=60 * 1024 * 1024
        ),
        cost_estimate=pl.CostEstimate(
            flops=2_200_000_000, bytes_accessed=2_000_000, transcendentals=0
        ),
    )(psi, precond, env_left, env_right, mixers, sizes)
    return psi_new, residual_new, energy.reshape(())


def solution(mesh):
    placed = (
        P("sec", "tr", None, None),
        P("sec", "tr", None, None),
        P(None, "sec", None, None),
        P(None, "sec", None, None),
        P(),
        P("sec", None),
    )
    return jax.shard_map(
        body,
        mesh=mesh,
        in_specs=placed,
        out_specs=(P("sec", "tr", None, None), P("sec", "tr", None, None), P()),
        check_vma=False,
    )
```

```python
import jax
import jax.numpy as jnp
from jax import lax
from jax.experimental import pallas as pl
from jax.experimental.pallas import tpu as pltpu
from jax.sharding import PartitionSpec as P

EPSILON = 1e-06
MESH = pl.DeviceIdType.MESH
F32 = jnp.float32
BF16 = jnp.bfloat16
TR = 16
SEC = 32
ROWS = 32
PHYS = 8
WIDTH = 512
HALF = 256
LINES = ROWS * PHYS
COUNT = float(SEC * WIDTH * PHYS * WIDTH)
STEPS = (1, 3, 2)


def dot(a, b):
    return jnp.dot(a, b, preferred_element_type=F32)


def dot_nt(a, b):
    return lax.dot_general(a, b, (((1,), (1,)), ((), ())), preferred_element_type=F32)


def iota(shape, axis):
    return lax.broadcasted_iota(jnp.int32, shape, axis)


def wrap(value, size):
    return jnp.where(value >= size, value - size, value)


def over(value, bits):
    return lax.shift_right_logical(value, jnp.full_like(value, bits))


def under(value, bits):
    return value - lax.shift_left(over(value, bits), jnp.full_like(value, bits))


def partial_sum(x):
    rows = jnp.sum(x, axis=0, keepdims=True)
    total = rows[:, 0:128]
    for lane in range(128, x.shape[1], 128):
        total = total + rows[:, lane : lane + 128]
    return total


def phys_major(block):
    pieces = [jnp.concatenate([block[2 * p], block[2 * p + 1]], axis=1) for p in range(PHYS)]
    return jnp.concatenate(pieces, axis=0)


def store_columns(ref, value):
    for j in range(TR):
        p, side = divmod(j, 2)
        ref[j] = value[p * ROWS : (p + 1) * ROWS, side * HALF : (side + 1) * HALF]


def kernel(
    psi_hbm,
    pc_hbm,
    left_hbm,
    right_hbm,
    mix_hbm,
    sizes_hbm,
    psi_out,
    res_out,
    energy_out,
    psi_in,
    pc_in,
    mix,
    sizes,
    own_env,
    land_env,
    env,
    kron,
    swap,
    to_new,
    to_old,
    right_old,
    left_turned,
    start_rows,
    cols_send,
    cols_mid,
    cols,
    near_cols,
    turn_send,
    turn_recv,
    pc_send,
    pc_mid,
    pc_new,
    vec,
    near_vec,
    half_send,
    half_recv,
    first_send,
    first_old,
    second_send,
    second_old,
    red_send,
    red_tr,
    red_sec,
    in_sem,
    scatter_send_sem,
    scatter_recv_sem,
    own_send_sem,
    own_recv_sem,
    gather_send_sem,
    gather_recv_sem,
    near_send_sem,
    near_recv_sem,
    turn_send_sem,
    turn_recv_sem,
    move_send_sem,
    move_one_sem,
    move_two_sem,
    red_send_sem,
    red_recv_sem,
):
    z = lax.axis_index("tr")
    sec = lax.axis_index("sec")
    k = over(sec, 1)
    core = sec - 2 * k
    y = over(k, 2)
    x = k - 4 * y
    next_z = wrap(z + 1, TR)
    rows_at = [y] + [wrap(y + d, 4) for d in range(1, 4)]
    columns_at = [x] + [wrap(x + d, 4) for d in range(1, 4)]

    def ring(z2):
        return {"tr": z2}

    def plane(k2):
        return {"sec": 2 * k2 + core}

    def turned(m):
        return jnp.where(m >= TR - 1, m - (TR - 1), m)

    def ring_peer(i):
        m = turned(i + k)
        half = over(m, 1)
        step = half + 1
        return wrap(z + jnp.where(m == 2 * half, step, TR - step), TR)

    def plane_peer(i):
        down = over(i, 2)
        return 4 * wrap(y + down, 4) + wrap(x + i - 4 * down, 4)

    def remote(src, dst, send_sem, recv_sem, device):
        return pltpu.make_async_remote_copy(
            src_ref=src,
            dst_ref=dst,
            send_sem=send_sem,
            recv_sem=recv_sem,
            device_id=device,
            device_id_type=MESH,
        )

    def several(ref, count, send_sem, recv_sem):
        part = ref.at[pl.ds(0, count)]
        return remote(part, part, send_sem, recv_sem, ring(next_z))

    ends = []

    loads = [
        pltpu.make_async_copy(psi_hbm.at[0], psi_in, in_sem.at[0]),
        pltpu.make_async_copy(pc_hbm.at[0], pc_in, in_sem.at[1]),
        pltpu.make_async_copy(mix_hbm, mix, in_sem.at[2]),
        pltpu.make_async_copy(sizes_hbm, sizes, in_sem.at[3]),
    ]
    env_loads = [
        pltpu.make_async_copy(right_hbm.at[:, 0], own_env.at[0], in_sem.at[4]),
        pltpu.make_async_copy(left_hbm.at[:, 0], own_env.at[1], in_sem.at[5]),
    ]
    for load in loads:
        load.start()
    gap = lax.rem(z - k + TR + 1, TR)

    @pl.when(gap < 4)
    def _():
        for load in env_loads:
            load.start()

    barrier = pltpu.get_barrier_semaphore()

    def greet_tr(i, carry):
        pl.semaphore_signal(barrier, inc=1, device_id=ring(wrap(z + i, TR)), device_id_type=MESH)
        return carry

    def greet_sec(i, carry):
        pl.semaphore_signal(
            barrier, inc=1, device_id={"sec": wrap(sec + i, SEC)}, device_id_type=MESH
        )
        return carry

    partner = sec + 1 - 2 * core
    pl.semaphore_signal(
        barrier,
        inc=1,
        device_id={"tr": lax.rem(z + 2 * core - 1 + TR, TR), "sec": partner},
        device_id_type=MESH,
    )
    def greet_far(j, carry):
        @pl.when((k != z) | (j != k))
        def _():
            pl.semaphore_signal(
                barrier,
                inc=1,
                device_id={"tr": k, "sec": 2 * j + core},
                device_id_type=MESH,
            )

        return carry

    lax.fori_loop(1, SEC, greet_sec, 0)
    lax.fori_loop(1, TR, greet_tr, 0)
    lax.fori_loop(0, TR, greet_far, 0)

    line = iota((LINES, LINES), 0)
    other = iota((LINES, LINES), 1)

    for n, (one, two) in enumerate(((line, other), (other, line))):
        same = one == under(two, 3) * ROWS + over(two, 3)
        swap[n] = same.astype(BF16)

    def to_phys_major(value):
        return dot(swap[0], value)

    def to_row_major(value):
        return dot(swap[1], value)

    loads[3].wait()
    used_left = sizes[0, 0]
    used_right = sizes[0, 1]
    keep = ((z * ROWS + over(iota((LINES, WIDTH), 0), 3)) < used_right) & (
        iota((LINES, WIDTH), 1) < used_left
    )
    loads[0].wait()
    start = jnp.where(keep, psi_in[...].astype(F32).reshape(LINES, WIDTH), 0.0).astype(BF16)
    start_rows[...] = start
    store_columns(cols_send, to_phys_major(start).astype(BF16))
    loads[1].wait()
    pc_send[...] = pc_in[...].astype(F32).reshape(TR, 2 * PHYS, WIDTH).astype(BF16)

    pl.semaphore_wait(barrier, TR + SEC - 1 + TR - jnp.where(k == z, 1, 0))

    def move_in_plane(n, source, middle):
        def send(i, carry):
            peer = plane_peer(i)
            remote(
                source.at[peer],
                middle.at[k],
                move_send_sem.at[n, 0],
                move_one_sem.at[n, k],
                plane(peer),
            ).start()
            return carry

        lax.fori_loop(1, TR, send, 0)
        middle[k] = source[k]
        ends.append(several(middle, TR - 1, move_send_sem.at[n, 0], move_two_sem.at[n]))

    def arrived(n, middle, index):
        return remote(
            middle.at[index],
            middle.at[index],
            move_send_sem.at[n, 0],
            move_one_sem.at[n, index],
            ring(next_z),
        )

    def move_in_ring(n, middle, target):
        def send(i, carry):
            peer = ring_peer(i)

            @pl.when(peer != k)
            def _():
                arrived(n, middle, peer).wait_recv()

            remote(
                middle.at[peer], target.at[z], move_send_sem.at[n, 1], move_two_sem.at[n], ring(peer)
            ).start()
            return carry

        lax.fori_loop(0, TR - 1, send, 0)

        @pl.when(z != k)
        def _():
            arrived(n, middle, z).wait_recv()

        target[z] = middle[z]
        done = several(target, TR - 1, move_send_sem.at[n, 1], move_two_sem.at[n])
        ends.append(done)
        return done

    def back(n, source, target, begin, end):
        def send(i, carry):
            peer = ring_peer(i)
            remote(
                source.at[peer],
                target.at[k],
                move_send_sem.at[n, 0],
                move_two_sem.at[n],
                {"tr": peer, "sec": 2 * z + core},
            ).start()
            return carry

        lax.fori_loop(begin, end, send, 0)

    def back_home(n, source, target):
        @pl.when(z != k)
        def _():
            remote(
                source.at[z],
                target.at[k],
                move_send_sem.at[n, 0],
                move_two_sem.at[n],
                {"tr": z, "sec": 2 * z + core},
            ).start()

        @pl.when(z == k)
        def _():
            target[k] = source[k]

    def back_wait(n, target, sent):
        for same in range(2):

            @pl.when((z == k) if same else (z != k))
            def _():
                done = several(target, TR - same, move_send_sem.at[n, 0], move_two_sem.at[n])
                if sent:
                    done.wait_send()
                else:
                    done.wait_recv()

    def env_matrix(m, c):
        return env[m, c].reshape(WIDTH, WIDTH)

    def piece(m, dy, dx, part=(pl.ds(0, ROWS), pl.ds(0, WIDTH))):
        return env.at[m, :, rows_at[dy % 4], columns_at[dx % 4], part[0], part[1]]

    def row_set(m, dy, part):
        return env.at[m, :, rows_at[dy % 4], :, part[0], part[1]]

    def column_set(m, dx, part):
        return env.at[m, :, :, columns_at[dx % 4], part[0], part[1]]

    def scatter_copy(m, d, n):
        return remote(
            own_env.at[m, :, pl.ds((4 * d + n) * ROWS, ROWS), :],
            land_env.at[m],
            scatter_send_sem.at[m, n],
            scatter_recv_sem.at[m],
            plane(4 * d + n),
        )

    def scatter(m):
        used = used_right if m == 0 else used_left
        for d in range(4):

            @pl.when(gap == d)
            def _():
                env_loads[m].wait()
                span = pl.ds(4 * d * ROWS, 4 * ROWS)
                rows = own_env[m, :, span, :]
                own_env[m, :, span, :] = jnp.where(4 * d * ROWS < used, rows, jnp.zeros_like(rows))
                for n in range(4):

                    @pl.when(k != 4 * d + n)
                    def _():
                        scatter_copy(m, d, n).start()

                    @pl.when(k == 4 * d + n)
                    def _():
                        land_env[m] = own_env[m, :, pl.ds((4 * d + n) * ROWS, ROWS), :]

    def scatter_end(m):
        for d in range(4):

            @pl.when(gap == d)
            def _():
                for n in range(4):

                    @pl.when(k != 4 * d + n)
                    def _():
                        scatter_copy(m, d, n).wait_send()

    shift = y - 1
    home = lax.rem(z - shift + TR, TR)

    def hand_over(m):
        return remote(
            land_env.at[m], piece(m, 0, 0), own_send_sem.at[m], own_recv_sem.at[m], ring(home)
        )

    def keep_here(m):
        return pltpu.make_async_copy(land_env.at[m], piece(m, 0, 0), own_recv_sem.at[m])

    def own_start(m):
        @pl.when(home != k)
        def _():
            remote(
                land_env.at[m],
                land_env.at[m],
                own_send_sem.at[m],
                scatter_recv_sem.at[m],
                ring(next_z),
            ).wait_recv()

        @pl.when(shift != 0)
        def _():
            hand_over(m).start()

        @pl.when(shift == 0)
        def _():
            keep_here(m).start()

    def own_wait(m):
        @pl.when(shift != 0)
        def _():
            hand_over(m).wait_recv()

        @pl.when(shift == 0)
        def _():
            keep_here(m).wait()

    first = (pl.ds(0, 16), pl.ds(0, WIDTH))
    last = (pl.ds(16, 16), pl.ds(0, WIDTH))
    quarters = [(pl.ds(n // 2 * 16, 16), pl.ds(n % 2 * HALF, HALF)) for n in range(4)]

    def hop(m, n, ref, dy, dx):
        target = 4 * rows_at[dy % 4] + columns_at[dx % 4]
        return remote(ref, ref, gather_send_sem.at[m], gather_recv_sem.at[m, n], plane(target))

    def gather_one(m):
        own_wait(m)
        hop(m, 0, piece(m, 0, 0, first), 0, 1).start()
        hop(m, 1, piece(m, 0, 0, first), 0, -1).start()
        hop(m, 2, piece(m, 0, 0, last), 1, 0).start()
        hop(m, 3, piece(m, 0, 0, last), -1, 0).start()

    def gather_two(m):
        hop(m, 0, piece(m, 0, -1, first), 0, -1).wait_recv()
        hop(m, 4, piece(m, 0, -1, quarters[0]), 0, 1).start()
        hop(m, 1, piece(m, 0, 1, first), 0, 1).wait_recv()
        hop(m, 5, piece(m, 0, 1, quarters[1]), 0, -1).start()
        hop(m, 2, piece(m, -1, 0, last), -1, 0).wait_recv()
        hop(m, 6, piece(m, -1, 0, quarters[2]), 1, 0).start()
        hop(m, 3, piece(m, 1, 0, last), 1, 0).wait_recv()
        hop(m, 7, piece(m, 1, 0, quarters[3]), -1, 0).start()

    def gather_three(m):
        hop(m, 4, piece(m, 0, 2, quarters[0]), 0, -1).wait_recv()
        hop(m, 5, piece(m, 0, 2, quarters[1]), 0, 1).wait_recv()
        hop(m, 8, row_set(m, 0, first), 1, 0).start()
        hop(m, 9, row_set(m, 0, first), -1, 0).start()
        hop(m, 6, piece(m, 2, 0, quarters[2]), -1, 0).wait_recv()
        hop(m, 7, piece(m, 2, 0, quarters[3]), 1, 0).wait_recv()
        hop(m, 10, column_set(m, 0, last), 0, 1).start()
        hop(m, 11, column_set(m, 0, last), 0, -1).start()

    def gather_four(m):
        hop(m, 8, row_set(m, -1, first), -1, 0).wait_recv()
        hop(m, 12, row_set(m, -1, quarters[0]), 1, 0).start()
        hop(m, 9, row_set(m, 1, first), 1, 0).wait_recv()
        hop(m, 13, row_set(m, 1, quarters[1]), -1, 0).start()
        hop(m, 10, column_set(m, -1, last), 0, -1).wait_recv()
        hop(m, 14, column_set(m, -1, quarters[2]), 0, 1).start()
        hop(m, 11, column_set(m, 1, last), 0, 1).wait_recv()
        hop(m, 15, column_set(m, 1, quarters[3]), 0, -1).start()

    def gather_wait(m):
        hop(m, 12, row_set(m, 2, quarters[0]), -1, 0).wait_recv()
        hop(m, 13, row_set(m, 2, quarters[1]), 1, 0).wait_recv()
        hop(m, 14, column_set(m, 2, quarters[2]), 0, -1).wait_recv()
        hop(m, 15, column_set(m, 2, quarters[3]), 0, 1).wait_recv()

    def gather_end(m):
        sent = own_env.at[m, :, pl.ds(0, WIDTH - ROWS), :]
        remote(
            sent, sent, gather_send_sem.at[m], own_recv_sem.at[m], ring(next_z)
        ).wait_send()

    def turn(n, sources, targets, begin, count):
        source = sources.at[pl.ds(begin, count)]
        target = targets.at[pl.ds(begin, count)]

        def send(i, carry):
            peer = plane_peer(i)
            remote(
                source.at[:, peer],
                target.at[:, k],
                turn_send_sem.at[n],
                turn_recv_sem.at[n],
                plane(peer),
            ).start()
            return carry

        lax.fori_loop(1, TR, send, 0)
        for place in range(begin, begin + count):
            targets[place, k] = sources[place, k]
        part = target.at[:, pl.ds(0, TR - 1)]
        done = remote(
            part, part, turn_send_sem.at[n], turn_recv_sem.at[n], ring(next_z)
        )
        ends.append(done)
        return done

    sector = 2 * z + core

    def shifts(n, source, target):
        copies = []
        for way in range(2):
            copy = remote(
                source,
                target.at[way],
                near_send_sem.at[n, way],
                near_recv_sem.at[n, way],
                {"tr": lax.rem(z + core - way + TR, TR), "sec": partner},
            )
            copy.start()
            copies.append(copy)
        ends.extend(copies)
        return copies

    def inside(way, value):
        exists = sector > 0 if way == 0 else sector < SEC - 1
        return jnp.where(exists, value, jnp.zeros_like(value))

    move_in_plane(0, cols_send, cols_mid)
    scatter(0)
    own_start(0)
    cols_done = move_in_ring(0, cols_mid, cols)
    scatter(1)
    gather_one(0)
    move_in_plane(1, pc_send, pc_mid)

    wide_line = iota((WIDTH, WIDTH), 0)
    wide_other = iota((WIDTH, WIDTH), 1)

    def old_row(r):
        pair = over(r, 1)
        return under(pair, 4) * 32 + over(r, 5) * 2 + r - 2 * pair

    to_new[...] = (old_row(wide_line) == wide_other).astype(BF16)
    gather_two(0)
    to_old[...] = (old_row(wide_other) == wide_line).astype(BF16)
    loads[2].wait()
    spread = (over(iota((LINES, PHYS), 0), 5) == iota((LINES, PHYS), 1)).astype(BF16)
    same_row = under(line, 5) == under(other, 5)
    for c in range(3):
        mixed = dot_nt(dot(spread, mix[c]).astype(BF16), spread)
        kron[c] = jnp.where(same_row, mixed, 0.0).astype(BF16)
    own_start(1)
    gather_three(0)

    def reordered(value):
        return dot(to_new[...], value).astype(BF16).reshape(TR, ROWS, HALF)

    def right_part(c, value):
        return reordered(dot(env_matrix(0, c), value).astype(BF16))

    cols_done.wait_recv()
    copies = shifts(0, cols, near_cols)
    own_cols = cols[...].reshape(WIDTH, HALF)
    turn_send[3] = reordered(own_cols)
    start_turn = turn(2, turn_send, turn_recv, 3, 1)
    gather_four(0)
    gather_one(1)
    gather_wait(0)
    turn_send[0] = right_part(0, own_cols)
    turns = [turn(0, turn_send, turn_recv, 0, 1)]
    gather_two(1)
    for way in range(2):
        copies[way].wait_recv()
        turn_send[way + 1] = right_part(
            way + 1, inside(way, near_cols[way].reshape(WIDTH, HALF))
        )
    turns.append(turn(1, turn_send, turn_recv, 1, 2))
    gather_three(1)
    pc_done = move_in_ring(1, pc_mid, pc_new)
    gather_four(1)
    for c in range(3):
        right_old[c] = dot(env_matrix(0, c), to_old[...]).astype(BF16)
    gather_wait(1)
    total = None
    for c in range(3):
        if c < 2:
            turns[c].wait_recv()
        mixed = dot(kron[c], phys_major(turn_recv[c])).astype(BF16)
        term = dot_nt(mixed, env_matrix(1, c))
        total = term if total is None else total + term
    rounded = total.astype(BF16)
    first_send[...] = to_row_major(rounded).astype(BF16).reshape(TR, 2 * PHYS, WIDTH)
    image0 = rounded.astype(F32)
    start_turn.wait_recv()
    s = phys_major(turn_recv[3]).astype(F32)
    pc_done.wait_recv()
    factors = to_phys_major(pc_new[...].reshape(LINES, WIDTH))

    def tr_start(h, block):
        red_send[h, 0] = block

        def send(i, carry):
            remote(
                red_send.at[h, 0],
                red_tr.at[h, z],
                red_send_sem.at[h, 0],
                red_recv_sem.at[h, 0],
                ring(ring_peer(i)),
            ).start()
            return carry

        lax.fori_loop(0, TR - 1, send, 0)
        red_tr[h, z] = block
        done = several(red_tr.at[h], TR - 1, red_send_sem.at[h, 0], red_recv_sem.at[h, 0])
        ends.append(done)
        return done

    def sec_start(h, block):
        red_send[h, 1] = block

        def send(i, carry):
            remote(
                red_send.at[h, 1],
                red_sec.at[h, sec],
                red_send_sem.at[h, 1],
                red_recv_sem.at[h, 1],
                {"sec": wrap(sec + i, SEC)},
            ).start()
            return carry

        lax.fori_loop(1, SEC, send, 0)
        red_sec[h, sec] = block
        done = several(red_sec.at[h], SEC - 1, red_send_sem.at[h, 1], red_recv_sem.at[h, 1])
        ends.append(done)
        return done

    def means(block):
        whole = jnp.sum(block, axis=1, keepdims=True)
        return [whole[n : n + 1] / COUNT for n in range(4)]

    weighted = s * factors
    parts = (s * s, s * image0, weighted * image0, weighted * s)
    block = jnp.concatenate([partial_sum(part) for part in parts] * 2, axis=0)
    tr_start(0, block).wait_recv()
    sums_done = sec_start(0, jnp.sum(red_tr[0], axis=0))
    back(2, first_send, first_old, 0, 5)
    for c in range(3):
        left_turned[c] = env_matrix(1, c).T
    sums_done.wait_recv()
    ss, sw, spw, sps = means(jnp.sum(red_sec[0], axis=0))
    norm = lax.rsqrt(ss + EPSILON)
    theta = norm * norm * sw
    along = norm * norm * (spw - theta * sps)

    def trial_of(image, vector, weights):
        return (image - theta * vector) * weights - along * vector

    trial = trial_of(image0, s, factors)
    trial_bf = trial.astype(BF16)
    vec[...] = trial_bf

    copies = shifts(1, vec, near_vec)
    turns = []

    def left_part(c, value):
        mixed = dot(kron[c], value).astype(BF16)
        return dot(mixed, left_turned[c]).astype(BF16)

    store_columns(half_send.at[0], left_part(0, trial_bf))
    turns = [turn(3, half_send, half_recv, 0, 1)]
    store_columns(half_send.at[3], trial_bf)
    for way in range(2):
        copies[way].wait_recv()
        store_columns(half_send.at[way + 1], left_part(way + 1, inside(way, near_vec[way])))
    turns.append(turn(4, half_send, half_recv, 1, 2))
    trial_turn = turn(5, half_send, half_recv, 3, 1)
    back(2, first_send, first_old, 5, TR - 1)
    back_home(2, first_send, first_old)
    second = trial_bf.astype(F32)
    tt = partial_sum(trial * trial)
    t0 = partial_sum(second * image0)
    total = None
    for c in range(3):
        if c < 2:
            turns[c].wait_recv()
        term = dot(right_old[c], half_recv[c].reshape(WIDTH, HALF))
        total = term if total is None else total + term
    second_send[...] = total.astype(BF16).reshape(TR, ROWS, HALF)
    back(3, second_send, second_old, 0, TR - 1)
    back_home(3, second_send, second_old)
    image1_cols = total.astype(BF16).astype(F32)
    trial_turn.wait_recv()
    trial_cols = dot(to_old[...], half_recv[3].reshape(WIDTH, HALF))
    s1 = partial_sum(cols[...].reshape(WIDTH, HALF).astype(F32) * image1_cols)
    t1 = partial_sum(trial_cols * image1_cols)
    block = jnp.concatenate([tt, s1, t0, t1] * 2, axis=0)
    sec_start(1, block).wait_recv()
    sums_done = tr_start(1, jnp.sum(red_sec[1], axis=0))
    sums_done.wait_recv()
    tt, s1, t0, t1 = means(jnp.sum(red_tr[1], axis=0))

    fresh = norm * norm * tt
    grow = norm * lax.rsqrt(fresh + EPSILON)
    cross = 0.5 * norm * grow * (s1 + t0)
    corner = grow * grow * t1
    halfgap = 0.5 * (theta - corner)
    energy = 0.5 * (theta + corner) - jnp.sqrt(halfgap * halfgap + cross * cross)
    weight_one = corner - energy
    weight_two = -cross
    scale = lax.rsqrt(weight_one * weight_one + weight_two * weight_two)
    one = weight_one * scale * norm
    two = weight_two * scale * grow
    energy_out[...] = energy

    back_wait(2, first_old, False)
    old_image = first_old[...].reshape(LINES, WIDTH).astype(F32)
    old_start = start_rows[...].astype(F32)
    old_factors = pc_send[...].reshape(LINES, WIDTH).astype(F32)
    old_trial = trial_of(old_image, old_start, old_factors).astype(BF16).astype(F32)
    ritz = one * old_start + two * old_trial
    psi_out[...] = ritz.reshape(ROWS, PHYS, WIDTH).astype(BF16)[None]
    partial = one * old_image - energy * ritz
    back_wait(3, second_old, False)
    residual = partial + two * to_row_major(phys_major(second_old[...]))
    res_out[...] = residual.reshape(ROWS, PHYS, WIDTH).astype(BF16)[None]

    for m in range(2):
        scatter_end(m)
        gather_end(m)

        @pl.when(shift != 0)
        def _():
            hand_over(m).wait_send()

    back_wait(2, first_old, True)
    back_wait(3, second_old, True)
    for end in ends:
        end.wait_send()


def body(psi, precond, env_left, env_right, mixers, sizes):
    anywhere = pl.BlockSpec(memory_space=pl.ANY)
    vmem = pl.BlockSpec(memory_space=pltpu.VMEM)
    dma = pltpu.SemaphoreType.DMA
    columns = (TR, ROWS, HALF)
    fours = (4, TR, ROWS, HALF)
    rows = (TR, 2 * PHYS, WIDTH)
    psi_new, residual_new, energy = pl.pallas_call(
        kernel,
        out_shape=(
            jax.ShapeDtypeStruct(psi.shape, BF16),
            jax.ShapeDtypeStruct(psi.shape, BF16),
            jax.ShapeDtypeStruct((1, 1), F32),
        ),
        in_specs=[anywhere] * 6,
        out_specs=(vmem, vmem, vmem),
        scratch_shapes=[
            pltpu.VMEM((ROWS, PHYS, WIDTH), BF16),
            pltpu.VMEM((ROWS, PHYS, WIDTH), BF16),
            pltpu.VMEM((3, PHYS, PHYS), BF16),
            pltpu.SMEM((1, 2), jnp.int32),
            pltpu.VMEM((2, 3, WIDTH, WIDTH), BF16),
            pltpu.VMEM((2, 3, ROWS, WIDTH), BF16),
            pltpu.VMEM((2, 3, 4, 4, ROWS, WIDTH), BF16),
            pltpu.VMEM((3, LINES, LINES), BF16),
            pltpu.VMEM((2, LINES, LINES), BF16),
            pltpu.VMEM((WIDTH, WIDTH), BF16),
            pltpu.VMEM((WIDTH, WIDTH), BF16),
            pltpu.VMEM((3, WIDTH, WIDTH), BF16),
            pltpu.VMEM((3, WIDTH, WIDTH), BF16),
            pltpu.VMEM((LINES, WIDTH), BF16),
            pltpu.VMEM(columns, BF16),
            pltpu.VMEM(columns, BF16),
            pltpu.VMEM(columns, BF16),
            pltpu.VMEM((2, *columns), BF16),
            pltpu.VMEM(fours, BF16),
            pltpu.VMEM(fours, BF16),
            pltpu.VMEM(rows, BF16),
            pltpu.VMEM(rows, BF16),
            pltpu.VMEM(rows, BF16),
            pltpu.VMEM((LINES, WIDTH), BF16),
            pltpu.VMEM((2, LINES, WIDTH), BF16),
            pltpu.VMEM(fours, BF16),
            pltpu.VMEM(fours, BF16),
            pltpu.VMEM(rows, BF16),
            pltpu.VMEM(rows, BF16),
            pltpu.VMEM(columns, BF16),
            pltpu.VMEM(columns, BF16),
            pltpu.VMEM((2, 2, 8, 128), F32),
            pltpu.VMEM((2, TR, 8, 128), F32),
            pltpu.VMEM((2, SEC, 8, 128), F32),
            dma((6,)),
            dma((2, 4)),
            dma((2,)),
            dma((2,)),
            dma((2,)),
            dma((2,)),
            dma((2, 16)),
            dma((2, 2)),
            dma((2, 2)),
            dma((6,)),
            dma((6,)),
            dma((4, 2)),
            dma((4, TR)),
            dma((4,)),
            dma((2, 2)),
            dma((2, 2)),
        ],
        compiler_params=pltpu.CompilerParams(
            collective_id=0, has_side_effects=True, vmem_limit_bytes=60 * 1024 * 1024
        ),
        cost_estimate=pl.CostEstimate(
            flops=2_200_000_000, bytes_accessed=2_000_000, transcendentals=0
        ),
    )(psi, precond, env_left, env_right, mixers, sizes)
    return psi_new, residual_new, energy.reshape(())


def solution(mesh):
    placed = (
        P("sec", "tr", None, None),
        P("sec", "tr", None, None),
        P(None, "sec", None, None),
        P(None, "sec", None, None),
        P(),
        P("sec", None),
    )
    return jax.shard_map(
        body,
        mesh=mesh,
        in_specs=placed,
        out_specs=(P("sec", "tr", None, None), P("sec", "tr", None, None), P()),
        check_vma=False,
    )
```

```python
import jax
import jax.numpy as jnp
from jax import lax
from jax.experimental import pallas as pl
from jax.experimental.pallas import tpu as pltpu
from jax.sharding import PartitionSpec as P

EPSILON = 1e-06
MESH = pl.DeviceIdType.MESH
F32 = jnp.float32
BF16 = jnp.bfloat16
TR = 16
SEC = 32
ROWS = 32
PHYS = 8
WIDTH = 512
HALF = 256
LINES = ROWS * PHYS
COUNT = float(SEC * WIDTH * PHYS * WIDTH)
STEPS = (1, 3, 2)


def dot(a, b):
    return jnp.dot(a, b, preferred_element_type=F32)


def dot_nt(a, b):
    return lax.dot_general(a, b, (((1,), (1,)), ((), ())), preferred_element_type=F32)


def iota(shape, axis):
    return lax.broadcasted_iota(jnp.int32, shape, axis)


def wrap(value, size):
    return jnp.where(value >= size, value - size, value)


def over(value, bits):
    return lax.shift_right_logical(value, jnp.full_like(value, bits))


def under(value, bits):
    return value - lax.shift_left(over(value, bits), jnp.full_like(value, bits))


def partial_sum(x):
    rows = jnp.sum(x, axis=0, keepdims=True)
    total = rows[:, 0:128]
    for lane in range(128, x.shape[1], 128):
        total = total + rows[:, lane : lane + 128]
    return total


def phys_major(block):
    pieces = [jnp.concatenate([block[2 * p], block[2 * p + 1]], axis=1) for p in range(PHYS)]
    return jnp.concatenate(pieces, axis=0)


def store_columns(ref, value):
    for j in range(TR):
        p, side = divmod(j, 2)
        ref[j] = value[p * ROWS : (p + 1) * ROWS, side * HALF : (side + 1) * HALF]


def kernel(
    psi_hbm,
    pc_hbm,
    left_hbm,
    right_hbm,
    mix_hbm,
    sizes_hbm,
    psi_out,
    res_out,
    energy_out,
    psi_in,
    pc_in,
    mix,
    sizes,
    own_env,
    land_env,
    env,
    kron,
    swap,
    to_new,
    to_old,
    right_old,
    left_turned,
    start_rows,
    cols_send,
    cols_mid,
    cols,
    near_cols,
    turn_send,
    turn_recv,
    pc_send,
    pc_mid,
    pc_new,
    vec,
    near_vec,
    half_send,
    half_recv,
    first_send,
    first_mid,
    first_old,
    second_send,
    second_mid,
    second_old,
    red_send,
    red_tr,
    red_sec,
    in_sem,
    scatter_send_sem,
    scatter_recv_sem,
    own_send_sem,
    own_recv_sem,
    gather_send_sem,
    gather_recv_sem,
    near_send_sem,
    near_recv_sem,
    turn_send_sem,
    turn_recv_sem,
    move_send_sem,
    move_one_sem,
    move_two_sem,
    red_send_sem,
    red_recv_sem,
):
    z = lax.axis_index("tr")
    sec = lax.axis_index("sec")
    k = over(sec, 1)
    core = sec - 2 * k
    y = over(k, 2)
    x = k - 4 * y
    next_z = wrap(z + 1, TR)
    rows_at = [y] + [wrap(y + d, 4) for d in range(1, 4)]
    columns_at = [x] + [wrap(x + d, 4) for d in range(1, 4)]

    def ring(z2):
        return {"tr": z2}

    def plane(k2):
        return {"sec": 2 * k2 + core}

    def turned(m):
        return jnp.where(m >= TR - 1, m - (TR - 1), m)

    def ring_peer(i):
        m = turned(i + k)
        half = over(m, 1)
        step = half + 1
        return wrap(z + jnp.where(m == 2 * half, step, TR - step), TR)

    def ring_source(i):
        m = turned(i + k)
        half = over(m, 1)
        step = half + 1
        return wrap(z + jnp.where(m == 2 * half, TR - step, step), TR)

    def plane_peer(i):
        down = over(i, 2)
        return 4 * wrap(y + down, 4) + wrap(x + i - 4 * down, 4)

    def remote(src, dst, send_sem, recv_sem, device):
        return pltpu.make_async_remote_copy(
            src_ref=src,
            dst_ref=dst,
            send_sem=send_sem,
            recv_sem=recv_sem,
            device_id=device,
            device_id_type=MESH,
        )

    def several(ref, count, send_sem, recv_sem):
        part = ref.at[pl.ds(0, count)]
        return remote(part, part, send_sem, recv_sem, ring(next_z))

    ends = []

    loads = [
        pltpu.make_async_copy(psi_hbm.at[0], psi_in, in_sem.at[0]),
        pltpu.make_async_copy(pc_hbm.at[0], pc_in, in_sem.at[1]),
        pltpu.make_async_copy(mix_hbm, mix, in_sem.at[2]),
        pltpu.make_async_copy(sizes_hbm, sizes, in_sem.at[3]),
    ]
    env_loads = [
        pltpu.make_async_copy(right_hbm.at[:, 0], own_env.at[0], in_sem.at[4]),
        pltpu.make_async_copy(left_hbm.at[:, 0], own_env.at[1], in_sem.at[5]),
    ]
    for load in loads:
        load.start()
    gap = lax.rem(z - k + TR + 1, TR)

    @pl.when(gap < 4)
    def _():
        for load in env_loads:
            load.start()

    barrier = pltpu.get_barrier_semaphore()

    def greet_tr(i, carry):
        pl.semaphore_signal(barrier, inc=1, device_id=ring(wrap(z + i, TR)), device_id_type=MESH)
        return carry

    def greet_sec(i, carry):
        pl.semaphore_signal(
            barrier, inc=1, device_id={"sec": wrap(sec + i, SEC)}, device_id_type=MESH
        )
        return carry

    partner = sec + 1 - 2 * core
    pl.semaphore_signal(
        barrier,
        inc=1,
        device_id={"tr": lax.rem(z + 2 * core - 1 + TR, TR), "sec": partner},
        device_id_type=MESH,
    )
    lax.fori_loop(1, SEC, greet_sec, 0)
    lax.fori_loop(1, TR, greet_tr, 0)

    line = iota((LINES, LINES), 0)
    other = iota((LINES, LINES), 1)

    for n, (one, two) in enumerate(((line, other), (other, line))):
        same = one == under(two, 3) * ROWS + over(two, 3)
        swap[n] = same.astype(BF16)

    def to_phys_major(value):
        return dot(swap[0], value)

    def to_row_major(value):
        return dot(swap[1], value)

    loads[3].wait()
    used_left = sizes[0, 0]
    used_right = sizes[0, 1]
    keep = ((z * ROWS + over(iota((LINES, WIDTH), 0), 3)) < used_right) & (
        iota((LINES, WIDTH), 1) < used_left
    )
    loads[0].wait()
    start = jnp.where(keep, psi_in[...].astype(F32).reshape(LINES, WIDTH), 0.0).astype(BF16)
    start_rows[...] = start
    store_columns(cols_send, to_phys_major(start).astype(BF16))
    loads[1].wait()
    pc_send[...] = pc_in[...].astype(F32).reshape(TR, 2 * PHYS, WIDTH).astype(BF16)

    pl.semaphore_wait(barrier, TR + SEC - 1)

    def move_in_plane(n, source, middle):
        def send(i, carry):
            peer = plane_peer(i)
            remote(
                source.at[peer],
                middle.at[k],
                move_send_sem.at[n, 0],
                move_one_sem.at[n, k],
                plane(peer),
            ).start()
            return carry

        lax.fori_loop(1, TR, send, 0)
        middle[k] = source[k]
        ends.append(several(middle, TR - 1, move_send_sem.at[n, 0], move_two_sem.at[n]))

    def arrived(n, middle, index):
        return remote(
            middle.at[index],
            middle.at[index],
            move_send_sem.at[n, 0],
            move_one_sem.at[n, index],
            ring(next_z),
        )

    def move_in_ring(n, middle, target):
        def send(i, carry):
            peer = ring_peer(i)

            @pl.when(peer != k)
            def _():
                arrived(n, middle, peer).wait_recv()

            remote(
                middle.at[peer], target.at[z], move_send_sem.at[n, 1], move_two_sem.at[n], ring(peer)
            ).start()
            return carry

        lax.fori_loop(0, TR - 1, send, 0)

        @pl.when(z != k)
        def _():
            arrived(n, middle, z).wait_recv()

        target[z] = middle[z]
        done = several(target, TR - 1, move_send_sem.at[n, 1], move_two_sem.at[n])
        ends.append(done)
        return done

    def back_in_ring(n, source, middle):
        def send(i, carry):
            peer = ring_peer(i)
            remote(
                source.at[peer],
                middle.at[z],
                move_send_sem.at[n, 0],
                move_one_sem.at[n, z],
                ring(peer),
            ).start()
            return carry

        lax.fori_loop(0, TR - 1, send, 0)
        middle[z] = source[z]
        ends.append(several(middle, TR - 1, move_send_sem.at[n, 0], move_two_sem.at[n]))

    def back_in_plane(n, middle, target):
        def forward(index):
            @pl.when(index != k)
            def _():
                remote(
                    middle.at[index],
                    target.at[k],
                    move_send_sem.at[n, 1],
                    move_two_sem.at[n],
                    plane(index),
                ).start()

        def send(i, carry):
            index = ring_source(i)
            arrived(n, middle, index).wait_recv()
            forward(index)
            return carry

        forward(z)
        lax.fori_loop(0, TR - 1, send, 0)
        target[k] = middle[k]
        done = several(target, TR - 1, move_send_sem.at[n, 1], move_two_sem.at[n])
        ends.append(done)
        return done

    def env_matrix(m, c):
        return env[m, c].reshape(WIDTH, WIDTH)

    def piece(m, dy, dx, part=(pl.ds(0, ROWS), pl.ds(0, WIDTH))):
        return env.at[m, :, rows_at[dy % 4], columns_at[dx % 4], part[0], part[1]]

    def row_set(m, dy, part):
        return env.at[m, :, rows_at[dy % 4], :, part[0], part[1]]

    def column_set(m, dx, part):
        return env.at[m, :, :, columns_at[dx % 4], part[0], part[1]]

    def scatter_copy(m, d, n):
        return remote(
            own_env.at[m, :, pl.ds((4 * d + n) * ROWS, ROWS), :],
            land_env.at[m],
            scatter_send_sem.at[m, n],
            scatter_recv_sem.at[m],
            plane(4 * d + n),
        )

    def scatter(m):
        used = used_right if m == 0 else used_left
        for d in range(4):

            @pl.when(gap == d)
            def _():
                env_loads[m].wait()
                span = pl.ds(4 * d * ROWS, 4 * ROWS)
                rows = own_env[m, :, span, :]
                own_env[m, :, span, :] = jnp.where(4 * d * ROWS < used, rows, jnp.zeros_like(rows))
                for n in range(4):

                    @pl.when(k != 4 * d + n)
                    def _():
                        scatter_copy(m, d, n).start()

                    @pl.when(k == 4 * d + n)
                    def _():
                        land_env[m] = own_env[m, :, pl.ds((4 * d + n) * ROWS, ROWS), :]

    def scatter_end(m):
        for d in range(4):

            @pl.when(gap == d)
            def _():
                for n in range(4):

                    @pl.when(k != 4 * d + n)
                    def _():
                        scatter_copy(m, d, n).wait_send()

    shift = y - 1
    home = lax.rem(z - shift + TR, TR)

    def hand_over(m):
        return remote(
            land_env.at[m], piece(m, 0, 0), own_send_sem.at[m], own_recv_sem.at[m], ring(home)
        )

    def keep_here(m):
        return pltpu.make_async_copy(land_env.at[m], piece(m, 0, 0), own_recv_sem.at[m])

    def own_start(m):
        @pl.when(home != k)
        def _():
            remote(
                land_env.at[m],
                land_env.at[m],
                own_send_sem.at[m],
                scatter_recv_sem.at[m],
                ring(next_z),
            ).wait_recv()

        @pl.when(shift != 0)
        def _():
            hand_over(m).start()

        @pl.when(shift == 0)
        def _():
            keep_here(m).start()

    def own_wait(m):
        @pl.when(shift != 0)
        def _():
            hand_over(m).wait_recv()

        @pl.when(shift == 0)
        def _():
            keep_here(m).wait()

    first = (pl.ds(0, 16), pl.ds(0, WIDTH))
    last = (pl.ds(16, 16), pl.ds(0, WIDTH))
    quarters = [(pl.ds(n // 2 * 16, 16), pl.ds(n % 2 * HALF, HALF)) for n in range(4)]

    def hop(m, n, ref, dy, dx):
        target = 4 * rows_at[dy % 4] + columns_at[dx % 4]
        return remote(ref, ref, gather_send_sem.at[m], gather_recv_sem.at[m, n], plane(target))

    def gather_one(m):
        own_wait(m)
        hop(m, 0, piece(m, 0, 0, first), 0, 1).start()
        hop(m, 1, piece(m, 0, 0, first), 0, -1).start()
        hop(m, 2, piece(m, 0, 0, last), 1, 0).start()
        hop(m, 3, piece(m, 0, 0, last), -1, 0).start()

    def gather_two(m):
        hop(m, 0, piece(m, 0, -1, first), 0, -1).wait_recv()
        hop(m, 4, piece(m, 0, -1, quarters[0]), 0, 1).start()
        hop(m, 1, piece(m, 0, 1, first), 0, 1).wait_recv()
        hop(m, 5, piece(m, 0, 1, quarters[1]), 0, -1).start()
        hop(m, 2, piece(m, -1, 0, last), -1, 0).wait_recv()
        hop(m, 6, piece(m, -1, 0, quarters[2]), 1, 0).start()
        hop(m, 3, piece(m, 1, 0, last), 1, 0).wait_recv()
        hop(m, 7, piece(m, 1, 0, quarters[3]), -1, 0).start()

    def gather_three(m):
        hop(m, 4, piece(m, 0, 2, quarters[0]), 0, -1).wait_recv()
        hop(m, 5, piece(m, 0, 2, quarters[1]), 0, 1).wait_recv()
        hop(m, 8, row_set(m, 0, first), 1, 0).start()
        hop(m, 9, row_set(m, 0, first), -1, 0).start()
        hop(m, 6, piece(m, 2, 0, quarters[2]), -1, 0).wait_recv()
        hop(m, 7, piece(m, 2, 0, quarters[3]), 1, 0).wait_recv()
        hop(m, 10, column_set(m, 0, last), 0, 1).start()
        hop(m, 11, column_set(m, 0, last), 0, -1).start()

    def gather_four(m):
        hop(m, 8, row_set(m, -1, first), -1, 0).wait_recv()
        hop(m, 12, row_set(m, -1, quarters[0]), 1, 0).start()
        hop(m, 9, row_set(m, 1, first), 1, 0).wait_recv()
        hop(m, 13, row_set(m, 1, quarters[1]), -1, 0).start()
        hop(m, 10, column_set(m, -1, last), 0, -1).wait_recv()
        hop(m, 14, column_set(m, -1, quarters[2]), 0, 1).start()
        hop(m, 11, column_set(m, 1, last), 0, 1).wait_recv()
        hop(m, 15, column_set(m, 1, quarters[3]), 0, -1).start()

    def gather_wait(m):
        hop(m, 12, row_set(m, 2, quarters[0]), -1, 0).wait_recv()
        hop(m, 13, row_set(m, 2, quarters[1]), 1, 0).wait_recv()
        hop(m, 14, column_set(m, 2, quarters[2]), 0, -1).wait_recv()
        hop(m, 15, column_set(m, 2, quarters[3]), 0, 1).wait_recv()

    def gather_end(m):
        sent = own_env.at[m, :, pl.ds(0, WIDTH - ROWS), :]
        remote(
            sent, sent, gather_send_sem.at[m], own_recv_sem.at[m], ring(next_z)
        ).wait_send()

    def turn(n, sources, targets, begin, count):
        source = sources.at[pl.ds(begin, count)]
        target = targets.at[pl.ds(begin, count)]

        def send(i, carry):
            peer = plane_peer(i)
            remote(
                source.at[:, peer],
                target.at[:, k],
                turn_send_sem.at[n],
                turn_recv_sem.at[n],
                plane(peer),
            ).start()
            return carry

        lax.fori_loop(1, TR, send, 0)
        for place in range(begin, begin + count):
            targets[place, k] = sources[place, k]
        part = target.at[:, pl.ds(0, TR - 1)]
        done = remote(
            part, part, turn_send_sem.at[n], turn_recv_sem.at[n], ring(next_z)
        )
        ends.append(done)
        return done

    sector = 2 * z + core

    def shifts(n, source, target):
        copies = []
        for way in range(2):
            copy = remote(
                source,
                target.at[way],
                near_send_sem.at[n, way],
                near_recv_sem.at[n, way],
                {"tr": lax.rem(z + core - way + TR, TR), "sec": partner},
            )
            copy.start()
            copies.append(copy)
        ends.extend(copies)
        return copies

    def inside(way, value):
        exists = sector > 0 if way == 0 else sector < SEC - 1
        return jnp.where(exists, value, jnp.zeros_like(value))

    move_in_plane(0, cols_send, cols_mid)
    scatter(0)
    own_start(0)
    cols_done = move_in_ring(0, cols_mid, cols)
    scatter(1)
    gather_one(0)
    move_in_plane(1, pc_send, pc_mid)

    wide_line = iota((WIDTH, WIDTH), 0)
    wide_other = iota((WIDTH, WIDTH), 1)

    def old_row(r):
        pair = over(r, 1)
        return under(pair, 4) * 32 + over(r, 5) * 2 + r - 2 * pair

    to_new[...] = (old_row(wide_line) == wide_other).astype(BF16)
    gather_two(0)
    to_old[...] = (old_row(wide_other) == wide_line).astype(BF16)
    loads[2].wait()
    spread = (over(iota((LINES, PHYS), 0), 5) == iota((LINES, PHYS), 1)).astype(BF16)
    same_row = under(line, 5) == under(other, 5)
    for c in range(3):
        mixed = dot_nt(dot(spread, mix[c]).astype(BF16), spread)
        kron[c] = jnp.where(same_row, mixed, 0.0).astype(BF16)
    own_start(1)
    gather_three(0)

    def reordered(value):
        return dot(to_new[...], value).astype(BF16).reshape(TR, ROWS, HALF)

    def right_part(c, value):
        return reordered(dot(env_matrix(0, c), value).astype(BF16))

    cols_done.wait_recv()
    copies = shifts(0, cols, near_cols)
    own_cols = cols[...].reshape(WIDTH, HALF)
    turn_send[3] = reordered(own_cols)
    start_turn = turn(2, turn_send, turn_recv, 3, 1)
    gather_four(0)
    gather_one(1)
    gather_wait(0)
    turn_send[0] = right_part(0, own_cols)
    turns = [turn(0, turn_send, turn_recv, 0, 1)]
    gather_two(1)
    for way in range(2):
        copies[way].wait_recv()
        turn_send[way + 1] = right_part(
            way + 1, inside(way, near_cols[way].reshape(WIDTH, HALF))
        )
    turns.append(turn(1, turn_send, turn_recv, 1, 2))
    gather_three(1)
    pc_done = move_in_ring(1, pc_mid, pc_new)
    gather_four(1)
    for c in range(3):
        right_old[c] = dot(env_matrix(0, c), to_old[...]).astype(BF16)
    gather_wait(1)
    total = None
    for c in range(3):
        if c < 2:
            turns[c].wait_recv()
        mixed = dot(kron[c], phys_major(turn_recv[c])).astype(BF16)
        term = dot_nt(mixed, env_matrix(1, c))
        total = term if total is None else total + term
    rounded = total.astype(BF16)
    first_send[...] = to_row_major(rounded).astype(BF16).reshape(TR, 2 * PHYS, WIDTH)
    image0 = rounded.astype(F32)
    start_turn.wait_recv()
    s = phys_major(turn_recv[3]).astype(F32)
    pc_done.wait_recv()
    factors = to_phys_major(pc_new[...].reshape(LINES, WIDTH))

    def tr_start(h, block):
        red_send[h, 0] = block

        def send(i, carry):
            remote(
                red_send.at[h, 0],
                red_tr.at[h, z],
                red_send_sem.at[h, 0],
                red_recv_sem.at[h, 0],
                ring(ring_peer(i)),
            ).start()
            return carry

        lax.fori_loop(0, TR - 1, send, 0)
        red_tr[h, z] = block
        done = several(red_tr.at[h], TR - 1, red_send_sem.at[h, 0], red_recv_sem.at[h, 0])
        ends.append(done)
        return done

    def sec_start(h, block):
        red_send[h, 1] = block

        def send(i, carry):
            remote(
                red_send.at[h, 1],
                red_sec.at[h, sec],
                red_send_sem.at[h, 1],
                red_recv_sem.at[h, 1],
                {"sec": wrap(sec + i, SEC)},
            ).start()
            return carry

        lax.fori_loop(1, SEC, send, 0)
        red_sec[h, sec] = block
        done = several(red_sec.at[h], SEC - 1, red_send_sem.at[h, 1], red_recv_sem.at[h, 1])
        ends.append(done)
        return done

    def means(block):
        whole = jnp.sum(block, axis=1, keepdims=True)
        return [whole[n : n + 1] / COUNT for n in range(4)]

    weighted = s * factors
    parts = (s * s, s * image0, weighted * image0, weighted * s)
    block = jnp.concatenate([partial_sum(part) for part in parts] * 2, axis=0)
    tr_start(0, block).wait_recv()
    sums_done = sec_start(0, jnp.sum(red_tr[0], axis=0))
    back_in_ring(2, first_send, first_mid)
    for c in range(3):
        left_turned[c] = env_matrix(1, c).T
    sums_done.wait_recv()
    ss, sw, spw, sps = means(jnp.sum(red_sec[0], axis=0))
    norm = lax.rsqrt(ss + EPSILON)
    theta = norm * norm * sw
    along = norm * norm * (spw - theta * sps)

    def trial_of(image, vector, weights):
        return (image - theta * vector) * weights - along * vector

    trial = trial_of(image0, s, factors)
    trial_bf = trial.astype(BF16)
    vec[...] = trial_bf

    copies = shifts(1, vec, near_vec)
    turns = []

    def left_part(c, value):
        mixed = dot(kron[c], value).astype(BF16)
        return dot(mixed, left_turned[c]).astype(BF16)

    store_columns(half_send.at[0], left_part(0, trial_bf))
    turns = [turn(3, half_send, half_recv, 0, 1)]
    store_columns(half_send.at[3], trial_bf)
    for way in range(2):
        copies[way].wait_recv()
        store_columns(half_send.at[way + 1], left_part(way + 1, inside(way, near_vec[way])))
    turns.append(turn(4, half_send, half_recv, 1, 2))
    trial_turn = turn(5, half_send, half_recv, 3, 1)
    second = trial_bf.astype(F32)
    tt = partial_sum(trial * trial)
    t0 = partial_sum(second * image0)
    total = None
    for c in range(3):
        if c < 2:
            turns[c].wait_recv()
        term = dot(right_old[c], half_recv[c].reshape(WIDTH, HALF))
        total = term if total is None else total + term
    second_send[...] = total.astype(BF16).reshape(TR, ROWS, HALF)
    back_in_ring(3, second_send, second_mid)
    image1_cols = total.astype(BF16).astype(F32)
    trial_turn.wait_recv()
    trial_cols = dot(to_old[...], half_recv[3].reshape(WIDTH, HALF))
    s1 = partial_sum(cols[...].reshape(WIDTH, HALF).astype(F32) * image1_cols)
    t1 = partial_sum(trial_cols * image1_cols)
    block = jnp.concatenate([tt, s1, t0, t1] * 2, axis=0)
    sec_start(1, block).wait_recv()
    sums_done = tr_start(1, jnp.sum(red_sec[1], axis=0))
    first_done = back_in_plane(2, first_mid, first_old)
    second_done = back_in_plane(3, second_mid, second_old)
    sums_done.wait_recv()
    tt, s1, t0, t1 = means(jnp.sum(red_tr[1], axis=0))

    fresh = norm * norm * tt
    grow = norm * lax.rsqrt(fresh + EPSILON)
    cross = 0.5 * norm * grow * (s1 + t0)
    corner = grow * grow * t1
    halfgap = 0.5 * (theta - corner)
    energy = 0.5 * (theta + corner) - jnp.sqrt(halfgap * halfgap + cross * cross)
    weight_one = corner - energy
    weight_two = -cross
    scale = lax.rsqrt(weight_one * weight_one + weight_two * weight_two)
    one = weight_one * scale * norm
    two = weight_two * scale * grow
    energy_out[...] = energy

    first_done.wait_recv()
    old_image = first_old[...].reshape(LINES, WIDTH).astype(F32)
    old_start = start_rows[...].astype(F32)
    old_factors = pc_send[...].reshape(LINES, WIDTH).astype(F32)
    old_trial = trial_of(old_image, old_start, old_factors).astype(BF16).astype(F32)
    ritz = one * old_start + two * old_trial
    psi_out[...] = ritz.reshape(ROWS, PHYS, WIDTH).astype(BF16)[None]
    partial = one * old_image - energy * ritz
    second_done.wait_recv()
    residual = partial + two * to_row_major(phys_major(second_old[...]))
    res_out[...] = residual.reshape(ROWS, PHYS, WIDTH).astype(BF16)[None]

    for m in range(2):
        scatter_end(m)
        gather_end(m)

        @pl.when(shift != 0)
        def _():
            hand_over(m).wait_send()

    for end in ends:
        end.wait_send()


def body(psi, precond, env_left, env_right, mixers, sizes):
    anywhere = pl.BlockSpec(memory_space=pl.ANY)
    vmem = pl.BlockSpec(memory_space=pltpu.VMEM)
    dma = pltpu.SemaphoreType.DMA
    columns = (TR, ROWS, HALF)
    fours = (4, TR, ROWS, HALF)
    rows = (TR, 2 * PHYS, WIDTH)
    psi_new, residual_new, energy = pl.pallas_call(
        kernel,
        out_shape=(
            jax.ShapeDtypeStruct(psi.shape, BF16),
            jax.ShapeDtypeStruct(psi.shape, BF16),
            jax.ShapeDtypeStruct((1, 1), F32),
        ),
        in_specs=[anywhere] * 6,
        out_specs=(vmem, vmem, vmem),
        scratch_shapes=[
            pltpu.VMEM((ROWS, PHYS, WIDTH), BF16),
            pltpu.VMEM((ROWS, PHYS, WIDTH), BF16),
            pltpu.VMEM((3, PHYS, PHYS), BF16),
            pltpu.SMEM((1, 2), jnp.int32),
            pltpu.VMEM((2, 3, WIDTH, WIDTH), BF16),
            pltpu.VMEM((2, 3, ROWS, WIDTH), BF16),
            pltpu.VMEM((2, 3, 4, 4, ROWS, WIDTH), BF16),
            pltpu.VMEM((3, LINES, LINES), BF16),
            pltpu.VMEM((2, LINES, LINES), BF16),
            pltpu.VMEM((WIDTH, WIDTH), BF16),
            pltpu.VMEM((WIDTH, WIDTH), BF16),
            pltpu.VMEM((3, WIDTH, WIDTH), BF16),
            pltpu.VMEM((3, WIDTH, WIDTH), BF16),
            pltpu.VMEM((LINES, WIDTH), BF16),
            pltpu.VMEM(columns, BF16),
            pltpu.VMEM(columns, BF16),
            pltpu.VMEM(columns, BF16),
            pltpu.VMEM((2, *columns), BF16),
            pltpu.VMEM(fours, BF16),
            pltpu.VMEM(fours, BF16),
            pltpu.VMEM(rows, BF16),
            pltpu.VMEM(rows, BF16),
            pltpu.VMEM(rows, BF16),
            pltpu.VMEM((LINES, WIDTH), BF16),
            pltpu.VMEM((2, LINES, WIDTH), BF16),
            pltpu.VMEM(fours, BF16),
            pltpu.VMEM(fours, BF16),
            pltpu.VMEM(rows, BF16),
            pltpu.VMEM(rows, BF16),
            pltpu.VMEM(rows, BF16),
            pltpu.VMEM(columns, BF16),
            pltpu.VMEM(columns, BF16),
            pltpu.VMEM(columns, BF16),
            pltpu.VMEM((2, 2, 8, 128), F32),
            pltpu.VMEM((2, TR, 8, 128), F32),
            pltpu.VMEM((2, SEC, 8, 128), F32),
            dma((6,)),
            dma((2, 4)),
            dma((2,)),
            dma((2,)),
            dma((2,)),
            dma((2,)),
            dma((2, 16)),
            dma((2, 2)),
            dma((2, 2)),
            dma((6,)),
            dma((6,)),
            dma((4, 2)),
            dma((4, TR)),
            dma((4,)),
            dma((2, 2)),
            dma((2, 2)),
        ],
        compiler_params=pltpu.CompilerParams(
            collective_id=0, has_side_effects=True, vmem_limit_bytes=60 * 1024 * 1024
        ),
        cost_estimate=pl.CostEstimate(
            flops=2_200_000_000, bytes_accessed=2_000_000, transcendentals=0
        ),
    )(psi, precond, env_left, env_right, mixers, sizes)
    return psi_new, residual_new, energy.reshape(())


def solution(mesh):
    placed = (
        P("sec", "tr", None, None),
        P("sec", "tr", None, None),
        P(None, "sec", None, None),
        P(None, "sec", None, None),
        P(),
        P("sec", None),
    )
    return jax.shard_map(
        body,
        mesh=mesh,
        in_specs=placed,
        out_specs=(P("sec", "tr", None, None), P("sec", "tr", None, None), P()),
        check_vma=False,
    )
```
